32 devices in a mesh: expert: 8 (over z, x), dp: 4 (over y, core).
Axes of the slice: x: 2, y: 2, z: 4, core: 2. Of those that a mesh axis runs over, the one named last changes fastest.
Arguments:
- block_in: bfloat16 [32768, 1024], P(('expert', 'dp')), may hold values from -6 to 6
- seq_lengths: int32 [32, 16], P(('expert', 'dp')), may hold values from 0 to 1024, as said below
- slot_position: int32 [32, 1024], P(('expert', 'dp')), may hold values from 0 to 1023, as said below
- first_gain: float32 [1024], replicated, may hold values from 0.5 to 1.5
- first_bias: float32 [1024], replicated, may hold values from -1.2 to 1.2
- query_weight: bfloat16 [1024, 1024], replicated, may hold values from -0.1875 to 0.1875
- query_bias: float32 [1024], replicated, may hold values from -1.2 to 1.2
- key_weight: bfloat16 [1024, 1024], replicated, may hold values from -0.1875 to 0.1875
- value_weight: bfloat16 [1024, 1024], replicated, may hold values from -0.1875 to 0.1875
- value_bias: float32 [1024], replicated, may hold values from -1.2 to 1.2
- out_weight: bfloat16 [1024, 1024], replicated, may hold values from -1.5 to 1.5
- out_bias: float32 [1024], replicated, may hold values from -0.6 to 0.6
- second_gain: float32 [1024], replicated, may hold values from 0.5 to 1.5
- second_bias: float32 [1024], replicated, may hold values from -0.6 to 0.6
- expert_up: bfloat16 [8, 1024, 4096], P('expert', None, 'dp'), may hold values from -0.1875 to 0.1875
- expert_up_bias: float32 [8, 4096], P('expert'), may hold values from -0.6 to 0.6
- expert_down: bfloat16 [8, 4096, 1024], P('expert', 'dp'), may hold values from -0.09375 to 0.09375
- expert_down_bias: float32 [8, 1024], P('expert'), may hold values from -0.6 to 0.6
- block_cot: bfloat16 [32768, 1024], P(('expert', 'dp')), may hold values from -6 to 6
Outputs:
- block_out: bfloat16 [32768, 1024], P(('expert', 'dp'))
- input_grad: bfloat16 [32768, 1024], P(('expert', 'dp'))
- grad_first_gain: float32 [1024], replicated
- grad_first_bias: float32 [1024], replicated
- grad_query_weight: float32 [1024, 1024], replicated
- grad_query_bias: float32 [1024], replicated
- grad_key_weight: float32 [1024, 1024], replicated
- grad_value_weight: float32 [1024, 1024], replicated
- grad_value_bias: float32 [1024], replicated
- grad_out_weight: float32 [1024, 1024], replicated
- grad_out_bias: float32 [1024], replicated
- grad_second_gain: float32 [1024], replicated
- grad_second_bias: float32 [1024], replicated
- grad_expert_up: float32 [8, 1024, 4096], P('expert', None, 'dp')
- grad_expert_up_bias: float32 [8, 4096], P('expert', 'dp')
- grad_expert_down: float32 [8, 4096, 1024], P('expert', 'dp')
- grad_expert_down_bias: float32 [8, 1024], P('expert', 'dp')
The draws below stay inside these ranges and needn't reach their ends.
Inputs may be any that keep to these rules, and one draw needn't show every extreme that they name: `seq_lengths`: each row lists the group's dialogue lengths, each 64 or more, first, then zeros; a row sums to at most 1024. `slot_position`: each row is a permutation of 0 to 1023.
All inputs are finite; a program needn't handle non-finite values.
Results may differ from the reference program's by a relative error of at most 0.012.
Values may be sent and summed in bfloat16 or wider, within the bound.
No kernel may reach another device: no remote copies, remote signals or barrier semaphores. Data moves between devices by JAX's collectives and lax.ppermute only.
A program may use at most 384 MiB of HBM per device.

```python
import math
import jax
import jax.numpy as jnp
from jax import lax

D = 1024
HEADS = 16
FF = 4096
SLOTS = 1024
MAXLEN = 1024
MINLEN = 64
NSEQ = 16
EXPERTS = 8
TOKENS = 32768
N_EXPERT = 8
N_DP = 4


def draw_seq_lengths(key, part):
    key = jax.random.fold_in(key, 11)
    row_count = N_EXPERT * N_DP
    subkeys = jax.random.split(key, 3)
    budget = jax.random.randint(subkeys[0], (row_count,), SLOTS // 2, SLOTS + 1)
    chosen = jax.random.randint(subkeys[1], (), 0, row_count)
    lengths = jax.random.randint(subkeys[2], (row_count, NSEQ), MINLEN, MAXLEN + 1)
    row_ids = jnp.arange(row_count)
    budget = jnp.where(row_ids == chosen, SLOTS, budget)
    leading = jnp.where(row_ids == chosen, MAXLEN, jnp.minimum(lengths[:, 0], budget))
    lengths = lengths.at[:, 0].set(leading)
    end_points = jnp.cumsum(lengths, axis=1)
    return jnp.where(end_points <= budget[:, None], lengths, 0).astype(jnp.int32)


def draw_slot_position(key, part):
    key = jax.random.fold_in(key, 23)
    subkeys = jax.random.split(key, N_EXPERT * N_DP)
    return jax.vmap(lambda single: jax.random.permutation(single, SLOTS))(subkeys).astype(jnp.int32)


def steps_of(stream_key, extent, cuts, low, top_value):
    level, own = 1.0, jax.random.fold_in(stream_key, 6)
    for position, blocks in cuts:
        heights = jnp.exp(jax.random.uniform(jax.random.fold_in(own, position), (blocks,), jnp.float32, low / len(cuts), top_value / len(cuts)))
        level = level * jnp.repeat(heights, extent[position] // blocks).reshape([-1 if axis == position else 1 for axis in range(len(extent))])
    return level


def gaussian(rng, extent, spread, reach, cuts=(), kind=jnp.bfloat16):
    factor_of = steps_of(rng, extent, cuts, -0.22, 0.18) if cuts else 1.0
    entries = jax.random.normal(rng, extent, jnp.float32) * spread * factor_of
    return jnp.minimum(jnp.maximum(entries, -reach), reach).astype(kind)


def setup_inputs(seed: int = 0) -> dict:
    streams_of = jax.random.split(jax.random.key(seed), 20)
    block_in = gaussian(streams_of[0], (TOKENS, D), 1.0, 6.0, ((0, 32),))
    seq_lengths = draw_seq_lengths(jax.random.fold_in(streams_of[19], 71), 0)
    slot_position = draw_slot_position(jax.random.fold_in(streams_of[19], 71), 0)
    first_gain = jnp.clip(1.0 + 0.1 * jax.random.normal(streams_of[3], (D,), jnp.float32), 0.5, 1.5)
    first_bias = gaussian(streams_of[4], (D,), 0.2, 1.2, (), jnp.float32)
    query_weight = gaussian(streams_of[5], (D, D), D ** -0.5, 0.1875)
    query_bias = gaussian(streams_of[6], (D,), 0.2, 1.2, (), jnp.float32)
    key_weight = gaussian(streams_of[7], (D, D), D ** -0.5, 0.1875)
    value_weight = gaussian(streams_of[8], (D, D), D ** -0.5, 0.1875)
    value_bias = gaussian(streams_of[9], (D,), 0.2, 1.2, (), jnp.float32)
    out_weight = gaussian(streams_of[10], (D, D), (max(D // 64, 1)) ** -0.5, 1.5)
    out_bias = gaussian(streams_of[11], (D,), 0.1, 0.6, (), jnp.float32)
    second_gain = jnp.clip(1.0 + 0.1 * jax.random.normal(streams_of[12], (D,), jnp.float32), 0.5, 1.5)
    second_bias = gaussian(streams_of[13], (D,), 0.1, 0.6, (), jnp.float32)
    expert_up = gaussian(streams_of[14], (EXPERTS, D, FF), D ** -0.5, 0.1875, ((0, 8), (2, 4)))
    expert_up_bias = gaussian(streams_of[15], (EXPERTS, FF), 0.1, 0.6, ((0, 8),), jnp.float32)
    expert_down = gaussian(streams_of[16], (EXPERTS, FF, D), FF ** -0.5, 0.09375, ((0, 8), (1, 4)))
    expert_down_bias = gaussian(streams_of[17], (EXPERTS, D), 0.1, 0.6, ((0, 8),), jnp.float32)
    block_cot = gaussian(streams_of[18], (TOKENS, D), 1.0, 6.0, ((0, 32),))
    return dict(block_in=block_in, seq_lengths=seq_lengths, slot_position=slot_position, first_gain=first_gain, first_bias=first_bias, query_weight=query_weight, query_bias=query_bias, key_weight=key_weight, value_weight=value_weight, value_bias=value_bias, out_weight=out_weight, out_bias=out_bias, second_gain=second_gain, second_bias=second_bias, expert_up=expert_up, expert_up_bias=expert_up_bias, expert_down=expert_down, expert_down_bias=expert_down_bias, block_cot=block_cot)


@jax.custom_vjp
def low(v):
    return lax.optimization_barrier(v.astype(jnp.bfloat16)).astype(jnp.float32)

@jax.custom_vjp
def low_back(v):
    return v

def low_keep(v):
    return (low(v), None)

def low_pass(kept, grad):
    return (grad,)

def back_keep(v):
    return (v, None)

def back_low(kept, grad):
    return (low(grad),)
low.defvjp(low_keep, low_pass)
low_back.defvjp(back_keep, back_low)
epsilon = 1e-05
negative = -1e+30
highest = lax.Precision.HIGHEST

def round_both(values):
    return low_back(low(values))

def matmul(left, right):
    return jnp.dot(left, right, precision=highest, preferred_element_type=jnp.float32)

def layer_norm(values, gain_row, offset):
    center = values - lax.optimization_barrier(jnp.mean(values, axis=-1, keepdims=True))
    variance = lax.optimization_barrier(jnp.mean(center * center, axis=-1, keepdims=True))
    return center * lax.rsqrt(variance + epsilon) * gain_row + offset

def sequence_group(tokens, segment, live_mask, params):
    first_gain, first_bias, query_weight, query_bias, key_weight, value_weight, value_bias, out_weight, out_bias = params
    slot_count, model_width = tokens.shape
    head_dim = model_width // HEADS
    query_rows = min(512, slot_count)
    normed = low(layer_norm(tokens, first_gain, first_bias))
    query = round_both(matmul(normed, query_weight) + query_bias)
    key_heads = round_both(matmul(normed, key_weight)).reshape(slot_count, HEADS, head_dim)
    value_heads = round_both(matmul(normed, value_weight) + value_bias).reshape(slot_count, HEADS, head_dim)
    key_pos = jnp.arange(slot_count, dtype=jnp.int32)

    def one_block(block_id):
        query_start = (block_id * query_rows).astype(jnp.int32)
        query_block = lax.dynamic_slice_in_dim(query, query_start, query_rows, 0).reshape(query_rows, HEADS, head_dim)
        scores = low_back(jnp.einsum('qhd,khd->hqk', query_block, key_heads, precision=highest) / math.sqrt(head_dim))
        query_pos = query_start + jnp.arange(query_rows, dtype=jnp.int32)
        query_seg = lax.dynamic_slice_in_dim(segment, query_start, query_rows, 0)
        query_live = lax.dynamic_slice_in_dim(live_mask, query_start, query_rows, 0) > 0.5
        allowed = (query_seg[:, None] == segment[None, :]) & (key_pos[None, :] <= query_pos[:, None]) & query_live[:, None] | (key_pos[None, :] == query_pos[:, None])
        masked = jnp.where(allowed[None], scores, negative)
        weights_low = low(jax.nn.softmax(masked, axis=-1))
        mixed_block = jnp.einsum('hqk,khd->qhd', weights_low, value_heads, precision=highest)
        return mixed_block.reshape(query_rows, model_width)
    block_ids = jnp.arange(slot_count // query_rows, dtype=jnp.int32)
    mixed_heads = round_both(lax.map(jax.checkpoint(one_block), block_ids).reshape(slot_count, model_width))
    return tokens + live_mask[:, None] * (matmul(mixed_heads, out_weight) + out_bias)

def expert_rows(routed, route_live, second_gain, second_bias, up_weight, up_bias, down_weight, down_bias):
    ffn_in = low(layer_norm(routed, second_gain, second_bias))
    pre_act = low_back(matmul(ffn_in, up_weight) + up_bias)
    activation = low(jax.nn.gelu(pre_act))
    return routed + route_live[:, None] * (matmul(activation, down_weight) + down_bias)

def reference(block_in, seq_lengths, slot_position, first_gain, first_bias, query_weight, query_bias, key_weight, value_weight, value_bias, out_weight, out_bias, second_gain, second_bias, expert_up, expert_up_bias, expert_down, expert_down_bias, block_cot):
    groups = N_EXPERT * N_DP
    cap_rows = SLOTS // N_EXPERT
    indices = jnp.arange(SLOTS, dtype=jnp.int32)
    inverse = jax.vmap(lambda order_row: jnp.zeros((SLOTS,), jnp.int32).at[order_row].set(indices))(slot_position)
    end_points = jnp.cumsum(seq_lengths, axis=1).astype(jnp.int32)
    segment = lax.optimization_barrier(jnp.sum((indices[None, :, None] >= end_points[:, None, :]).astype(jnp.int32), axis=2)).astype(jnp.int32)
    live_mask = (indices[None, :] < end_points[:, -1:]).astype(jnp.float32)
    sent_live = jnp.take_along_axis(live_mask, slot_position, axis=1)
    route_live = sent_live.reshape(N_EXPERT, N_DP, N_EXPERT, cap_rows).transpose(2, 1, 0, 3).reshape(N_EXPERT, N_DP * SLOTS)

    def forward(tokens_in, gain_one, bias_one, weight_query, bias_query, weight_key, weight_value, bias_value, weight_out, bias_out, gain_two, bias_two, up_all, up_bias_all, down_all, down_bias_all):
        shaped = tokens_in.reshape(N_EXPERT, N_DP, N_EXPERT, cap_rows, D)
        slotted = shaped.transpose(2, 1, 0, 3, 4).reshape(groups, SLOTS, D)
        tokens = jnp.take_along_axis(slotted, inverse[:, :, None], axis=1)
        params = (gain_one, bias_one, weight_query, bias_query, weight_key, weight_value, bias_value, weight_out, bias_out)

        def group_step(state, inputs):
            return (state, sequence_group(inputs[0], inputs[1], inputs[2], params))
        residual = lax.scan(jax.checkpoint(group_step), jnp.zeros((), jnp.float32), (tokens, segment, live_mask))[1]
        residual = round_both(residual)
        sent = jnp.take_along_axis(residual, slot_position[:, :, None], axis=1)
        routed = sent.reshape(N_EXPERT, N_DP, N_EXPERT, cap_rows, D).transpose(2, 1, 0, 3, 4).reshape(N_EXPERT, N_DP * SLOTS, D)

        def expert_step(state, inputs):
            return (state, expert_rows(inputs[0], inputs[1], gain_two, bias_two, inputs[2], inputs[3], inputs[4], inputs[5]))
        outputs = lax.scan(jax.checkpoint(expert_step), jnp.zeros((), jnp.float32), (routed, route_live, up_all, up_bias_all, down_all, down_bias_all))[1]
        return outputs.reshape(N_EXPERT * N_DP * SLOTS, D)
    primals = (block_in.astype(jnp.float32), first_gain, first_bias, query_weight.astype(jnp.float32), query_bias, key_weight.astype(jnp.float32), value_weight.astype(jnp.float32), value_bias, out_weight.astype(jnp.float32), out_bias, second_gain, second_bias, expert_up.astype(jnp.float32), expert_up_bias, expert_down.astype(jnp.float32), expert_down_bias)
    block_out, pullback = jax.vjp(forward, *primals)
    grads = pullback(block_cot.astype(jnp.float32))
    return (block_out.astype(jnp.bfloat16), grads[0].astype(jnp.bfloat16), grads[1], grads[2], grads[3], grads[4], grads[5], grads[6], grads[7], grads[8], grads[9], grads[10], grads[11], grads[12], grads[13], grads[14], grads[15])
```

```python
import functools
import math

import jax
import jax.numpy as jnp
from jax import lax
from jax.experimental import pallas as pl
from jax.experimental.pallas import tpu as pltpu
from jax.sharding import PartitionSpec as P

HEADS = 16
EPS = 1e-05
NEG = -1e30
LOG2E = math.log2(math.e)
F32 = jnp.float32
BF16 = jnp.bfloat16
VMEM_LIMIT = 60 * 1024 * 1024
ROWS = 256


def nn(a, b):
    return lax.dot_general(a, b, (((1,), (0,)), ((), ())), preferred_element_type=F32)


def nt(a, b):
    return lax.dot_general(a, b, (((1,), (1,)), ((), ())), preferred_element_type=F32)


def tn(a, b):
    return lax.dot_general(a, b, (((0,), (0,)), ((), ())), preferred_element_type=F32)


def params(**more):
    return pltpu.CompilerParams(vmem_limit_bytes=VMEM_LIMIT, **more)


def cost(flops, bytes_accessed, transcendentals=0):
    return pl.CostEstimate(
        flops=int(flops), bytes_accessed=int(bytes_accessed), transcendentals=int(transcendentals)
    )


def whole(shape):
    return pl.BlockSpec(shape, lambda *_: (0,) * len(shape))


def rows_of(block, width):
    return pl.BlockSpec((block, width), lambda i, *_: (i, 0))


def norm_parts(values):
    mean = jnp.mean(values, axis=-1, keepdims=True)
    center = values - mean
    variance = jnp.mean(center * center, axis=-1, keepdims=True)
    root = lax.rsqrt(variance + EPS)
    return center * root, root


def norm_grad(grad, normal, root, gain):
    scaled = grad * gain
    mean_plain = jnp.mean(scaled, axis=-1, keepdims=True)
    mean_normal = jnp.mean(scaled * normal, axis=-1, keepdims=True)
    return root * (scaled - mean_plain - normal * mean_normal)


def pick_rows(first_row, pos_row, rows, count):
    ids = lax.broadcasted_iota(jnp.int32, (rows, count), 0) + first_row
    return jnp.where(ids == pos_row, 1.0, 0.0).astype(BF16)


def pick_slots(pos_col, count):
    ids = lax.broadcasted_iota(jnp.int32, (pos_col.shape[0], count), 1)
    return jnp.where(ids == pos_col, 1.0, 0.0).astype(BF16)


def entry_kernel(parts, *refs):
    slots = refs[:parts]
    pos_row, gain, offset, wq, bq, wk, wv, bv, tokens, normed, q, k, v = refs[parts:]
    i = pl.program_id(0)
    arrived = jnp.concatenate([r[...] for r in slots], axis=0)
    count = arrived.shape[0]
    rows = tokens.shape[0]
    picked = nn(pick_rows(i * rows, pos_row[...], rows, count), arrived)
    tokens[...] = picked.astype(BF16)
    normal, _ = norm_parts(picked)
    low = (normal * gain[...] + offset[...]).astype(BF16)
    normed[...] = low
    q[...] = ((nn(low, wq[...]) + bq[...]).astype(BF16).astype(F32) * 0.125).astype(BF16)
    k[...] = nn(low, wk[...]).astype(BF16)
    v[...] = (nn(low, wv[...]) + bv[...]).astype(BF16)


def entry(slots, pos_row, gain, offset, wq, bq, wk, wv, bv):
    parts = len(slots)
    piece, width = slots[0].shape
    count = piece * parts
    out = jax.ShapeDtypeStruct((count, width), BF16)
    return pl.pallas_call(
        functools.partial(entry_kernel, parts),
        grid=(count // ROWS,),
        in_specs=[whole((piece, width))] * parts
        + [whole((1, count))]
        + [whole((1, width))] * 2
        + [whole((width, width)), whole((1, width)), whole((width, width)), whole((width, width)), whole((1, width))],
        out_specs=[rows_of(ROWS, width)] * 5,
        out_shape=[out] * 5,
        compiler_params=params(),
        cost_estimate=cost(8 * count * width * width, 18 * count * width),
        name="entry",
    )(*slots, pos_row, gain, offset, wq, bq, wk, wv, bv)


def half_masks(width):
    lane = lax.broadcasted_iota(jnp.int32, (1, width), 1)
    return lane < width // 2


def split_heads(values):
    first = half_masks(values.shape[1])
    zero = jnp.zeros_like(values)
    return jnp.where(first, values, zero), jnp.where(first, zero, values)


def attend_kernel(start_col, q_ref, k_ref, v_ref, mixed_ref, lse_ref, bias):
    count = q_ref.shape[0]

    @pl.when(pl.program_id(0) == 0)
    def _():
        for i in range(count // ROWS):
            ext = (i + 1) * ROWS
            rows = pl.ds(i * ROWS, ROWS)
            kpos = lax.broadcasted_iota(jnp.int32, (ROWS, ext), 1)
            qpos = lax.broadcasted_iota(jnp.int32, (ROWS, ext), 0) + i * ROWS
            keep = (kpos >= start_col[rows, :]) & (kpos <= qpos)
            bias[rows, :ext] = jnp.where(keep, 0.0, NEG)

    values = split_heads(v_ref[...])
    keys = k_ref[...]
    first = half_masks(q_ref.shape[1])
    for i in range(count // ROWS):
        ext = (i + 1) * ROWS
        rows = pl.ds(i * ROWS, ROWS)
        total = None
        stats = []
        for query, value in zip(split_heads(q_ref[rows, :]), values):
            score = nt(query, keys[:ext]) * LOG2E + bias[rows, :ext]
            top = jnp.max(score, axis=1, keepdims=True)
            terms = jnp.exp2(score - top)
            sums = jnp.sum(terms, axis=1, keepdims=True)
            part = nn(terms.astype(BF16), value[:ext])
            total = part if total is None else total + part
            stats.append((top + jnp.log2(sums), 1.0 / sums))
        scale = jnp.where(first, stats[0][1], stats[1][1])
        mixed_ref[rows, :] = (total * scale).astype(BF16)
        both = jnp.where(first, stats[0][0], stats[1][0])
        turned = both.T
        lse_ref[0, 0:1, rows] = turned[0:1, :]
        lse_ref[0, 1:2, rows] = turned[64:65, :]


def attend(start_col, q, k, v):
    count, width = q.shape
    pairs = HEADS // 2
    lanes = width // pairs
    col = pl.BlockSpec((count, lanes), lambda p: (0, p))
    return pl.pallas_call(
        attend_kernel,
        grid=(pairs,),
        in_specs=[whole((count, 1)), col, col, col],
        out_specs=[col, pl.BlockSpec((1, 8, count), lambda p: (p, 0, 0))],
        out_shape=[
            jax.ShapeDtypeStruct((count, width), BF16),
            jax.ShapeDtypeStruct((pairs, 8, count), F32),
        ],
        scratch_shapes=[pltpu.VMEM((count, count), F32)],
        compiler_params=params(),
        cost_estimate=cost(8 * count * count * width, 8 * count * width, HEADS * count * count // 2),
        name="attend",
    )(start_col, q, k, v)


def leave_kernel(parts, mixed, wo, bo, tokens, live_col, pos_col, *refs):
    outs, kept = refs[:parts], refs[parts]
    i = pl.program_id(0)
    rows = mixed.shape[0]
    branch = nn(mixed[...], wo[...]) + bo[...]
    kept[pl.ds(pl.multiple_of(i * rows, rows), rows), :] = (
        tokens[...].astype(F32) + live_col[...] * branch
    ).astype(BF16)

    @pl.when(i == pl.num_programs(0) - 1)
    def _():
        count = kept.shape[0]
        piece = count // parts
        for r in range(parts):
            chosen = pick_slots(pos_col[pl.ds(r * piece, piece), :], count)
            outs[r][...] = nn(chosen, kept[...]).astype(BF16)


def leave(parts, mixed, wo, bo, tokens, live_col, pos_col):
    count, width = mixed.shape
    piece = count // parts
    return pl.pallas_call(
        functools.partial(leave_kernel, parts),
        grid=(count // ROWS,),
        in_specs=[
            rows_of(ROWS, width),
            whole((width, width)),
            whole((1, width)),
            rows_of(ROWS, width),
            rows_of(ROWS, 1),
            whole((count, 1)),
        ],
        out_specs=[whole((piece, width))] * parts,
        out_shape=[jax.ShapeDtypeStruct((piece, width), BF16)] * parts,
        scratch_shapes=[pltpu.VMEM((count, width), BF16)],
        compiler_params=params(),
        cost_estimate=cost(4 * count * width * width, 8 * count * width),
        name="leave",
    )(mixed, wo, bo, tokens, live_col, pos_col)


def reenter_kernel(parts, *refs):
    slots = refs[:parts]
    pos_row, live_col, wo, grad_residual, grad_proj, grad_mixed, bias_sum = refs[parts:]
    i = pl.program_id(0)
    arrived = jnp.concatenate([r[...] for r in slots], axis=0)
    rows = grad_residual.shape[0]
    picked = nn(pick_rows(i * rows, pos_row[...], rows, arrived.shape[0]), arrived)
    grad_residual[...] = picked.astype(BF16)
    masked = live_col[...] * picked
    low = masked.astype(BF16)
    grad_proj[...] = low
    grad_mixed[...] = nt(low, wo[...]).astype(BF16)

    @pl.when(i == 0)
    def _():
        bias_sum[...] = jnp.zeros_like(bias_sum)

    bias_sum[...] += jnp.sum(masked, axis=0, keepdims=True)


def reenter(slots, pos_row, live_col, wo):
    parts = len(slots)
    piece, width = slots[0].shape
    count = piece * parts
    out = jax.ShapeDtypeStruct((count, width), BF16)
    return pl.pallas_call(
        functools.partial(reenter_kernel, parts),
        grid=(count // ROWS,),
        in_specs=[whole((piece, width))] * parts
        + [whole((1, count)), rows_of(ROWS, 1), whole((width, width))],
        out_specs=[rows_of(ROWS, width)] * 3 + [whole((1, width))],
        out_shape=[out] * 3 + [jax.ShapeDtypeStruct((1, width), F32)],
        compiler_params=params(),
        cost_estimate=cost(4 * count * width * width, 10 * count * width),
        name="reenter",
    )(*slots, pos_row, live_col, wo)


def attend_back_kernel(
    start_row, q_ref, k_ref, v_ref, o_ref, g_ref, lse_ref, dq_ref, dk_ref, dv_ref, bias, dq_sum
):
    count, lanes = q_ref.shape

    @pl.when(pl.program_id(0) == 0)
    def _():
        for j in range(count // ROWS):
            cols = pl.ds(j * ROWS, count - j * ROWS)
            shape = (ROWS, count - j * ROWS)
            kpos = lax.broadcasted_iota(jnp.int32, shape, 0) + j * ROWS
            qpos = lax.broadcasted_iota(jnp.int32, shape, 1) + j * ROWS
            keep = (kpos >= start_row[:, cols]) & (kpos <= qpos)
            bias[pl.ds(j * ROWS, ROWS), cols] = jnp.where(keep, 0.0, NEG)

    products = o_ref[...].astype(F32) * g_ref[...].astype(F32)
    high = products.astype(BF16)
    low = (products - high.astype(F32)).astype(BF16)
    sel_row = lax.broadcasted_iota(jnp.int32, (8, lanes), 0)
    sel_lane = lax.broadcasted_iota(jnp.int32, (8, lanes), 1)
    select = jnp.where(sel_row == sel_lane // (lanes // 2), 1.0, 0.0).astype(BF16)
    deltas = nt(select, high) + nt(select, low)

    queries = split_heads(q_ref[...])
    grads = split_heads(g_ref[...])
    for j in range(count // ROWS):
        rows = pl.ds(j * ROWS, ROWS)
        ext = slice(j * ROWS, count)
        keys, vals = k_ref[rows, :], v_ref[rows, :]
        dk = dv = dq = None
        for h, key in enumerate(split_heads(keys)):
            query, grad = queries[h][ext], grads[h][ext]
            score = nt(keys, query) * LOG2E + bias[rows, ext]
            weights = jnp.exp2(score - lse_ref[0, h : h + 1, ext])
            weights_low = weights.astype(BF16)
            grad_weights = nt(vals, grad)
            grad_score = (weights * (grad_weights - deltas[h : h + 1, ext])).astype(BF16)
            dv_part = nn(weights_low, grad)
            dk_part = nn(grad_score, query)
            dq_part = tn(grad_score, key)
            dv = dv_part if dv is None else dv + dv_part
            dk = dk_part if dk is None else dk + dk_part
            dq = dq_part if dq is None else dq + dq_part
        dk_ref[rows, :] = dk.astype(BF16)
        dv_ref[rows, :] = dv.astype(BF16)
        if j == 0:
            dq_sum[...] = dq
        else:
            dq_sum[ext, :] += dq
    dq_ref[...] = (dq_sum[...] * 0.125).astype(BF16)


def attend_back(start_row, q, k, v, mixed, grad_mixed, lse):
    count, width = q.shape
    pairs = HEADS // 2
    lanes = width // pairs
    col = pl.BlockSpec((count, lanes), lambda p: (0, p))
    out = jax.ShapeDtypeStruct((count, width), BF16)
    return pl.pallas_call(
        attend_back_kernel,
        grid=(pairs,),
        in_specs=[whole((1, count))]
        + [col] * 5
        + [pl.BlockSpec((1, 8, count), lambda p: (p, 0, 0))],
        out_specs=[col] * 3,
        out_shape=[out] * 3,
        scratch_shapes=[pltpu.VMEM((count, count), F32), pltpu.VMEM((count, lanes), F32)],
        compiler_params=params(),
        cost_estimate=cost(20 * count * count * width, 16 * count * width, HEADS * count * count // 2),
        name="attend_back",
    )(start_row, q, k, v, mixed, grad_mixed, lse)


def finish_kernel(
    parts, dq, dk, dv, wq, wk, wv, tokens, grad_residual, gain, pos_col, *refs
):
    outs = refs[:parts]
    sums, kept = refs[parts:]
    i = pl.program_id(0)
    rows = dq.shape[0]
    grad = nt(dq[...], wq[...]) + nt(dk[...], wk[...]) + nt(dv[...], wv[...])
    normal, root = norm_parts(tokens[...].astype(F32))
    kept[pl.ds(pl.multiple_of(i * rows, rows), rows), :] = (
        grad_residual[...].astype(F32) + norm_grad(grad, normal, root, gain[...])
    ).astype(BF16)

    @pl.when(i == 0)
    def _():
        sums[...] = jnp.zeros_like(sums)

    sums[0:1, :] += jnp.sum(grad * normal, axis=0, keepdims=True)
    sums[1:2, :] += jnp.sum(grad, axis=0, keepdims=True)
    sums[2:3, :] += jnp.sum(dq[...].astype(F32), axis=0, keepdims=True)
    sums[3:4, :] += jnp.sum(dv[...].astype(F32), axis=0, keepdims=True)

    @pl.when(i == pl.num_programs(0) - 1)
    def _():
        count = kept.shape[0]
        piece = count // parts
        for r in range(parts):
            chosen = pick_slots(pos_col[pl.ds(r * piece, piece), :], count)
            outs[r][...] = nn(chosen, kept[...]).astype(BF16)


def finish(parts, dq, dk, dv, wq, wk, wv, tokens, grad_residual, gain, pos_col):
    count, width = dq.shape
    piece = count // parts
    return pl.pallas_call(
        functools.partial(finish_kernel, parts),
        grid=(count // ROWS,),
        in_specs=[rows_of(ROWS, width)] * 3
        + [whole((width, width))] * 3
        + [rows_of(ROWS, width)] * 2
        + [whole((1, width)), whole((count, 1))],
        out_specs=[whole((piece, width))] * parts + [whole((8, width))],
        out_shape=[jax.ShapeDtypeStruct((piece, width), BF16)] * parts
        + [jax.ShapeDtypeStruct((8, width), F32)],
        scratch_shapes=[pltpu.VMEM((count, width), BF16)],
        compiler_params=params(),
        cost_estimate=cost(8 * count * width * width, 20 * count * width),
        name="finish",
    )(dq, dk, dv, wq, wk, wv, tokens, grad_residual, gain, pos_col)


GELU_ROOT = math.sqrt(2.0 / math.pi)
GELU_CUBE = 0.044715
STEP = 512


def expert_kernel(parts, shards, first_chunk, source, *refs):
    it = iter(refs)
    take = lambda n: [next(it) for _ in range(n)]
    slots, cots, lives = take(parts), take(parts), take(parts)
    ups, downs = take(shards), take(shards)
    up_bias, down_bias, gain, offset = take(4)
    if not first_chunk:
        take(5)
    grads = take(parts)
    act_out, pre_out, ffn_out, branch_out, block_out, sums, up_sums = take(7)
    up, down, out_sum, grad_sum, out_low, up_sem, down_sem, out_sem = take(8)

    up_copies = [pltpu.make_async_copy(ups[k], up.at[k], up_sem.at[k]) for k in range(shards)]
    down_copies = [pltpu.make_async_copy(downs[k], down.at[k], down_sem.at[k]) for k in range(shards)]
    for k in range(shards):
        up_copies[k].start()
        down_copies[k].start()

    routed = jnp.concatenate([r[...] for r in slots], axis=0).astype(F32)
    cot = jnp.concatenate([r[...] for r in cots], axis=0).astype(F32)
    live = jnp.concatenate([r[...] for r in lives], axis=0)
    normal, root = norm_parts(routed)
    ffn_in = (normal * gain[...] + offset[...]).astype(BF16)
    branch = (live * cot).astype(BF16)
    ffn_out[...] = ffn_in
    branch_out[...] = branch
    out_sum[...] = jnp.broadcast_to(down_bias[...], out_sum.shape)
    grad_sum[...] = jnp.zeros_like(grad_sum)
    width = up.shape[2]
    for k in range(shards):
        up_copies[k].wait()
        down_copies[k].wait()

        for c in range(0, width, STEP):
            cols = pl.ds(c, STEP)
            pre = nn(ffn_out[...], up[k, :, cols]) + up_bias[k, :, cols]
            square = pre * pre
            tanh = jnp.tanh(pre * (GELU_ROOT + (GELU_ROOT * GELU_CUBE) * square))
            half = 0.5 * (1.0 + tanh)
            act = (pre * half).astype(BF16)
            slope = half + (0.5 * pre) * (1.0 - tanh * tanh) * (
                GELU_ROOT + (3.0 * GELU_ROOT * GELU_CUBE) * square
            )
            act_out[k, :, cols] = act
            grad_pre = (nt(branch_out[...], down[k, cols, :]) * slope).astype(BF16)
            pre_out[k, :, cols] = grad_pre
            up_sums[k, :, cols] = jnp.sum(grad_pre.astype(F32), axis=0, keepdims=True)
            grad_sum[...] += nt(grad_pre, up[k, :, cols])
            out_sum[...] += nn(act, down[k, cols, :])
    grad = grad_sum[...]
    grad_routed = (cot + norm_grad(grad, normal, root, gain[...])).astype(BF16)
    out_low[...] = (routed + live * out_sum[...]).astype(BF16)
    piece = slots[0].shape[0]
    out_copies = []
    for j in range(parts):
        grads[j][...] = grad_routed[j * piece : (j + 1) * piece]
        place = pl.multiple_of(source[j] * piece, piece)
        copy = pltpu.make_async_copy(
            out_low.at[pl.ds(j * piece, piece)], block_out.at[pl.ds(place, piece)], out_sem.at[j]
        )
        copy.start()
        out_copies.append(copy)
    sums[...] = jnp.zeros_like(sums)
    sums[0:1, :] = jnp.sum(grad * normal, axis=0, keepdims=True)
    sums[1:2, :] = jnp.sum(grad, axis=0, keepdims=True)
    sums[2:3, :] = jnp.sum(branch.astype(F32), axis=0, keepdims=True)
    for copy in out_copies:
        copy.wait()


def expert_chunk(chunk, source, slots, cot, live, ups, downs, up_bias, down_bias, gain, offset, carried):
    parts, shards = len(slots), len(ups)
    piece, width = slots[0].shape
    rows = parts * piece
    count = cot.shape[0]
    part = ups[0].shape[1]
    picked = lambda j, w: pl.BlockSpec((piece, w), lambda i, source, j=j: (source[j], 0))
    anywhere = pl.BlockSpec(memory_space=pl.ANY)
    big = pl.BlockSpec((shards, rows, part), lambda *_: (0, chunk, 0))
    flat = pl.BlockSpec((rows, width), lambda *_: (chunk, 0))
    first = carried is None
    previous = [] if first else list(carried)
    before = 1 + 3 * parts + 2 * shards + 4
    full = jax.ShapeDtypeStruct((count, width), BF16)
    wide = jax.ShapeDtypeStruct((shards, count, part), BF16)
    outs = pl.pallas_call(
        functools.partial(expert_kernel, parts, shards, first),
        grid_spec=pltpu.PrefetchScalarGridSpec(
            num_scalar_prefetch=1,
            grid=(1,),
            in_specs=[whole((piece, width))] * parts
            + [picked(j, width) for j in range(parts)]
            + [picked(j, 1) for j in range(parts)]
            + [anywhere] * (2 * shards)
            + [whole((shards, 1, part)), whole((1, width)), whole((1, width)), whole((1, width))]
            + [anywhere] * len(previous),
            out_specs=[whole((piece, width))] * parts
            + [big, big, flat, flat, anywhere, whole((8, width)), whole((shards, 1, part))],
            scratch_shapes=[
                pltpu.VMEM((shards, width, part), BF16),
                pltpu.VMEM((shards, part, width), BF16),
                pltpu.VMEM((rows, width), F32),
                pltpu.VMEM((rows, width), F32),
                pltpu.VMEM((rows, width), BF16),
                pltpu.SemaphoreType.DMA((shards,)),
                pltpu.SemaphoreType.DMA((shards,)),
                pltpu.SemaphoreType.DMA((parts,)),
            ],
        ),
        out_shape=[jax.ShapeDtypeStruct((piece, width), BF16)] * parts
        + [wide, wide, full, full, full]
        + [jax.ShapeDtypeStruct((8, width), F32), jax.ShapeDtypeStruct((shards, 1, part), F32)],
        input_output_aliases={before + n: parts + n for n in range(len(previous))},
        compiler_params=params(),
        cost_estimate=cost(
            8 * rows * width * part * shards, 4 * shards * width * part, rows * part * shards
        ),
        name="expert_chunk",
    )(
        source,
        *slots,
        *([cot] * parts),
        *([live] * parts),
        *ups,
        *downs,
        up_bias,
        down_bias,
        gain,
        offset,
        *previous,
    )
    grads = outs[:parts]
    return grads, outs[parts : parts + 5], outs[parts + 5], outs[parts + 6]


def expert_grads_kernel(act, pre, ffn_in, branch, down_out, up_out):
    down_out[0] = tn(act[0], branch[...]).astype(BF16)
    up_out[0] = tn(ffn_in[...], pre[0]).astype(BF16)


def expert_grads(first, step, act, pre, ffn_in, branch):
    shards, count, part = act.shape
    width = ffn_in.shape[1]
    number = shards // step
    pick = pl.BlockSpec((1, count, part), lambda i: (first + step * i, 0, 0))
    return pl.pallas_call(
        expert_grads_kernel,
        grid=(number,),
        in_specs=[pick, pick, whole((count, width)), whole((count, width))],
        out_specs=[
            pl.BlockSpec((1, part, width), lambda i: (i, 0, 0)),
            pl.BlockSpec((1, width, part), lambda i: (i, 0, 0)),
        ],
        out_shape=[
            jax.ShapeDtypeStruct((number, part, width), BF16),
            jax.ShapeDtypeStruct((number, width, part), BF16),
        ],
        compiler_params=params(),
        cost_estimate=cost(4 * number * count * width * part, 10 * number * width * part),
        name="expert_grads",
    )(act, pre, ffn_in, branch)


def shared_grads_kernel(blocks, code, left, right, keep, send, total):
    total[...] = tn(left[...], right[...])
    size = total.shape[0] // blocks
    half = blocks // 2
    for j in range(blocks):
        place = pl.multiple_of((code[0] ^ j) * size, size)
        target = keep if j < half else send
        target[0, pl.ds((j % half) * size, size), :] = total[pl.ds(place, size), :].astype(BF16)


def shared_grads(blocks, code, left, rights):
    count, width = left.shape
    number = len(rights)
    if number > 1:
        raise NotImplementedError
    half = pl.BlockSpec((1, width // 2, width), lambda i, *_: (0, 0, 0))
    return pl.pallas_call(
        functools.partial(shared_grads_kernel, blocks),
        grid_spec=pltpu.PrefetchScalarGridSpec(
            num_scalar_prefetch=1,
            grid=(1,),
            in_specs=[whole((count, width))] * 2,
            out_specs=[half, half],
            scratch_shapes=[pltpu.VMEM((width, width), F32)],
        ),
        out_shape=[jax.ShapeDtypeStruct((1, width // 2, width), BF16)] * 2,
        compiler_params=params(),
        cost_estimate=cost(2 * count * width * width, 6 * width * width),
        name="shared_grads",
    )(code, left, rights[0])


def unmix_kernel(blocks, code, low, high, out):
    half = blocks // 2
    size = out.shape[0] // blocks
    for j in range(blocks):
        place = pl.multiple_of((code[0] ^ j) * size, size)
        source = low if j < half else high
        out[pl.ds(place, size), :] = source[0, pl.ds((j % half) * size, size), :].astype(F32)


def unmix(blocks, code, low, high):
    _, rows, width = low.shape
    half = pl.BlockSpec((1, rows, width), lambda i, *_: (0, 0, 0))
    return pl.pallas_call(
        functools.partial(unmix_kernel, blocks),
        grid_spec=pltpu.PrefetchScalarGridSpec(
            num_scalar_prefetch=1,
            grid=(1,),
            in_specs=[half, half],
            out_specs=whole((2 * rows, width)),
        ),
        out_shape=jax.ShapeDtypeStruct((2 * rows, width), F32),
        compiler_params=params(),
        cost_estimate=cost(2 * rows * width, 12 * rows * width),
        name="unmix",
    )(code, low, high)


def assemble_kernel(parts, source, *refs):
    pieces, out, sem = refs[:parts], refs[parts], refs[parts + 1]
    size = pieces[0].shape[0]
    copies = []
    for r in range(parts):
        place = pl.multiple_of(source[r] * size, size)
        copies.append(pltpu.make_async_copy(pieces[r], out.at[pl.ds(place, size)], sem.at[r]))
    for copy in copies:
        copy.start()
    for copy in copies:
        copy.wait()


def assemble(source, pieces):
    parts = len(pieces)
    size, width = pieces[0].shape
    anywhere = pl.BlockSpec(memory_space=pl.ANY)
    return pl.pallas_call(
        functools.partial(assemble_kernel, parts),
        grid_spec=pltpu.PrefetchScalarGridSpec(
            num_scalar_prefetch=1,
            grid=(1,),
            in_specs=[anywhere] * parts,
            out_specs=anywhere,
            scratch_shapes=[pltpu.SemaphoreType.DMA((parts,))],
        ),
        out_shape=jax.ShapeDtypeStruct((parts * size, width), BF16),
        compiler_params=params(),
        cost_estimate=cost(0, 4 * parts * size * width),
        name="assemble",
    )(source, *pieces)


def turn(values, axis, size, by):
    return lax.ppermute(values, axis, [(i, (i + by) % size) for i in range(size)])


def swap(values, axis, size, bit):
    return lax.ppermute(values, axis, [(i, i ^ bit) for i in range(size)])


def swap_steps(n_expert, n_dp):
    bits_dp = [1 << b for b in range(n_dp.bit_length() - 1)]
    bits_expert = [1 << b for b in range(n_expert.bit_length() - 1)]
    steps = []
    for n in range(max(len(bits_dp), len(bits_expert))):
        if n < len(bits_dp):
            steps.append(("dp", n_dp, bits_dp[n]))
        if n < len(bits_expert):
            steps.append(("expert", n_expert, bits_expert[n]))
    return steps


def add_low(left, right):
    return (left.astype(F32) + right.astype(F32)).astype(BF16)


class SharedSum:
    def __init__(self, n_expert, n_dp, rows):
        steps = swap_steps(n_expert, n_dp)
        cut = 0
        while cut < len(steps) and rows >> (cut + 1) >= 32:
            cut += 1
        self.halving, self.whole_steps = steps[:cut], steps[cut:]
        self.blocks = 1 << cut
        code = jnp.int32(0)
        for axis, _, bit in self.halving:
            code = code * 2 + (lax.axis_index(axis) // bit) % 2
        self.code = code.astype(jnp.int32).reshape(1)

    def __call__(self, keep, send):
        for n, (axis, size, bit) in enumerate(self.halving):
            total = add_low(keep, swap(send, axis, size, bit))
            if n + 1 < len(self.halving):
                middle = total.shape[1] // 2
                keep, send = total[:, :middle], total[:, middle:]
        for axis, size, bit in self.whole_steps:
            total = add_low(total, swap(total, axis, size, bit))
        for n, (axis, size, bit) in reversed(list(enumerate(self.halving))):
            other = swap(total, axis, size, bit)
            if n > 0:
                total = jnp.concatenate([total, other], axis=1)
        return unmix(self.blocks, self.code, total, other)


def small_sum(values, n_expert, n_dp):
    for axis, size, bit in swap_steps(n_expert, n_dp):
        values = values + swap(values, axis, size, bit)
    return values


def per_device(
    n_expert,
    n_dp,
    block_in,
    seq_lengths,
    slot_position,
    first_gain,
    first_bias,
    query_weight,
    query_bias,
    key_weight,
    value_weight,
    value_bias,
    out_weight,
    out_bias,
    second_gain,
    second_bias,
    expert_up,
    expert_up_bias,
    expert_down,
    expert_down_bias,
    block_cot,
):
    count, width = block_in.shape
    piece = count // n_expert
    row = lambda v: v.reshape(1, -1)
    e = lax.axis_index("expert")
    d = lax.axis_index("dp")
    part = expert_up.shape[2]

    def gathered(own):
        found = [own]
        bit = 1
        own_list = [own]
        far = [own]
        bits = [1 << b for b in range(n_dp.bit_length() - 1)]
        shards = {0: own}
        for bit in reversed(bits):
            for k in list(shards):
                shards[k | bit] = swap(shards[k], "dp", n_dp, bit)
        return [shards[k] for k in range(n_dp)]

    blocks = block_in.reshape(n_expert, piece, width)
    arrived = []
    for r in range(n_expert):
        block = lax.dynamic_index_in_dim(blocks, (e - r) % n_expert, 0, keepdims=False)
        arrived.append(block if r == 0 else turn(block, "expert", n_expert, -r))
    ups, downs = gathered(expert_up[0]), gathered(expert_down[0])

    position = slot_position[0]
    ends = jnp.cumsum(seq_lengths[0])
    total_live = ends[-1]
    ids = jnp.arange(count, dtype=jnp.int32)
    live = ids < total_live
    begin = jnp.max(jnp.where(ends[None, :] <= ids[:, None], ends[None, :], 0), axis=1)
    begin = jnp.where(live, begin, ids).astype(jnp.int32)
    live_col = live.astype(F32).reshape(count, 1)
    turned = jnp.roll(position.reshape(n_expert, piece), -e, axis=0).reshape(count)
    pos_row, pos_col = turned.reshape(1, count), turned.reshape(count, 1)
    slot_live = (position < total_live).astype(F32).reshape(n_expert, piece)
    route_live = lax.all_to_all(slot_live, "expert", split_axis=0, concat_axis=0, tiled=True)
    route_live = route_live.reshape(count, 1)

    tokens, normed, query, key, value = entry(
        arrived, pos_row, row(first_gain), row(first_bias), query_weight, row(query_bias),
        key_weight, value_weight, row(value_bias),
    )
    mixed, lse = attend(begin.reshape(count, 1), query, key, value)
    sent = leave(n_expert, mixed, out_weight, row(out_bias), tokens, live_col, pos_col)

    routed = [v if r == 0 else turn(v, "expert", n_expert, r) for r, v in enumerate(sent)]
    order = [0]
    for n in range(1, n_expert):
        order.append((n + 1) // 2 if n % 2 else n_expert - n // 2)
    chunks = min(CHUNKS, n_expert)
    per = n_expert // chunks
    shard_order = jnp.arange(n_dp, dtype=jnp.int32) ^ d
    up_bias = jnp.take(expert_up_bias[0].reshape(n_dp, 1, part), shard_order, axis=0)
    carried = None
    returned = [None] * n_expert
    sums, up_sums = 0.0, 0.0
    for c in range(chunks):
        turns = order[c * per : (c + 1) * per]
        source = jnp.stack([(e - r) % n_expert for r in turns]).astype(jnp.int32)
        grads, carried, chunk_sums, chunk_up = expert_chunk(
            c, source, [routed[r] for r in turns], block_cot, route_live, ups, downs, up_bias,
            row(expert_down_bias[0]), row(second_gain), row(second_bias), carried,
        )
        sums, up_sums = sums + chunk_sums, up_sums + chunk_up
        for r, grad in zip(turns, grads):
            returned[r] = grad if r == 0 else turn(grad, "expert", n_expert, -r)
    act, grad_pre, ffn_in, branch, block_out = carried

    down_send, up_send = expert_grads(1, 2, act, grad_pre, ffn_in, branch)
    down_got, up_got = swap(down_send, "dp", n_dp, 1), swap(up_send, "dp", n_dp, 1)
    down_keep, up_keep = expert_grads(0, 2, act, grad_pre, ffn_in, branch)

    def reduced(keep, got):
        bits = [1 << b for b in range(1, n_dp.bit_length() - 1)]
        for bit in reversed(bits):
            middle = keep.shape[0] // 2
            other = swap(add_low(keep[middle:], got[middle:]), "dp", n_dp, bit)
            keep, got = keep[:middle].astype(F32) + got[:middle].astype(F32), other
        return keep + got.astype(F32)

    grad_down, grad_up = reduced(down_keep, down_got), reduced(up_keep, up_got)
    bias_sums = up_sums.reshape(n_dp, part)
    down_bias_sums = sums[2:3]
    for bit in [1 << b for b in range(n_dp.bit_length() - 1)]:
        packed = jnp.concatenate([bias_sums, down_bias_sums.reshape(-1, part)], axis=0)
        other = swap(packed, "dp", n_dp, bit)
        bias_sums = bias_sums + other[jnp.array([k ^ bit for k in range(n_dp)])]
        down_bias_sums = down_bias_sums + other[n_dp:].reshape(1, width)
    grad_up_bias = bias_sums[0:1]
    share = width // n_dp
    grad_down_bias = lax.dynamic_slice_in_dim(down_bias_sums, d * share, share, 1)

    grad_residual, grad_proj, grad_mixed, out_bias_sum = reenter(
        returned, pos_row, live_col, out_weight
    )
    shared = SharedSum(n_expert, n_dp, width)
    grad_out_weight = shared(*shared_grads(shared.blocks, shared.code, mixed, [grad_proj]))
    grad_query, grad_key, grad_value = attend_back(
        begin.reshape(1, count), query, key, value, mixed, grad_mixed, lse
    )
    *leaving, token_sums = finish(
        n_expert, grad_query, grad_key, grad_value, query_weight, key_weight, value_weight,
        tokens, grad_residual, row(first_gain), pos_col,
    )
    received = [v if r == 0 else turn(v, "expert", n_expert, r) for r, v in enumerate(leaving)]
    sources = jnp.stack([(e - r) % n_expert for r in range(n_expert)]).astype(jnp.int32)
    input_grad = assemble(sources, received)
    grad_query_weight, grad_key_weight, grad_value_weight = (
        shared(*shared_grads(shared.blocks, shared.code, normed, [g]))
        for g in (grad_query, grad_key, grad_value)
    )
    small = jnp.concatenate(
        [token_sums[0:4], out_bias_sum, sums[0:2], jnp.zeros((1, width), F32)], axis=0
    )
    small = small_sum(small, n_expert, n_dp)
    return (
        block_out,
        input_grad,
        small[0],
        small[1],
        grad_query_weight,
        small[2],
        grad_key_weight,
        grad_value_weight,
        small[3],
        grad_out_weight,
        small[4],
        small[5],
        small[6],
        grad_up,
        grad_up_bias,
        grad_down,
        grad_down_bias,
    )


CHUNKS = 4


def solution(mesh):
    both = P(("expert", "dp"), None)
    return jax.shard_map(
        functools.partial(per_device, mesh.shape["expert"], mesh.shape["dp"]),
        mesh=mesh,
        in_specs=(both,) * 3
        + (P(),) * 11
        + (P("expert", None, "dp"), P("expert", None), P("expert", "dp", None), P("expert", None), both),
        out_specs=(both,) * 2
        + (P(),) * 11
        + (P("expert", None, "dp"), P("expert", "dp"), P("expert", "dp", None), P("expert", "dp")),
        check_vma=False,
    )
```

```python
import functools
import math

import jax
import jax.numpy as jnp
from jax import lax
from jax.experimental import pallas as pl
from jax.experimental.pallas import tpu as pltpu
from jax.sharding import PartitionSpec as P

HEADS = 16
EPS = 1e-05
NEG = -1e30
LOG2E = math.log2(math.e)
F32 = jnp.float32
BF16 = jnp.bfloat16
VMEM_LIMIT = 60 * 1024 * 1024
ROWS = 256


def nn(a, b):
    return lax.dot_general(a, b, (((1,), (0,)), ((), ())), preferred_element_type=F32)


def nt(a, b):
    return lax.dot_general(a, b, (((1,), (1,)), ((), ())), preferred_element_type=F32)


def tn(a, b):
    return lax.dot_general(a, b, (((0,), (0,)), ((), ())), preferred_element_type=F32)


def params(**more):
    return pltpu.CompilerParams(vmem_limit_bytes=VMEM_LIMIT, **more)


def cost(flops, bytes_accessed, transcendentals=0):
    return pl.CostEstimate(
        flops=int(flops), bytes_accessed=int(bytes_accessed), transcendentals=int(transcendentals)
    )


def whole(shape):
    return pl.BlockSpec(shape, lambda *_: (0,) * len(shape))


def rows_of(block, width):
    return pl.BlockSpec((block, width), lambda i, *_: (i, 0))


def norm_parts(values):
    mean = jnp.mean(values, axis=-1, keepdims=True)
    center = values - mean
    variance = jnp.mean(center * center, axis=-1, keepdims=True)
    root = lax.rsqrt(variance + EPS)
    return center * root, root


def norm_grad(grad, normal, root, gain):
    scaled = grad * gain
    mean_plain = jnp.mean(scaled, axis=-1, keepdims=True)
    mean_normal = jnp.mean(scaled * normal, axis=-1, keepdims=True)
    return root * (scaled - mean_plain - normal * mean_normal)


def pick_rows(first_row, pos_row, rows, count):
    ids = lax.broadcasted_iota(jnp.int32, (rows, count), 0) + first_row
    return jnp.where(ids == pos_row, 1.0, 0.0).astype(BF16)


def pick_slots(pos_col, count):
    ids = lax.broadcasted_iota(jnp.int32, (pos_col.shape[0], count), 1)
    return jnp.where(ids == pos_col, 1.0, 0.0).astype(BF16)


def entry_kernel(parts, *refs):
    slots = refs[:parts]
    pos_row, gain, offset, wq, bq, wk, wv, bv, tokens, normed, q, k, v = refs[parts:]
    i = pl.program_id(0)
    arrived = jnp.concatenate([r[...] for r in slots], axis=0)
    count = arrived.shape[0]
    rows = tokens.shape[0]
    picked = nn(pick_rows(i * rows, pos_row[...], rows, count), arrived)
    tokens[...] = picked.astype(BF16)
    normal, _ = norm_parts(picked)
    low = (normal * gain[...] + offset[...]).astype(BF16)
    normed[...] = low
    q[...] = ((nn(low, wq[...]) + bq[...]).astype(BF16).astype(F32) * 0.125).astype(BF16)
    k[...] = nn(low, wk[...]).astype(BF16)
    v[...] = (nn(low, wv[...]) + bv[...]).astype(BF16)


def entry(slots, pos_row, gain, offset, wq, bq, wk, wv, bv):
    parts = len(slots)
    width = slots[0].shape[1]
    count = sum(v.shape[0] for v in slots)
    out = jax.ShapeDtypeStruct((count, width), BF16)
    return pl.pallas_call(
        functools.partial(entry_kernel, parts),
        grid=(count // ROWS,),
        in_specs=[whole(v.shape) for v in slots]
        + [whole((1, count))]
        + [whole((1, width))] * 2
        + [whole((width, width)), whole((1, width)), whole((width, width)), whole((width, width)), whole((1, width))],
        out_specs=[rows_of(ROWS, width)] * 5,
        out_shape=[out] * 5,
        compiler_params=params(),
        cost_estimate=cost(8 * count * width * width, 18 * count * width),
        name="entry",
    )(*slots, pos_row, gain, offset, wq, bq, wk, wv, bv)


def half_masks(width):
    lane = lax.broadcasted_iota(jnp.int32, (1, width), 1)
    return lane < width // 2


def split_heads(values):
    first = half_masks(values.shape[1])
    zero = jnp.zeros_like(values)
    return jnp.where(first, values, zero), jnp.where(first, zero, values)


def attend_kernel(start_col, q_ref, k_ref, v_ref, mixed_ref, lse_ref, bias):
    count = q_ref.shape[0]

    @pl.when(pl.program_id(0) == 0)
    def _():
        for i in range(count // ROWS):
            ext = (i + 1) * ROWS
            rows = pl.ds(i * ROWS, ROWS)
            kpos = lax.broadcasted_iota(jnp.int32, (ROWS, ext), 1)
            qpos = lax.broadcasted_iota(jnp.int32, (ROWS, ext), 0) + i * ROWS
            keep = (kpos >= start_col[rows, :]) & (kpos <= qpos)
            bias[rows, :ext] = jnp.where(keep, 0.0, NEG)

    values = split_heads(v_ref[...])
    keys = k_ref[...]
    first = half_masks(q_ref.shape[1])
    for i in range(count // ROWS):
        ext = (i + 1) * ROWS
        rows = pl.ds(i * ROWS, ROWS)
        total = None
        stats = []
        for query, value in zip(split_heads(q_ref[rows, :]), values):
            score = nt(query, keys[:ext]) * LOG2E + bias[rows, :ext]
            top = jnp.max(score, axis=1, keepdims=True)
            terms = jnp.exp2(score - top)
            sums = jnp.sum(terms, axis=1, keepdims=True)
            part = nn(terms.astype(BF16), value[:ext])
            total = part if total is None else total + part
            stats.append((top + jnp.log2(sums), 1.0 / sums))
        scale = jnp.where(first, stats[0][1], stats[1][1])
        mixed_ref[rows, :] = (total * scale).astype(BF16)
        both = jnp.where(first, stats[0][0], stats[1][0])
        turned = both.T
        lse_ref[0, 0:1, rows] = turned[0:1, :]
        lse_ref[0, 1:2, rows] = turned[64:65, :]


def attend(start_col, q, k, v):
    count, width = q.shape
    pairs = HEADS // 2
    lanes = width // pairs
    col = pl.BlockSpec((count, lanes), lambda p: (0, p))
    return pl.pallas_call(
        attend_kernel,
        grid=(pairs,),
        in_specs=[whole((count, 1)), col, col, col],
        out_specs=[col, pl.BlockSpec((1, 8, count), lambda p: (p, 0, 0))],
        out_shape=[
            jax.ShapeDtypeStruct((count, width), BF16),
            jax.ShapeDtypeStruct((pairs, 8, count), F32),
        ],
        scratch_shapes=[pltpu.VMEM((count, count), F32)],
        compiler_params=params(),
        cost_estimate=cost(8 * count * count * width, 8 * count * width, HEADS * count * count // 2),
        name="attend",
    )(start_col, q, k, v)


def leave_kernel(parts, mixed, wo, bo, tokens, live_col, pos_col, *refs):
    outs, kept = refs[:parts], refs[parts]
    i = pl.program_id(0)
    rows = mixed.shape[0]
    branch = nn(mixed[...], wo[...]) + bo[...]
    kept[pl.ds(pl.multiple_of(i * rows, rows), rows), :] = (
        tokens[...].astype(F32) + live_col[...] * branch
    ).astype(BF16)

    @pl.when(i == pl.num_programs(0) - 1)
    def _():
        count = kept.shape[0]
        piece = count // parts
        for r in range(parts):
            chosen = pick_slots(pos_col[pl.ds(r * piece, piece), :], count)
            outs[r][...] = nn(chosen, kept[...]).astype(BF16)


def leave(parts, mixed, wo, bo, tokens, live_col, pos_col):
    count, width = mixed.shape
    piece = count // parts
    return pl.pallas_call(
        functools.partial(leave_kernel, parts),
        grid=(count // ROWS,),
        in_specs=[
            rows_of(ROWS, width),
            whole((width, width)),
            whole((1, width)),
            rows_of(ROWS, width),
            rows_of(ROWS, 1),
            whole((count, 1)),
        ],
        out_specs=[whole((piece, width))] * parts,
        out_shape=[jax.ShapeDtypeStruct((piece, width), BF16)] * parts,
        scratch_shapes=[pltpu.VMEM((count, width), BF16)],
        compiler_params=params(),
        cost_estimate=cost(4 * count * width * width, 8 * count * width),
        name="leave",
    )(mixed, wo, bo, tokens, live_col, pos_col)


def reenter_kernel(parts, *refs):
    slots = refs[:parts]
    pos_row, live_col, wo, grad_residual, grad_proj, grad_mixed, bias_sum = refs[parts:]
    i = pl.program_id(0)
    arrived = jnp.concatenate([r[...] for r in slots], axis=0)
    rows = grad_residual.shape[0]
    picked = nn(pick_rows(i * rows, pos_row[...], rows, arrived.shape[0]), arrived)
    grad_residual[...] = picked.astype(BF16)
    masked = live_col[...] * picked
    low = masked.astype(BF16)
    grad_proj[...] = low
    grad_mixed[...] = nt(low, wo[...]).astype(BF16)

    @pl.when(i == 0)
    def _():
        bias_sum[...] = jnp.zeros_like(bias_sum)

    bias_sum[...] += jnp.sum(masked, axis=0, keepdims=True)


def reenter(slots, pos_row, live_col, wo):
    parts = len(slots)
    width = slots[0].shape[1]
    count = sum(v.shape[0] for v in slots)
    out = jax.ShapeDtypeStruct((count, width), BF16)
    return pl.pallas_call(
        functools.partial(reenter_kernel, parts),
        grid=(count // ROWS,),
        in_specs=[whole(v.shape) for v in slots]
        + [whole((1, count)), rows_of(ROWS, 1), whole((width, width))],
        out_specs=[rows_of(ROWS, width)] * 3 + [whole((1, width))],
        out_shape=[out] * 3 + [jax.ShapeDtypeStruct((1, width), F32)],
        compiler_params=params(),
        cost_estimate=cost(4 * count * width * width, 10 * count * width),
        name="reenter",
    )(*slots, pos_row, live_col, wo)


def attend_back_kernel(
    start_row, q_ref, k_ref, v_ref, o_ref, g_ref, lse_ref, dq_ref, dk_ref, dv_ref, bias, dq_sum
):
    count, lanes = q_ref.shape

    @pl.when(pl.program_id(0) == 0)
    def _():
        for j in range(count // ROWS):
            cols = pl.ds(j * ROWS, count - j * ROWS)
            shape = (ROWS, count - j * ROWS)
            kpos = lax.broadcasted_iota(jnp.int32, shape, 0) + j * ROWS
            qpos = lax.broadcasted_iota(jnp.int32, shape, 1) + j * ROWS
            keep = (kpos >= start_row[:, cols]) & (kpos <= qpos)
            bias[pl.ds(j * ROWS, ROWS), cols] = jnp.where(keep, 0.0, NEG)

    products = o_ref[...].astype(F32) * g_ref[...].astype(F32)
    high = products.astype(BF16)
    low = (products - high.astype(F32)).astype(BF16)
    sel_row = lax.broadcasted_iota(jnp.int32, (8, lanes), 0)
    sel_lane = lax.broadcasted_iota(jnp.int32, (8, lanes), 1)
    select = jnp.where(sel_row == sel_lane // (lanes // 2), 1.0, 0.0).astype(BF16)
    deltas = nt(select, high) + nt(select, low)

    queries = split_heads(q_ref[...])
    grads = split_heads(g_ref[...])
    for j in range(count // ROWS):
        rows = pl.ds(j * ROWS, ROWS)
        ext = slice(j * ROWS, count)
        keys, vals = k_ref[rows, :], v_ref[rows, :]
        dk = dv = dq = None
        for h, key in enumerate(split_heads(keys)):
            query, grad = queries[h][ext], grads[h][ext]
            score = nt(keys, query) * LOG2E + bias[rows, ext]
            weights = jnp.exp2(score - lse_ref[0, h : h + 1, ext])
            weights_low = weights.astype(BF16)
            grad_weights = nt(vals, grad)
            grad_score = (weights * (grad_weights - deltas[h : h + 1, ext])).astype(BF16)
            dv_part = nn(weights_low, grad)
            dk_part = nn(grad_score, query)
            dq_part = tn(grad_score, key)
            dv = dv_part if dv is None else dv + dv_part
            dk = dk_part if dk is None else dk + dk_part
            dq = dq_part if dq is None else dq + dq_part
        dk_ref[rows, :] = dk.astype(BF16)
        dv_ref[rows, :] = dv.astype(BF16)
        if j == 0:
            dq_sum[...] = dq
        else:
            dq_sum[ext, :] += dq
    dq_ref[...] = (dq_sum[...] * 0.125).astype(BF16)


def attend_back(start_row, q, k, v, mixed, grad_mixed, lse):
    count, width = q.shape
    pairs = HEADS // 2
    lanes = width // pairs
    col = pl.BlockSpec((count, lanes), lambda p: (0, p))
    out = jax.ShapeDtypeStruct((count, width), BF16)
    return pl.pallas_call(
        attend_back_kernel,
        grid=(pairs,),
        in_specs=[whole((1, count))]
        + [col] * 5
        + [pl.BlockSpec((1, 8, count), lambda p: (p, 0, 0))],
        out_specs=[col] * 3,
        out_shape=[out] * 3,
        scratch_shapes=[pltpu.VMEM((count, count), F32), pltpu.VMEM((count, lanes), F32)],
        compiler_params=params(),
        cost_estimate=cost(20 * count * count * width, 16 * count * width, HEADS * count * count // 2),
        name="attend_back",
    )(start_row, q, k, v, mixed, grad_mixed, lse)


def finish_kernel(
    parts, dq, dk, dv, wq, wk, wv, tokens, grad_residual, gain, pos_col, *refs
):
    outs = refs[:parts]
    sums, kept = refs[parts:]
    i = pl.program_id(0)
    rows = dq.shape[0]
    grad = nt(dq[...], wq[...]) + nt(dk[...], wk[...]) + nt(dv[...], wv[...])
    normal, root = norm_parts(tokens[...].astype(F32))
    kept[pl.ds(pl.multiple_of(i * rows, rows), rows), :] = (
        grad_residual[...].astype(F32) + norm_grad(grad, normal, root, gain[...])
    ).astype(BF16)

    @pl.when(i == 0)
    def _():
        sums[...] = jnp.zeros_like(sums)

    sums[0:1, :] += jnp.sum(grad * normal, axis=0, keepdims=True)
    sums[1:2, :] += jnp.sum(grad, axis=0, keepdims=True)
    sums[2:3, :] += jnp.sum(dq[...].astype(F32), axis=0, keepdims=True)
    sums[3:4, :] += jnp.sum(dv[...].astype(F32), axis=0, keepdims=True)

    @pl.when(i == pl.num_programs(0) - 1)
    def _():
        count = kept.shape[0]
        piece = count // parts
        for r in range(parts):
            chosen = pick_slots(pos_col[pl.ds(r * piece, piece), :], count)
            outs[r][...] = nn(chosen, kept[...]).astype(BF16)


def finish(parts, dq, dk, dv, wq, wk, wv, tokens, grad_residual, gain, pos_col):
    count, width = dq.shape
    piece = count // parts
    return pl.pallas_call(
        functools.partial(finish_kernel, parts),
        grid=(count // ROWS,),
        in_specs=[rows_of(ROWS, width)] * 3
        + [whole((width, width))] * 3
        + [rows_of(ROWS, width)] * 2
        + [whole((1, width)), whole((count, 1))],
        out_specs=[whole((piece, width))] * parts + [whole((8, width))],
        out_shape=[jax.ShapeDtypeStruct((piece, width), BF16)] * parts
        + [jax.ShapeDtypeStruct((8, width), F32)],
        scratch_shapes=[pltpu.VMEM((count, width), BF16)],
        compiler_params=params(),
        cost_estimate=cost(8 * count * width * width, 20 * count * width),
        name="finish",
    )(dq, dk, dv, wq, wk, wv, tokens, grad_residual, gain, pos_col)


GELU_ROOT = math.sqrt(2.0 / math.pi)
GELU_CUBE = 0.044715
STEP = 512


def expert_kernel(first_chunk, parts, *refs):
    it = iter(refs)
    take = lambda n: [next(it) for _ in range(n)]
    (source,) = take(1)
    slots, cots, lives, ups, downs, up_bias, down_bias, gain, offset = take(9)
    if not first_chunk:
        take(5)
    grads = take(parts)
    act_out, pre_out, ffn_out, branch_out, block_out, sums, up_sums = take(7)
    up, down, out_sum, grad_sum, grad_low, up_sem, down_sem = take(7)
    shards = up.shape[0]
    rows, model = slots.shape

    up_copies = [pltpu.make_async_copy(ups.at[k], up.at[k], up_sem.at[k]) for k in range(shards)]
    down_copies = [
        pltpu.make_async_copy(downs.at[k], down.at[k], down_sem.at[k]) for k in range(shards)
    ]
    for k in range(shards):
        up_copies[k].start()
        down_copies[k].start()

    routed = slots[...].astype(F32)
    cot = cots[...].reshape(rows, model).astype(F32)
    live = lives[...].reshape(rows, 1)
    normal, _ = norm_parts(routed)
    ffn_out[...] = (normal * gain[...] + offset[...]).astype(BF16)
    branch_out[...] = (live * cot).astype(BF16)
    width = up.shape[2]
    for k in range(shards):
        up_copies[k].wait()
        down_copies[k].wait()

        for c in range(0, width, STEP):
            cols = pl.ds(c, STEP)
            pre = nn(ffn_out[...], up[k, :, cols]) + up_bias[k, :, cols]
            square = pre * pre
            tanh = jnp.tanh(pre * (GELU_ROOT + (GELU_ROOT * GELU_CUBE) * square))
            half = 0.5 * (1.0 + tanh)
            act = (pre * half).astype(BF16)
            slope = half + (0.5 * pre) * (1.0 - tanh * tanh) * (
                GELU_ROOT + (3.0 * GELU_ROOT * GELU_CUBE) * square
            )
            act_out[k, :, cols] = act
            grad_pre = (nt(branch_out[...], down[k, cols, :]) * slope).astype(BF16)
            pre_out[k, :, cols] = grad_pre
            up_sums[k, :, cols] = jnp.sum(grad_pre.astype(F32), axis=0, keepdims=True)
            grad_part = nt(grad_pre, up[k, :, cols])
            out_part = nn(act, down[k, cols, :])
            if k == 0 and c == 0:
                grad_sum[...] = grad_part
                out_sum[...] = out_part
            else:
                grad_sum[...] += grad_part
                out_sum[...] += out_part
    routed = slots[...].astype(F32)
    normal, root = norm_parts(routed)
    grad = grad_sum[...]
    cot = cots[...].reshape(rows, model).astype(F32)
    grad_routed = (cot + norm_grad(grad, normal, root, gain[...])).astype(BF16)
    if parts == 1:
        grads[0][...] = grad_routed
    else:
        grad_low[...] = grad_routed
        short = rows // parts
        for r in range(parts):
            grads[r][...] = grad_low[pl.ds(pl.multiple_of(source[r] * short, short), short), :]
    out = routed + lives[...].reshape(rows, 1) * (out_sum[...] + down_bias[...])
    block_out[...] = out.astype(BF16).reshape(block_out.shape)
    sums[...] = jnp.zeros_like(sums)
    sums[0:1, :] = jnp.sum(grad * normal, axis=0, keepdims=True)
    sums[1:2, :] = jnp.sum(grad, axis=0, keepdims=True)
    sums[2:3, :] = jnp.sum(branch_out[...].astype(F32), axis=0, keepdims=True)


def expert_chunk(
    chunk, parts, source, slots, cot, live, ups, downs, up_bias, down_bias, gain, offset, carried
):
    rows, width = slots.shape
    groups, piece, _ = cot.shape
    short = rows // groups
    count = groups * piece
    shards, _, part = ups.shape
    anywhere = pl.BlockSpec(memory_space=pl.ANY)
    big = pl.BlockSpec((shards, rows, part), lambda i, *_: (0, chunk, 0))
    flat = pl.BlockSpec((rows, width), lambda i, *_: (chunk, 0))
    block = pl.BlockSpec((groups, short, width), lambda i, *_: (0, chunk, 0))
    first = carried is None
    previous = [] if first else list(carried)
    full = jax.ShapeDtypeStruct((count, width), BF16)
    wide = jax.ShapeDtypeStruct((shards, count, part), BF16)
    outs = pl.pallas_call(
        functools.partial(expert_kernel, first, parts),
        grid_spec=pltpu.PrefetchScalarGridSpec(
            num_scalar_prefetch=1,
            grid=(1,),
            in_specs=[
                whole((rows, width)),
                block,
                pl.BlockSpec((groups, short, 1), lambda i, *_: (0, chunk, 0)),
                anywhere,
                anywhere,
                whole((shards, 1, part)),
                whole((1, width)),
                whole((1, width)),
                whole((1, width)),
            ]
            + [anywhere] * len(previous),
            out_specs=[whole((rows // parts, width))] * parts
            + [big, big, flat, flat, block, whole((8, width)), whole((shards, 1, part))],
            scratch_shapes=[
                pltpu.VMEM((shards, width, part), BF16),
                pltpu.VMEM((shards, part, width), BF16),
                pltpu.VMEM((rows, width), F32),
                pltpu.VMEM((rows, width), F32),
                pltpu.VMEM((rows, width), BF16),
                pltpu.SemaphoreType.DMA((shards,)),
                pltpu.SemaphoreType.DMA((shards,)),
            ],
        ),
        out_shape=[jax.ShapeDtypeStruct((rows // parts, width), BF16)] * parts
        + [
            wide,
            wide,
            full,
            full,
            jax.ShapeDtypeStruct((groups, piece, width), BF16),
            jax.ShapeDtypeStruct((8, width), F32),
            jax.ShapeDtypeStruct((shards, 1, part), F32),
        ],
        input_output_aliases={10 + n: parts + n for n in range(len(previous))},
        compiler_params=params(),
        cost_estimate=cost(
            8 * rows * width * part * shards, 4 * shards * width * part, rows * part * shards
        ),
        name="expert_chunk",
    )(source, slots, cot, live, ups, downs, up_bias, down_bias, gain, offset, *previous)
    return outs[:parts], outs[parts : parts + 5], outs[parts + 5], outs[parts + 6]


def shard_grads_kernel(left, right, out):
    first = left[0] if len(left.shape) == 3 else left[...]
    second = right[0] if len(right.shape) == 3 else right[...]
    out[0] = tn(first, second).astype(BF16)


def shard_grads(left, right):
    def spec(v):
        if v.ndim == 2:
            return whole(v.shape)
        return pl.BlockSpec((1,) + v.shape[1:], lambda i: (i, 0, 0))

    shards = left.shape[0] if left.ndim == 3 else right.shape[0]
    count = left.shape[-2]
    tall, wide = left.shape[-1], right.shape[-1]
    return pl.pallas_call(
        shard_grads_kernel,
        grid=(shards,),
        in_specs=[spec(left), spec(right)],
        out_specs=pl.BlockSpec((1, tall, wide), lambda i: (i, 0, 0)),
        out_shape=jax.ShapeDtypeStruct((shards, tall, wide), BF16),
        compiler_params=params(),
        cost_estimate=cost(2 * shards * count * tall * wide, 6 * shards * tall * wide),
        name="shard_grads",
    )(left, right)


def block_place(codes, streams, blocks, j, size):
    stream = (j // (blocks // (2 * streams))) % streams
    return pl.multiple_of((codes[stream] ^ j) * size, size)


def shared_grads_kernel(streams, blocks, codes, left, right, keep, send, total):
    total[...] = tn(left[...], right[...])
    size = total.shape[0] // blocks
    half = blocks // 2
    for j in range(blocks):
        place = block_place(codes, streams, blocks, j, size)
        target = keep if j < half else send
        target[0, pl.ds((j % half) * size, size), :] = total[pl.ds(place, size), :].astype(BF16)


def shared_grads_many_kernel(streams, blocks, owners, lefts, codes, *refs):
    number = len(owners)
    left_refs, rights, (keep, send, total) = refs[:lefts], refs[lefts : lefts + number], refs[lefts + number :]
    for m in range(number):

        @pl.when(pl.program_id(0) == m)
        def _():
            shared_grads_kernel(streams, blocks, codes, left_refs[owners[m]], rights[m], keep, send, total)


def shared_grads(layout, lefts, owners, rights):
    count, width = lefts[0].shape
    number = len(rights)
    half = pl.BlockSpec((1, width // 2, width), lambda i, *_: (i, 0, 0))
    return pl.pallas_call(
        functools.partial(
            shared_grads_many_kernel, layout.streams, layout.blocks, owners, len(lefts)
        ),
        grid_spec=pltpu.PrefetchScalarGridSpec(
            num_scalar_prefetch=1,
            grid=(number,),
            in_specs=[whole((count, width))] * (len(lefts) + number),
            out_specs=[half, half],
            scratch_shapes=[pltpu.VMEM((width, width), F32)],
        ),
        out_shape=[jax.ShapeDtypeStruct((number, width // 2, width), BF16)] * 2,
        compiler_params=params(),
        cost_estimate=cost(2 * number * count * width * width, 6 * number * width * width),
        name="shared_grads",
    )(layout.codes, *lefts, *rights)


def unmix_kernel(streams, blocks, number, codes, half_place, *refs):
    pieces, outs = refs[0], refs[-number:]
    half = blocks // 2
    size = outs[0].shape[0] // half
    for m in range(number):
        for j in range(half):
            place = block_place(codes, streams, blocks, j, size)
            place = pl.multiple_of(place % (half * size), size)
            outs[m][pl.ds(place, size), :] = pieces[m, pl.ds(j * size, size), :].astype(F32)


def unmix(layout, half_place, pieces, before=None):
    number, rows, width = pieces.shape
    earlier = [] if before is None else list(before)
    out = pl.BlockSpec((rows, width), lambda i, codes, half_place: (half_place[0], 0))
    return pl.pallas_call(
        functools.partial(unmix_kernel, layout.streams, layout.blocks, number),
        grid_spec=pltpu.PrefetchScalarGridSpec(
            num_scalar_prefetch=2,
            grid=(1,),
            in_specs=[whole((number, rows, width))]
            + [pl.BlockSpec(memory_space=pl.ANY)] * len(earlier),
            out_specs=[out] * number,
        ),
        out_shape=[jax.ShapeDtypeStruct((2 * rows, width), F32)] * number,
        input_output_aliases={3 + m: m for m in range(len(earlier))},
        compiler_params=params(),
        cost_estimate=cost(number * rows * width, 6 * number * rows * width),
        name="unmix",
    )(layout.codes, half_place, pieces, *earlier)


def assemble_kernel(parts, source, *refs):
    pieces, out = refs[:parts], refs[parts]
    size = pieces[0].shape[0]
    for r in range(parts):
        out[pl.ds(pl.multiple_of(source[r] * size, size), size), :] = pieces[r][...]


def assemble(source, pieces):
    parts = len(pieces)
    size, width = pieces[0].shape
    return pl.pallas_call(
        functools.partial(assemble_kernel, parts),
        grid_spec=pltpu.PrefetchScalarGridSpec(
            num_scalar_prefetch=1,
            grid=(1,),
            in_specs=[whole((size, width))] * parts,
            out_specs=whole((parts * size, width)),
        ),
        out_shape=jax.ShapeDtypeStruct((parts * size, width), BF16),
        compiler_params=params(),
        cost_estimate=cost(0, 4 * parts * size * width),
        name="assemble",
    )(source, *pieces)


def swap(values, step):
    axis, size, bit = step
    return lax.ppermute(values, axis, [(i, i ^ bit) for i in range(size)])


def exchange(values):
    return lax.all_to_all(values, "expert", split_axis=0, concat_axis=0, tiled=True)


def turn(values, size, by):
    return lax.ppermute(values, "expert", [(i, (i + by) % size) for i in range(size)])


def bits_of(size):
    return [1 << b for b in range(size.bit_length() - 1)]


def add_low(left, right):
    return (left.astype(F32) + right.astype(F32)).astype(BF16)


def tie(*values):
    return lax.optimization_barrier(values)


class SharedSum:
    streams = 2
    least = 16

    def __init__(self, n_expert, n_dp, rows):
        steps = [("dp", n_dp, b) for b in bits_of(n_dp)] + [
            ("expert", n_expert, b) for b in bits_of(n_expert)
        ]
        steps.sort(key=lambda s: (s[2], s[0]))
        self.steps = steps
        self.first, one, two, *rest = steps
        self.pair = ((two, one), (one, two))
        cut = rows // (2 * self.streams * 4)
        self.rest = []
        while rest and cut // 2 >= self.least:
            self.rest.append(rest.pop(0))
            cut //= 2
        self.left = rest
        self.blocks = rows // cut
        self.codes = jnp.stack([self.code([self.first, None, *pair, *self.rest]) for pair in self.pair])

    def code(self, steps):
        total = jnp.int32(0)
        for step in steps:
            mine = 0 if step is None else (lax.axis_index(step[0]) // step[2]) % 2
            total = total * 2 + mine
        return total.astype(jnp.int32)

    @staticmethod
    def halve(values, step, axis):
        middle = values.shape[axis] // 2
        keep = lax.slice_in_dim(values, 0, middle, axis=axis)
        send = lax.slice_in_dim(values, middle, 2 * middle, axis=axis)
        return add_low(keep, swap(send, step))

    @staticmethod
    def double(values, step, axis):
        return jnp.concatenate([values, swap(values, step)], axis=axis)

    def reduce_first(self, keep, send):
        total = add_low(keep, swap(send, self.first))
        middle = total.shape[1] // 2
        return [total[:, :middle], total[:, middle:]]

    def reduce_pair(self, parts, n):
        return [self.halve(part, pair[n], 1) for part, pair in zip(parts, self.pair)]

    def reduce_rest(self, total, n):
        if n < len(self.rest):
            return self.halve(total, self.rest[n], 2)
        return total

    def reduce_left(self, total):
        for step in self.left:
            total = add_low(total, swap(total, step))
        return total

    def gather(self, total):
        for step in reversed(self.rest):
            total = self.double(total, step, 2)
        parts = []
        for stream, pair in enumerate(self.pair):
            part = total[:, stream]
            for step in reversed(pair):
                part = self.double(part, step, 1)
            parts.append(part)
        total = jnp.concatenate(parts, axis=1)
        other = swap(total, self.first)
        mine = ((lax.axis_index(self.first[0]) // self.first[2]) % 2).astype(jnp.int32).reshape(1)
        done = unmix(self, mine, total)
        return unmix(self, 1 - mine, other, done)


def small_sum(values, steps):
    for step in steps:
        values = values + swap(values, step)
    return values


CHUNKS = 2


def per_device(
    n_expert,
    n_dp,
    block_in,
    seq_lengths,
    slot_position,
    first_gain,
    first_bias,
    query_weight,
    query_bias,
    key_weight,
    value_weight,
    value_bias,
    out_weight,
    out_bias,
    second_gain,
    second_bias,
    expert_up,
    expert_up_bias,
    expert_down,
    expert_down_bias,
    block_cot,
):
    count, width = block_in.shape
    piece = count // n_expert
    row = lambda v: v.reshape(1, -1)
    device = lax.axis_index("dp")
    part = expert_up.shape[2]
    dp_steps = [("dp", n_dp, b) for b in bits_of(n_dp)]
    all_steps = dp_steps + [("expert", n_expert, b) for b in bits_of(n_expert)]

    arrived = exchange(block_in)
    ups = lax.all_gather(expert_up[0], "dp", axis=0)
    downs = lax.all_gather(expert_down[0], "dp", axis=0)

    position = slot_position[0]
    ends = jnp.cumsum(seq_lengths[0])
    total_live = ends[-1]
    ids = jnp.arange(count, dtype=jnp.int32)
    live = ids < total_live
    begin = jnp.max(jnp.where(ends[None, :] <= ids[:, None], ends[None, :], 0), axis=1)
    begin = jnp.where(live, begin, ids).astype(jnp.int32)
    live_col = live.astype(F32).reshape(count, 1)
    in_chunks = position.reshape(n_expert, CHUNKS, -1).transpose(1, 0, 2).reshape(count)
    slot_live = (position < total_live).astype(F32).reshape(n_expert, piece)
    route_live = exchange(slot_live).reshape(n_expert, piece, 1)

    tokens, normed, query, key, value = entry(
        [arrived], position.reshape(1, count), row(first_gain), row(first_bias), query_weight,
        row(query_bias), key_weight, value_weight, row(value_bias),
    )
    mixed, lse = attend(begin.reshape(count, 1), query, key, value)
    sent = leave(
        CHUNKS, mixed, out_weight, row(out_bias), tokens, live_col, in_chunks.reshape(count, 1)
    )

    blocks = lambda v: v.reshape(n_expert, piece, width)
    group = lax.axis_index("expert")
    ranks = jnp.arange(n_expert, dtype=jnp.int32)
    carried = None
    returned = []
    sums, up_sums = 0.0, 0.0
    for c in range(CHUNKS):
        (grads,), carried, chunk_sums, chunk_up = expert_chunk(
            c, 1, ((group + ranks) % n_expert).astype(jnp.int32),
            exchange(sent[c]), blocks(block_cot), route_live, ups, downs,
            expert_up_bias[0].reshape(n_dp, 1, part), row(expert_down_bias[0]), row(second_gain),
            row(second_bias), carried,
        )
        sums, up_sums = sums + chunk_sums, up_sums + chunk_up
        if returned:
            returned[-1], carried = tie(returned[-1], carried)
        returned.append(exchange(grads))
    act, grad_pre, ffn_in, branch, block_out = carried

    down_terms = shard_grads(act, branch)
    up_terms = shard_grads(ffn_in, grad_pre)
    bias_sums = jnp.concatenate([up_sums.reshape(1, -1), sums[2:3]], axis=1)
    bias_sums = small_sum(bias_sums, dp_steps)

    returned, down_terms, up_terms = tie(returned, down_terms, up_terms)
    down_sum = lax.psum_scatter(down_terms, "dp", scatter_dimension=0, tiled=True)
    up_sum = lax.psum_scatter(up_terms, "dp", scatter_dimension=0, tiled=True)
    grad_residual, grad_proj, grad_mixed, out_bias_sum = reenter(
        returned, in_chunks.reshape(1, count), live_col, out_weight
    )
    shared = SharedSum(n_expert, n_dp, width)
    token_grads = attend_back(begin.reshape(1, count), query, key, value, mixed, grad_mixed, lse)
    leaving, token_sums = finish(
        1, *token_grads, query_weight, key_weight, value_weight,
        tokens, grad_residual, row(first_gain), position.reshape(count, 1),
    )
    token_grads, leaving = tie(token_grads, leaving)
    halves = shared_grads(shared, [normed, mixed], (0, 0, 0, 1), [*token_grads, grad_proj])
    small = jnp.concatenate(
        [token_sums[0:4], out_bias_sum, sums[0:2], jnp.zeros((1, width), F32)], axis=0
    )
    small_steps = list(shared.steps)

    def small_step(small):
        return small_sum(small, [small_steps.pop(0)])

    total = shared.reduce_first(*halves)
    small = small_step(small)
    leaving, total, small = tie(leaving, total, small)
    input_grad = exchange(leaving)
    total = shared.reduce_pair(total, 0)
    total = jnp.stack(shared.reduce_pair(total, 1), axis=1)
    small = small_step(small)
    total, small, down_sum, input_grad, bias_sums = tie(total, small, down_sum, input_grad, bias_sums)
    for n in range(len(shared.rest)):
        total, small = tie(shared.reduce_rest(total, n), small_step(small))
    total = shared.reduce_left(total)
    small = small_sum(small, small_steps)
    total, up_sum, small = tie(total, up_sum, small)
    share = width // n_dp
    grad_up_bias = lax.dynamic_slice_in_dim(bias_sums, device * part, part, 1)
    grad_down_bias = lax.dynamic_slice_in_dim(bias_sums, n_dp * part + device * share, share, 1)
    grad_down, grad_up = down_sum.astype(F32), up_sum.astype(F32)
    grad_query_weight, grad_key_weight, grad_value_weight, grad_out_weight = shared.gather(total)
    return (
        block_out.reshape(count, width),
        input_grad,
        small[0],
        small[1],
        grad_query_weight,
        small[2],
        grad_key_weight,
        grad_value_weight,
        small[3],
        grad_out_weight,
        small[4],
        small[5],
        small[6],
        grad_up,
        grad_up_bias,
        grad_down,
        grad_down_bias,
    )


def solution(mesh):
    both = P(("expert", "dp"), None)
    return jax.shard_map(
        functools.partial(per_device, mesh.shape["expert"], mesh.shape["dp"]),
        mesh=mesh,
        in_specs=(both,) * 3
        + (P(),) * 11
        + (P("expert", None, "dp"), P("expert", None), P("expert", "dp", None), P("expert", None), both),
        out_specs=(both,) * 2
        + (P(),) * 11
        + (P("expert", None, "dp"), P("expert", "dp"), P("expert", "dp", None), P("expert", "dp")),
        check_vma=False,
    )
```

```python
import functools
import math

import jax
import jax.numpy as jnp
from jax import lax
from jax.experimental import pallas as pl
from jax.experimental.pallas import tpu as pltpu
from jax.sharding import PartitionSpec as P

HEADS = 16
EPS = 1e-05
NEG = -1e30
LOG2E = math.log2(math.e)
F32 = jnp.float32
BF16 = jnp.bfloat16
VMEM_LIMIT = 60 * 1024 * 1024
ROWS = 256


def nn(a, b):
    return lax.dot_general(a, b, (((1,), (0,)), ((), ())), preferred_element_type=F32)


def nt(a, b):
    return lax.dot_general(a, b, (((1,), (1,)), ((), ())), preferred_element_type=F32)


def tn(a, b):
    return lax.dot_general(a, b, (((0,), (0,)), ((), ())), preferred_element_type=F32)


def params(**more):
    return pltpu.CompilerParams(vmem_limit_bytes=VMEM_LIMIT, **more)


def cost(flops, bytes_accessed, transcendentals=0):
    return pl.CostEstimate(
        flops=int(flops), bytes_accessed=int(bytes_accessed), transcendentals=int(transcendentals)
    )


def whole(shape):
    return pl.BlockSpec(shape, lambda *_: (0,) * len(shape))


def rows_of(block, width):
    return pl.BlockSpec((block, width), lambda i, *_: (i, 0))


def norm_parts(values):
    mean = jnp.mean(values, axis=-1, keepdims=True)
    center = values - mean
    variance = jnp.mean(center * center, axis=-1, keepdims=True)
    root = lax.rsqrt(variance + EPS)
    return center * root, root


def norm_grad(grad, normal, root, gain):
    scaled = grad * gain
    mean_plain = jnp.mean(scaled, axis=-1, keepdims=True)
    mean_normal = jnp.mean(scaled * normal, axis=-1, keepdims=True)
    return root * (scaled - mean_plain - normal * mean_normal)


def pick_rows(first_row, pos_row, rows, count):
    ids = lax.broadcasted_iota(jnp.int32, (rows, count), 0) + first_row
    return jnp.where(ids == pos_row, 1.0, 0.0).astype(BF16)


def pick_slots(pos_col, count):
    ids = lax.broadcasted_iota(jnp.int32, (pos_col.shape[0], count), 1)
    return jnp.where(ids == pos_col, 1.0, 0.0).astype(BF16)


ANYWHERE = pl.BlockSpec(memory_space=pl.ANY)


class Copies:
    def __init__(self, sems):
        self.sems, self.used = sems, 0

    def start(self, source, target):
        copy = pltpu.make_async_copy(source, target, self.sems.at[self.used])
        self.used += 1
        copy.start()
        return copy


def entry_kernel(
    slots, pos_row, gain, offset, wq, bq, wk, wv, bv, tokens, normed, q, k, v,
    slots_in, weights, low_tokens, low_normed, low_out, sems
):
    copies = Copies(sems)
    count = slots.shape[0]
    half = count // 2
    came = copies.start(slots, slots_in)
    weights_came = [copies.start(w, weights.at[n]) for n, w in enumerate((wq, wk, wv))]
    came.wait()
    left = []
    for r in range(0, count, ROWS):
        rows = pl.ds(r, ROWS)
        picked = nn(pick_rows(r, pos_row[...], ROWS, count), slots_in[...])
        low_tokens[rows, :] = picked.astype(BF16)
        normal, _ = norm_parts(picked)
        low_normed[rows, :] = (normal * gain[...] + offset[...]).astype(BF16)
    left += [copies.start(low_tokens, tokens), copies.start(low_normed, normed)]
    for n, out in enumerate((q, k, v)):
        weights_came[n].wait()
        for r in range(0, count, half):
            rows = pl.ds(r, half)
            value = nn(low_normed[rows, :], weights[n])
            if n == 0:
                value = (value + bq[...]).astype(BF16).astype(F32) * 0.125
            elif n == 2:
                value = value + bv[...]
            low_out[n, rows, :] = value.astype(BF16)
            left.append(copies.start(low_out.at[n, rows], out.at[rows]))
    for copy in left:
        copy.wait()


def entry(slots, pos_row, gain, offset, wq, bq, wk, wv, bv):
    count, width = slots.shape
    out = jax.ShapeDtypeStruct((count, width), BF16)
    return pl.pallas_call(
        entry_kernel,
        grid=(1,),
        in_specs=[
            ANYWHERE,
            whole((1, count)),
            whole((1, width)),
            whole((1, width)),
            ANYWHERE,
            whole((1, width)),
            ANYWHERE,
            ANYWHERE,
            whole((1, width)),
        ],
        out_specs=[ANYWHERE] * 5,
        out_shape=[out] * 5,
        scratch_shapes=[
            pltpu.VMEM((count, width), BF16),
            pltpu.VMEM((3, width, width), BF16),
            pltpu.VMEM((count, width), BF16),
            pltpu.VMEM((count, width), BF16),
            pltpu.VMEM((3, count, width), BF16),
            pltpu.SemaphoreType.DMA((12,)),
        ],
        compiler_params=params(),
        cost_estimate=cost(8 * count * width * width, 18 * count * width),
        name="entry",
    )(slots, pos_row, gain, offset, wq, bq, wk, wv, bv)


def half_masks(width):
    lane = lax.broadcasted_iota(jnp.int32, (1, width), 1)
    return lane < width // 2


def split_heads(values):
    first = half_masks(values.shape[1])
    zero = jnp.zeros_like(values)
    return jnp.where(first, values, zero), jnp.where(first, zero, values)


def fill_bias(bias, start_col):
    count = bias.shape[0]
    for i in range(count // ROWS):
        ext = (i + 1) * ROWS
        rows = pl.ds(i * ROWS, ROWS)
        kpos = lax.broadcasted_iota(jnp.int32, (ROWS, ext), 1)
        qpos = lax.broadcasted_iota(jnp.int32, (ROWS, ext), 0) + i * ROWS
        keep = (kpos >= start_col[rows, :]) & (kpos <= qpos)
        bias[rows, :ext] = jnp.where(keep, 0.0, NEG)


def largest_square(values):
    lanes = values.shape[1]
    row = lax.broadcasted_iota(jnp.int32, (8, lanes), 0)
    lane = lax.broadcasted_iota(jnp.int32, (8, lanes), 1)
    select = jnp.where(row == lane // (lanes // 2), 1.0, 0.0).astype(BF16)
    wide = values.astype(F32)
    return jnp.max(nt(select, (wide * wide).astype(BF16)), axis=1, keepdims=True)


SAFE = 50.0


def attend_kernel(start_col, q_ref, k_ref, v_ref, mixed_ref, lse_ref, bias, total, sums):
    count, lanes = q_ref.shape

    @pl.when(pl.program_id(0) == 0)
    def _():
        fill_bias(bias, start_col)

    first = half_masks(lanes)
    bound = jnp.max(largest_square(q_ref[...]) * largest_square(k_ref[...]))
    safe = bound * (LOG2E * LOG2E) < SAFE * SAFE

    @pl.when(safe)
    def _():
        queries = split_heads(q_ref[...])
        work = [(j, h) for j in range(count // ROWS) for h in range(2)]

        def scores(j, h):
            return nt(queries[h][j * ROWS :], k_ref[j * ROWS : (j + 1) * ROWS, :])

        ahead = scores(*work[0])
        for n, (j, h) in enumerate(work):
            score = ahead
            if n + 1 < len(work):
                ahead = scores(*work[n + 1])
            ext = pl.ds(j * ROWS, count - j * ROWS)
            cols = pl.ds(j * ROWS, ROWS)
            terms = jnp.exp2(score * LOG2E + bias[ext, cols])
            part_sum = terms[:, :lanes]
            for c in range(lanes, ROWS, lanes):
                part_sum = part_sum + terms[:, c : c + lanes]
            value = split_heads(v_ref[cols, :])[h]
            part = nn(terms.astype(BF16), value)
            if j == 0:
                sums[h] = part_sum
                total[h] = part
            else:
                sums[h, ext, :] += part_sum
                total[h, ext, :] += part
        norms = [jnp.sum(sums[h], axis=1, keepdims=True) for h in range(2)]
        norm = jnp.where(first, norms[0], norms[1])
        mixed_ref[...] = ((total[0] + total[1]) / norm).astype(BF16)
        turned = jnp.log2(norm).T
        lse_ref[0, 0:1, :] = turned[0:1, :]
        lse_ref[0, 1:2, :] = turned[lanes // 2 : lanes // 2 + 1, :]

    @pl.when(jnp.logical_not(safe))
    def _():
        for i in range(count // ROWS):
            ext = (i + 1) * ROWS
            rows = pl.ds(i * ROWS, ROWS)
            out, stats = None, []
            for query, value in zip(split_heads(q_ref[rows, :]), split_heads(v_ref[:ext, :])):
                score = nt(query, k_ref[:ext, :]) * LOG2E + bias[rows, :ext]
                top = jnp.max(score, axis=1, keepdims=True)
                terms = jnp.exp2(score - top)
                norm = jnp.sum(terms, axis=1, keepdims=True)
                part = nn(terms.astype(BF16), value)
                out = part if out is None else out + part
                stats.append((top + jnp.log2(norm), norm))
            norm = jnp.where(first, stats[0][1], stats[1][1])
            mixed_ref[rows, :] = (out / norm).astype(BF16)
            turned = jnp.where(first, stats[0][0], stats[1][0]).T
            lse_ref[0, 0:1, rows] = turned[0:1, :]
            lse_ref[0, 1:2, rows] = turned[lanes // 2 : lanes // 2 + 1, :]


def attend(start_col, q, k, v):
    count, width = q.shape
    pairs = HEADS // 2
    lanes = width // pairs
    col = pl.BlockSpec((count, lanes), lambda p: (0, p))
    return pl.pallas_call(
        attend_kernel,
        grid=(pairs,),
        in_specs=[whole((count, 1)), col, col, col],
        out_specs=[col, pl.BlockSpec((1, 8, count), lambda p: (p, 0, 0))],
        out_shape=[
            jax.ShapeDtypeStruct((count, width), BF16),
            jax.ShapeDtypeStruct((pairs, 8, count), F32),
        ],
        scratch_shapes=[
            pltpu.VMEM((count, count), F32),
            pltpu.VMEM((2, count, lanes), F32),
            pltpu.VMEM((2, count, lanes), F32),
        ],
        compiler_params=params(),
        cost_estimate=cost(8 * count * count * width, 8 * count * width, HEADS * count * count // 2),
        name="attend",
    )(start_col, q, k, v)


def leave_kernel(mixed, wo, bo, tokens, live_col, pos_col, *refs):
    mixed_in, wo_in, tokens_in, kept, low, sems = refs[-6:]
    outs = refs[:-6]
    copies = Copies(sems)
    came = [copies.start(mixed, mixed_in), copies.start(wo, wo_in), copies.start(tokens, tokens_in)]
    for copy in came:
        copy.wait()
    count = kept.shape[0]
    half = count // 2
    for r in range(0, count, half):
        rows = pl.ds(r, half)
        branch = nn(mixed_in[rows, :], wo_in[...]) + bo[...]
        kept[rows, :] = (tokens_in[rows, :].astype(F32) + live_col[rows, :] * branch).astype(BF16)
    piece = count // len(outs)
    left = []
    for n, out in enumerate(outs):
        rows = pl.ds(n * piece, piece)
        low[rows, :] = nn(pick_slots(pos_col[rows, :], count), kept[...]).astype(BF16)
        left.append(copies.start(low.at[rows], out))
    for copy in left:
        copy.wait()


def leave(parts, mixed, wo, bo, tokens, live_col, pos_col):
    count, width = mixed.shape
    return pl.pallas_call(
        leave_kernel,
        grid=(1,),
        in_specs=[
            ANYWHERE,
            ANYWHERE,
            whole((1, width)),
            ANYWHERE,
            whole((count, 1)),
            whole((count, 1)),
        ],
        out_specs=[ANYWHERE] * parts,
        out_shape=[jax.ShapeDtypeStruct((count // parts, width), BF16)] * parts,
        scratch_shapes=[
            pltpu.VMEM((count, width), BF16),
            pltpu.VMEM((width, width), BF16),
            pltpu.VMEM((count, width), BF16),
            pltpu.VMEM((count, width), BF16),
            pltpu.VMEM((count, width), BF16),
            pltpu.SemaphoreType.DMA((3 + parts,)),
        ],
        compiler_params=params(),
        cost_estimate=cost(4 * count * width * width, 8 * count * width),
        name="leave",
    )(mixed, wo, bo, tokens, live_col, pos_col)


def reenter_kernel(parts, *refs):
    slots = refs[:parts]
    pos_row, live_col, wo, grad_residual, grad_proj, grad_mixed, bias_sum = refs[parts : parts + 7]
    slots_in, wo_in, low, sems = refs[parts + 7 :]
    copies = Copies(sems)
    came, start = [], 0
    for part in slots:
        size = part.shape[0]
        came.append(copies.start(part, slots_in.at[pl.ds(start, size)]))
        start += size
    wo_came = copies.start(wo, wo_in)
    for copy in came:
        copy.wait()
    count = slots_in.shape[0]
    half = count // 2
    total, left = None, []
    for r in range(0, count, half):
        rows = pl.ds(r, half)
        picked = nn(pick_rows(r, pos_row[...], half, count), slots_in[...])
        masked = live_col[rows, :] * picked
        low[0, rows, :] = picked.astype(BF16)
        low[1, rows, :] = masked.astype(BF16)
        part = jnp.sum(masked, axis=0, keepdims=True)
        total = part if total is None else total + part
        left.append(copies.start(low.at[0, rows], grad_residual.at[rows]))
        left.append(copies.start(low.at[1, rows], grad_proj.at[rows]))
    bias_sum[...] = total
    wo_came.wait()
    for r in range(0, count, half):
        rows = pl.ds(r, half)
        low[2, rows, :] = nt(low[1, rows, :], wo_in[...]).astype(BF16)
        left.append(copies.start(low.at[2, rows], grad_mixed.at[rows]))
    for copy in left:
        copy.wait()


def reenter(slots, pos_row, live_col, wo):
    parts = len(slots)
    width = slots[0].shape[1]
    count = sum(v.shape[0] for v in slots)
    out = jax.ShapeDtypeStruct((count, width), BF16)
    return pl.pallas_call(
        functools.partial(reenter_kernel, parts),
        grid=(1,),
        in_specs=[ANYWHERE] * parts + [whole((1, count)), whole((count, 1)), ANYWHERE],
        out_specs=[ANYWHERE] * 3 + [whole((1, width))],
        out_shape=[out] * 3 + [jax.ShapeDtypeStruct((1, width), F32)],
        scratch_shapes=[
            pltpu.VMEM((count, width), BF16),
            pltpu.VMEM((width, width), BF16),
            pltpu.VMEM((3, count, width), BF16),
            pltpu.SemaphoreType.DMA((parts + 7,)),
        ],
        compiler_params=params(),
        cost_estimate=cost(4 * count * width * width, 10 * count * width),
        name="reenter",
    )(*slots, pos_row, live_col, wo)


def attend_back_kernel(
    start_row, q_ref, k_ref, v_ref, o_ref, g_ref, lse_ref, out_ref, bias, dq_sum
):
    count, lanes = q_ref.shape

    @pl.when(pl.program_id(0) == 0)
    def _():
        for j in range(count // ROWS):
            cols = pl.ds(j * ROWS, count - j * ROWS)
            shape = (ROWS, count - j * ROWS)
            kpos = lax.broadcasted_iota(jnp.int32, shape, 0) + j * ROWS
            qpos = lax.broadcasted_iota(jnp.int32, shape, 1) + j * ROWS
            keep = (kpos >= start_row[:, cols]) & (kpos <= qpos)
            bias[pl.ds(j * ROWS, ROWS), cols] = jnp.where(keep, 0.0, NEG)

    products = o_ref[...].astype(F32) * g_ref[...].astype(F32)
    high = products.astype(BF16)
    low = (products - high.astype(F32)).astype(BF16)
    sel_row = lax.broadcasted_iota(jnp.int32, (8, lanes), 0)
    sel_lane = lax.broadcasted_iota(jnp.int32, (8, lanes), 1)
    select = jnp.where(sel_row == sel_lane // (lanes // 2), 1.0, 0.0).astype(BF16)
    deltas = nt(select, high) + nt(select, low)

    queries = split_heads(q_ref[...])
    grads = split_heads(g_ref[...])
    for j in range(count // ROWS):
        rows = pl.ds(j * ROWS, ROWS)
        ext = slice(j * ROWS, count)
        keys, vals = k_ref[rows, :], v_ref[rows, :]
        dk = dv = dq = None
        for h, key in enumerate(split_heads(keys)):
            query, grad = queries[h][ext], grads[h][ext]
            score = nt(keys, query) * LOG2E + bias[rows, ext]
            weights = jnp.exp2(score - lse_ref[0, h : h + 1, ext])
            weights_low = weights.astype(BF16)
            grad_weights = nt(vals, grad)
            grad_score = (weights * (grad_weights - deltas[h : h + 1, ext])).astype(BF16)
            dv_part = nn(weights_low, grad)
            dk_part = nn(grad_score, query)
            dq_part = tn(grad_score, key)
            dv = dv_part if dv is None else dv + dv_part
            dk = dk_part if dk is None else dk + dk_part
            dq = dq_part if dq is None else dq + dq_part
        out_ref[1, rows, :] = dk.astype(BF16)
        out_ref[2, rows, :] = dv.astype(BF16)
        if j == 0:
            dq_sum[...] = dq
        else:
            dq_sum[ext, :] += dq
    out_ref[0] = (dq_sum[...] * 0.125).astype(BF16)


def attend_back(start_row, q, k, v, mixed, grad_mixed, lse):
    count, width = q.shape
    pairs = HEADS // 2
    lanes = width // pairs
    col = pl.BlockSpec((count, lanes), lambda p: (0, p))
    return pl.pallas_call(
        attend_back_kernel,
        grid=(pairs,),
        in_specs=[whole((1, count))]
        + [col] * 5
        + [pl.BlockSpec((1, 8, count), lambda p: (p, 0, 0))],
        out_specs=pl.BlockSpec((3, count, lanes), lambda p: (0, 0, p)),
        out_shape=jax.ShapeDtypeStruct((3, count, width), BF16),
        scratch_shapes=[pltpu.VMEM((count, count), F32), pltpu.VMEM((count, lanes), F32)],
        compiler_params=params(),
        cost_estimate=cost(20 * count * count * width, 16 * count * width, HEADS * count * count // 2),
        name="attend_back",
    )(start_row, q, k, v, mixed, grad_mixed, lse)


def finish_kernel(
    grads, wq, wk, wv, tokens, grad_residual, gain, pos_col, others, out, sums,
    grads_in, weights, tokens_in, residual_in, total, kept, sems
):
    copies = Copies(sems)
    came = []
    for n, w in enumerate((wq, wk, wv)):
        came.append((copies.start(grads.at[n], grads_in.at[n]), copies.start(w, weights.at[n])))
    rest = [copies.start(tokens, tokens_in), copies.start(grad_residual, residual_in)]
    count = kept.shape[0]
    half = count // 2
    for n in range(3):
        for copy in came[n]:
            copy.wait()
        for r in range(0, count, half):
            rows = pl.ds(r, half)
            part = nt(grads_in[n, rows, :], weights[n])
            if n == 0:
                total[rows, :] = part
            else:
                total[rows, :] += part
    for copy in rest:
        copy.wait()
    sums[...] = others[...]
    for r in range(0, count, ROWS):
        rows = pl.ds(r, ROWS)
        grad = total[rows, :]
        normal, root = norm_parts(tokens_in[rows, :].astype(F32))
        kept[rows, :] = (
            residual_in[rows, :].astype(F32) + norm_grad(grad, normal, root, gain[...])
        ).astype(BF16)
        sums[0:1, :] += jnp.sum(grad * normal, axis=0, keepdims=True)
        sums[1:2, :] += jnp.sum(grad, axis=0, keepdims=True)
        sums[2:3, :] += jnp.sum(grads_in[0, rows, :].astype(F32), axis=0, keepdims=True)
        sums[3:4, :] += jnp.sum(grads_in[2, rows, :].astype(F32), axis=0, keepdims=True)
    left = []
    for r in range(0, count, half):
        rows = pl.ds(r, half)
        chosen = pick_slots(pos_col[rows, :], count)
        residual_in[rows, :] = nn(chosen, kept[...]).astype(BF16)
        left.append(copies.start(residual_in.at[rows], out.at[rows]))
    for copy in left:
        copy.wait()


def finish(grads, weights, tokens, grad_residual, gain, pos_col, others):
    count, width = tokens.shape
    return pl.pallas_call(
        finish_kernel,
        grid=(1,),
        in_specs=[ANYWHERE] * 6 + [whole((1, width)), whole((count, 1)), whole((8, width))],
        out_specs=[ANYWHERE, whole((8, width))],
        out_shape=[
            jax.ShapeDtypeStruct((count, width), BF16),
            jax.ShapeDtypeStruct((8, width), F32),
        ],
        scratch_shapes=[
            pltpu.VMEM((3, count, width), BF16),
            pltpu.VMEM((3, width, width), BF16),
            pltpu.VMEM((count, width), BF16),
            pltpu.VMEM((count, width), BF16),
            pltpu.VMEM((count, width), F32),
            pltpu.VMEM((count, width), BF16),
            pltpu.SemaphoreType.DMA((10,)),
        ],
        compiler_params=params(),
        cost_estimate=cost(8 * count * width * width, 20 * count * width),
        name="finish",
    )(grads, *weights, tokens, grad_residual, gain, pos_col, others)


GELU_ROOT = math.sqrt(2.0 / math.pi)
GELU_CUBE = 0.044715
STEP = 1024


def shard_of(step):
    return (step % 2) * 2 + step // 2


def expert_kernel(device, *refs):
    it = iter(refs)
    take = lambda n: [next(it) for _ in range(n)]
    slots, cots, lives = take(3)
    up, down, up_bias, gain, offset = take(5)
    grads, mine, theirs, sums, up_sums = take(5)
    ffn_in, branch, grad_sum = take(3)
    rows, model = slots.shape
    t = pl.program_id(0)

    @pl.when(t == 0)
    def _():
        normal, _ = norm_parts(slots[...].astype(F32))
        ffn_in[...] = (normal * gain[...] + offset[...]).astype(BF16)
        cot = cots[...].reshape(rows, model).astype(F32)
        branch[...] = (lives[...].reshape(rows, 1) * cot).astype(BF16)
        theirs[0] = ffn_in[...]
        theirs[1] = branch[...]
        grad_sum[...] = jnp.zeros_like(grad_sum)

    @pl.when(t == 2)
    def _():
        mine[0] = ffn_in[...]
        mine[1] = branch[...]

    width = up.shape[2]

    def compute(out):
        for c in range(0, width, STEP):
            cols = pl.ds(c, STEP)
            pre = nn(ffn_in[...], up[0, :, cols]) + up_bias[0, :, cols]
            square = pre * pre
            tanh = jnp.tanh(pre * (GELU_ROOT + (GELU_ROOT * GELU_CUBE) * square))
            half = 0.5 * (1.0 + tanh)
            slope = half + (0.5 * pre) * (1.0 - tanh * tanh) * (
                GELU_ROOT + (3.0 * GELU_ROOT * GELU_CUBE) * square
            )
            out[0, :, cols] = (pre * half).astype(BF16)
            grad_pre = (nt(branch[...], down[0, cols, :]) * slope).astype(BF16)
            out[1, :, cols] = grad_pre
            up_sums[0, :, cols] = jnp.sum(grad_pre.astype(F32), axis=0, keepdims=True)
            grad_sum[...] += nt(grad_pre, up[0, :, cols])

    @pl.when(t < 2)
    def _():
        compute(mine)

    @pl.when(t >= 2)
    def _():
        compute(theirs)

    @pl.when(t == 3)
    def _():
        routed = slots[...].astype(F32)
        normal, root = norm_parts(routed)
        grad = grad_sum[...]
        cot = cots[...].reshape(rows, model).astype(F32)
        grads[...] = (cot + norm_grad(grad, normal, root, gain[...])).astype(BF16)
        sums[...] = jnp.zeros_like(sums)
        sums[0:1, :] = jnp.sum(grad * normal, axis=0, keepdims=True)
        sums[1:2, :] = jnp.sum(grad, axis=0, keepdims=True)
        sums[2:3, :] = jnp.sum(branch[...].astype(F32), axis=0, keepdims=True)


def expert_chunk(chunk, device, slots, cot, live, ups, downs, up_bias, gain, offset):
    rows, width = slots.shape
    groups, piece, _ = cot.shape
    short = rows // groups
    part = ups.shape[2]
    assert part == width and ups.shape[0] == 4
    block = pl.BlockSpec((groups, short, width), lambda t, *_: (0, chunk, 0))
    packet = jax.ShapeDtypeStruct((6, rows, width), BF16)
    weights = pl.BlockSpec((1, width, part), lambda t, device: (shard_of(t) ^ device[0], 0, 0))
    bias = pl.BlockSpec((1, 1, part), lambda t, device: (shard_of(t) ^ device[0], 0, 0))
    return pl.pallas_call(
        expert_kernel,
        grid_spec=pltpu.PrefetchScalarGridSpec(
            num_scalar_prefetch=1,
            grid=(4,),
            in_specs=[
                whole((rows, width)),
                block,
                pl.BlockSpec((groups, short, 1), lambda t, *_: (0, chunk, 0)),
            ]
            + [weights, weights, bias, whole((1, width)), whole((1, width))],
            out_specs=[
                whole((rows, width)),
                pl.BlockSpec((2, rows, width), lambda t, *_: (jnp.minimum(t, 2), 0, 0)),
                pl.BlockSpec((2, rows, width), lambda t, *_: (jnp.where(t < 2, 2, t - 2), 0, 0)),
                whole((8, width)),
                bias,
            ],
            scratch_shapes=[
                pltpu.VMEM((rows, width), BF16),
                pltpu.VMEM((rows, width), BF16),
                pltpu.VMEM((rows, width), F32),
            ],
        ),
        out_shape=[
            jax.ShapeDtypeStruct((rows, width), BF16),
            packet,
            packet,
            jax.ShapeDtypeStruct((8, width), F32),
            jax.ShapeDtypeStruct((4, 1, part), F32),
        ],
        compiler_params=params(),
        cost_estimate=cost(24 * rows * width * part, 16 * width * part, 4 * rows * part),
        name="expert_chunk",
    )(device, slots, cot, live, ups, downs, up_bias, gain, offset)


def expert_out_kernel(chunks, device, *refs):
    mine, theirs, slots = refs[:chunks], refs[chunks : 2 * chunks], refs[2 * chunks : 3 * chunks]
    down, bias, live, out, total = refs[3 * chunks :]
    t = pl.program_id(0)
    rows = slots[0].shape[0]
    for n in range(4):

        @pl.when(t == n)
        def _(n=n):
            for c in range(chunks):
                part = nn((mine if n < 2 else theirs)[c][0], down[0])
                if n == 0:
                    total[c * rows : (c + 1) * rows, :] = part
                else:
                    total[c * rows : (c + 1) * rows, :] += part

    @pl.when(t == 3)
    def _():
        groups, piece, width = out.shape
        short = piece // chunks
        for c in range(chunks):
            branch = total[c * rows : (c + 1) * rows, :] + bias[...]
            keep = live[:, c * short : (c + 1) * short, :].reshape(rows, 1)
            value = (slots[c][...].astype(F32) + keep * branch).astype(BF16)
            out[:, c * short : (c + 1) * short, :] = value.reshape(groups, short, width)


def expert_out(device, mine, theirs, slots, downs, bias, live):
    chunks = len(slots)
    rows, width = slots[0].shape
    part = downs.shape[1]
    groups, piece, _ = live.shape
    act = lambda index: pl.BlockSpec((1, rows, part), index)
    return pl.pallas_call(
        functools.partial(expert_out_kernel, chunks),
        grid_spec=pltpu.PrefetchScalarGridSpec(
            num_scalar_prefetch=1,
            grid=(4,),
            in_specs=[act(lambda t, *_: (2 * jnp.minimum(t, 1), 0, 0))] * chunks
            + [act(lambda t, *_: (2 * jnp.maximum(t - 2, 0), 0, 0))] * chunks
            + [whole((rows, width))] * chunks
            + [pl.BlockSpec((1, part, width), lambda t, device: (shard_of(t) ^ device[0], 0, 0))]
            + [whole((1, width)), whole((groups, piece, 1))],
            out_specs=whole((groups, piece, width)),
            scratch_shapes=[pltpu.VMEM((chunks * rows, width), F32)],
        ),
        out_shape=jax.ShapeDtypeStruct((groups, piece, width), BF16),
        compiler_params=params(),
        cost_estimate=cost(8 * chunks * rows * part * width, 32 * rows * width),
        name="expert_out",
    )(device, *mine, *theirs, *slots, downs, bias, live)


CUTS = ((768, 256), (448, 576))


def expert_grads_kernel(count, *refs):
    packets, near, fars = refs[:count], refs[count : count + 2], refs[count + 2 : count + 6]
    far_act, branch, ffn_in, far_pre, near_act, near_pre, far_low, near_full, sems = refs[count + 6 :]
    copies = Copies(sems)
    rows = packets[0].shape[1]

    def fetch(slot, target):
        return [copies.start(p.at[slot], target.at[pl.ds(n * rows, rows)]) for n, p in enumerate(packets)]

    first = fetch(2, far_act) + fetch(5, branch)
    second = fetch(4, ffn_in) + fetch(3, far_pre)
    third = fetch(0, near_act)
    fourth = fetch(1, near_pre)
    left = []

    def far(m, came, one, two):
        for copy in came:
            copy.wait()
        far_low[m] = tn(one[...], two[...]).astype(BF16)
        start = 0
        for n, cut in enumerate(CUTS[m]):
            left.append(copies.start(far_low.at[m, pl.ds(start, cut)], fars[2 * m + n]))
            start += cut

    def close(m, came, one, two):
        for copy in came:
            copy.wait()
        near_full[m] = tn(one[...], two[...])
        left.append(copies.start(near_full.at[m], near[m].at[0]))

    far(0, first, far_act, branch)
    far(1, second, ffn_in, far_pre)
    close(0, third, near_act, branch)
    close(1, fourth, ffn_in, near_pre)
    for copy in left:
        copy.wait()


def expert_grads(packets):
    _, rows, width = packets[0].shape
    count = len(packets)
    assert sum(CUTS[0]) == sum(CUTS[1]) == width
    cuts = [c for cuts in CUTS for c in cuts]
    return pl.pallas_call(
        functools.partial(expert_grads_kernel, count),
        grid=(1,),
        in_specs=[ANYWHERE] * count,
        out_specs=[ANYWHERE] * 6,
        out_shape=[jax.ShapeDtypeStruct((1, width, width), F32)] * 2
        + [jax.ShapeDtypeStruct((c, width), BF16) for c in cuts],
        scratch_shapes=[pltpu.VMEM((count * rows, width), BF16)] * 6
        + [
            pltpu.VMEM((2, width, width), BF16),
            pltpu.VMEM((2, width, width), F32),
            pltpu.SemaphoreType.DMA((6 * count + 6,)),
        ],
        compiler_params=params(),
        cost_estimate=cost(8 * count * rows * width * width, 30 * width * width),
        name="expert_grads",
    )(*packets)


def shared_grads_kernel(
    streams, blocks, codes, normed, mixed, token_grads, grad_proj, keep, send,
    left_in, right_in, total, low, sems
):
    copies = Copies(sems)
    number = right_in.shape[0]
    came = [[copies.start(normed, left_in.at[0]), copies.start(token_grads.at[0], right_in.at[0])]]
    came += [[copies.start(token_grads.at[m], right_in.at[m])] for m in range(1, number - 1)]
    came.append([copies.start(mixed, left_in.at[1]), copies.start(grad_proj, right_in.at[number - 1])])
    half = blocks // 2
    rows = total.shape[1]
    size = rows // half
    first = codes[0] // half
    left = []
    for m in range(number):
        for copy in came[m]:
            copy.wait()
        for h, target in enumerate((keep, send)):
            n = (2 * m + h) % 2
            side = pl.ds(pl.multiple_of((first ^ h) * rows, rows), rows)
            total[n] = tn(left_in[0 if m < number - 1 else 1, :, side], right_in[m])
            for j in range(half):
                code = codes[(j // (half // streams)) % streams] % half
                place = pl.multiple_of((code ^ j) * size, size)
                low[m, h, pl.ds(j * size, size), :] = total[n, pl.ds(place, size), :].astype(BF16)
            left.append(copies.start(low.at[m, h], target.at[m]))
    for copy in left:
        copy.wait()


def shared_grads(layout, normed, mixed, token_grads, grad_proj):
    count, width = normed.shape
    number = token_grads.shape[0] + 1
    half = width // 2
    return pl.pallas_call(
        functools.partial(shared_grads_kernel, layout.streams, layout.blocks),
        grid_spec=pltpu.PrefetchScalarGridSpec(
            num_scalar_prefetch=1,
            grid=(1,),
            in_specs=[ANYWHERE] * 4,
            out_specs=[ANYWHERE] * 2,
            scratch_shapes=[
                pltpu.VMEM((2, count, width), BF16),
                pltpu.VMEM((number, count, width), BF16),
                pltpu.VMEM((2, half, width), F32),
                pltpu.VMEM((number, 2, half, width), BF16),
                pltpu.SemaphoreType.DMA((3 * number + 2,)),
            ],
        ),
        out_shape=[jax.ShapeDtypeStruct((number, half, width), BF16)] * 2,
        compiler_params=params(),
        cost_estimate=cost(2 * number * count * width * width, 6 * number * width * width),
        name="shared_grads",
    )(layout.codes, normed, mixed, token_grads, grad_proj)


def unmix_kernel(group, number, codes, half_place, *refs):
    pieces, outs = refs[:number], refs[-number:]
    size = outs[0].shape[0] // group
    code = codes[pl.program_id(0) // 2] % group
    for piece, out in zip(pieces, outs):
        for j in range(group):
            place = pl.multiple_of((code ^ j) * size, size)
            out[pl.ds(place, size), :] = piece[0, pl.ds(j * size, size), :].astype(F32)


def unmix(layout, half_place, pieces, before=None):
    number = len(pieces)
    _, rows, width = pieces[0].shape
    earlier = [] if before is None else list(before)
    group = layout.blocks // 8
    part = rows // 4

    def place(i, codes, half_place):
        return (0, i ^ ((codes[i // 2] // group) % 2), 0)

    return pl.pallas_call(
        functools.partial(unmix_kernel, group, number),
        grid_spec=pltpu.PrefetchScalarGridSpec(
            num_scalar_prefetch=2,
            grid=(4,),
            in_specs=[pl.BlockSpec((1, part, width), place)] * number
            + [pl.BlockSpec(memory_space=pl.ANY)] * len(earlier),
            out_specs=[
                pl.BlockSpec((part, width), lambda i, codes, half_place: (half_place[0] * 4 + i, 0))
            ]
            * number,
        ),
        out_shape=[jax.ShapeDtypeStruct((2 * rows, width), F32)] * number,
        input_output_aliases={2 + number + m: m for m in range(len(earlier))},
        compiler_params=params(),
        cost_estimate=cost(number * rows * width, 6 * number * rows * width),
        name="unmix",
    )(layout.codes, half_place, *pieces, *earlier)


def swap(values, step):
    axis, size, bit = step
    return lax.ppermute(values, axis, [(i, i ^ bit) for i in range(size)])


def exchange(values):
    return lax.all_to_all(values, "expert", split_axis=0, concat_axis=0, tiled=True)


def turn(values, size, by):
    return lax.ppermute(values, "expert", [(i, (i + by) % size) for i in range(size)])


def bits_of(size):
    return [1 << b for b in range(size.bit_length() - 1)]


def add_low(left, right):
    return (left.astype(F32) + right.astype(F32)).astype(BF16)


def tie(*values):
    return lax.optimization_barrier(values)


class SharedSum:
    streams = 2
    least = 16

    def __init__(self, n_expert, n_dp, rows):
        steps = [("dp", n_dp, b) for b in bits_of(n_dp)] + [
            ("expert", n_expert, b) for b in bits_of(n_expert)
        ]
        steps.sort(key=lambda s: (s[2], s[0]))
        self.steps = steps
        self.first, one, two, *rest = steps
        self.pair = ((two, one), (one, two))
        self.rest, self.left = rest[:2], rest[2:]
        self.blocks = 2 * self.streams * 4 * 4
        assert rows // self.blocks >= self.least and self.rest[0][0] == self.rest[1][0]
        self.codes = jnp.stack([self.code([self.first, None, *pair, *self.rest]) for pair in self.pair])

    def code(self, steps):
        total = jnp.int32(0)
        for step in steps:
            mine = 0 if step is None else (lax.axis_index(step[0]) // step[2]) % 2
            total = total * 2 + mine
        return total.astype(jnp.int32)

    @staticmethod
    def halve(values, step, axis):
        middle = values.shape[axis] // 2
        keep = lax.slice_in_dim(values, 0, middle, axis=axis)
        send = lax.slice_in_dim(values, middle, 2 * middle, axis=axis)
        return add_low(keep, swap(send, step))

    @staticmethod
    def double(values, step, axis):
        return jnp.concatenate([values, swap(values, step)], axis=axis)

    def reduce_first(self, keep, send):
        total = add_low(keep, swap(send, self.first))
        middle = total.shape[1] // 2
        return [total[:, :middle], total[:, middle:]]

    def reduce_pair(self, parts, n):
        return [self.halve(part, pair[n], 1) for part, pair in zip(parts, self.pair)]

    def partners(self, total, j):
        (axis, size, high), (_, _, low) = self.rest
        return swap(total, (axis, size, (j // 2) * high + (j % 2) * low))

    def reduce_rest(self, total):
        size = total.shape[2] // 4
        piece = lambda j: total[:, :, j * size : (j + 1) * size]
        sum_all = piece(0).astype(F32)
        for j in range(1, 4):
            sum_all = sum_all + self.partners(piece(j), j).astype(F32)
        total = sum_all.astype(BF16)
        for step in self.left:
            total = add_low(total, swap(total, step))
        return total

    def gather_rest(self, total):
        return jnp.concatenate([total] + [self.partners(total, j) for j in range(1, 4)], axis=2)

    def gather_pair(self, parts, n):
        return [self.double(part, pair[n], 1) for part, pair in zip(parts, self.pair)]

    def gather_first(self, parts):
        total = jnp.concatenate(parts, axis=1)
        pieces = [total[m : m + 1] for m in range(total.shape[0])]
        mine = ((lax.axis_index(self.first[0]) // self.first[2]) % 2).astype(jnp.int32).reshape(1)
        return (mine, pieces), (1 - mine, [swap(v, self.first) for v in pieces])


def small_sum(values, steps):
    for step in steps:
        if step[0] == "dp":
            values = values + swap(values, step)
        else:
            part = values[:8]
            values = jnp.concatenate([part + swap(part, step), values[8:]], axis=0)
    return values


CHUNKS = 2


def per_device(
    n_expert,
    n_dp,
    block_in,
    seq_lengths,
    slot_position,
    first_gain,
    first_bias,
    query_weight,
    query_bias,
    key_weight,
    value_weight,
    value_bias,
    out_weight,
    out_bias,
    second_gain,
    second_bias,
    expert_up,
    expert_up_bias,
    expert_down,
    expert_down_bias,
    block_cot,
):
    count, width = block_in.shape
    piece = count // n_expert
    row = lambda v: v.reshape(1, -1)
    device = lax.axis_index("dp")
    part = expert_up.shape[2]
    dp_steps = [("dp", n_dp, b) for b in bits_of(n_dp)]
    all_steps = dp_steps + [("expert", n_expert, b) for b in bits_of(n_expert)]

    core, far = dp_steps
    ups = lax.all_gather(expert_up[0], "dp", axis=0)
    downs = lax.all_gather(expert_down[0], "dp", axis=0)
    arrived = exchange(block_in)

    position = slot_position[0]
    ends = jnp.cumsum(seq_lengths[0])
    total_live = ends[-1]
    ids = jnp.arange(count, dtype=jnp.int32)
    live = ids < total_live
    begin = jnp.max(jnp.where(ends[None, :] <= ids[:, None], ends[None, :], 0), axis=1)
    begin = jnp.where(live, begin, ids).astype(jnp.int32)
    live_col = live.astype(F32).reshape(count, 1)
    in_chunks = position.reshape(n_expert, CHUNKS, -1).transpose(1, 0, 2).reshape(count)
    slot_live = (position < total_live).astype(F32).reshape(n_expert, piece)
    route_live = exchange(slot_live).reshape(n_expert, piece, 1)

    tokens, normed, query, key, value = entry(
        arrived, position.reshape(1, count), row(first_gain), row(first_bias), query_weight,
        row(query_bias), key_weight, value_weight, row(value_bias),
    )
    mixed, lse = attend(begin.reshape(count, 1), query, key, value)
    sent = leave(
        CHUNKS, mixed, out_weight, row(out_bias), tokens, live_col, in_chunks.reshape(count, 1)
    )
    routed = [exchange(sent[0])]

    blocks = lambda v: v.reshape(n_expert, piece, width)
    place = device.astype(jnp.int32).reshape(1)
    up_bias = expert_up_bias[0].reshape(n_dp, 1, part)
    grads, mine, theirs, got, sums, up_sums = ([None] * CHUNKS for _ in range(6))
    returned = []
    for c in range(CHUNKS):
        grads[c], mine[c], theirs[c], sums[c], up_sums[c] = expert_chunk(
            c, place, routed[c], blocks(block_cot), route_live, ups, downs, up_bias,
            row(second_gain), row(second_bias),
        )
        if c > 0:
            returned.append(exchange(grads[c - 1]))
            got[c - 1] = swap(theirs[c - 1], core)
            returned[-1], got[c - 1], grads[c], mine[c], theirs[c] = tie(
                returned[-1], got[c - 1], grads[c], mine[c], theirs[c]
            )
        if c + 1 < CHUNKS:
            routed.append(exchange(sent[c + 1]))
            routed[c + 1], grads[c], mine[c], theirs[c] = tie(
                routed[c + 1], grads[c], mine[c], theirs[c]
            )
    returned.append(exchange(grads[-1]))
    got[-1] = swap(theirs[-1], core)

    *near, down_a, down_b, up_a, up_b = expert_grads([*mine, *got])
    sums, up_sums = sum(sums), sum(up_sums)
    empty = jnp.zeros((8, width), F32)
    biases = jnp.concatenate([up_sums.reshape(-1, width), sums[2:3], empty[: 7 - n_dp]], axis=0)

    fars = [down_a, down_b, up_a, up_b]

    def over_y(n):
        fars[n] = swap(fars[n], far)

    returned, near, fars, biases = tie(returned, near, fars, biases)
    grad_residual, grad_proj, grad_mixed, out_bias_sum = reenter(
        returned, in_chunks.reshape(1, count), live_col, out_weight
    )
    others = jnp.concatenate([empty[:4], out_bias_sum, sums[0:2], empty[:1]], axis=0)
    grad_mixed, fars, others = tie(grad_mixed, fars, others)
    shared = SharedSum(n_expert, n_dp, width)
    unstack = lambda v: [v[:, n] for n in range(shared.streams)]

    over_y(0)
    token_grads = attend_back(
        begin.reshape(1, count), query, key, value, mixed, grad_mixed, lse
    )
    token_grads, fars = tie(token_grads, fars)

    over_y(1)
    halves = shared_grads(shared, normed, mixed, token_grads, grad_proj)
    token_grads, halves, fars = tie(token_grads, halves, fars)

    over_y(2)
    leaving, token_sums = finish(
        token_grads, [query_weight, key_weight, value_weight], tokens, grad_residual,
        row(first_gain), position.reshape(count, 1), others,
    )
    total = shared.reduce_first(*halves)
    small = jnp.concatenate([token_sums, biases], axis=0)
    leaving, total, small, fars = tie(leaving, total, small, fars)

    small_steps = list(shared.steps)
    small_step = lambda v: small_sum(v, [small_steps.pop(0)])
    total = shared.reduce_pair(total, 0)
    small = small_step(small)
    total, small = tie(total, small)

    total = jnp.stack(shared.reduce_pair(total, 1), axis=1)
    small = small_step(small)
    total, small, fars, mine = tie(total, small, fars, mine)

    over_y(3)
    block_out = expert_out(place, mine, theirs, routed, downs, row(expert_down_bias[0]), route_live)
    total = shared.reduce_rest(total)
    small = small_step(small)
    total, small, block_out, near, fars = tie(total, small, block_out, near, fars)

    total = unstack(shared.gather_rest(total))
    grad_down = near[0] + jnp.concatenate(fars[:2], axis=0).astype(F32)[None]
    grad_up = near[1] + jnp.concatenate(fars[2:], axis=0).astype(F32)[None]
    small = small_step(small)
    total, small, grad_down, grad_up, leaving = tie(total, small, grad_down, grad_up, leaving)

    input_grad = exchange(leaving)
    total = shared.gather_pair(total, 1)
    total, small = tie(total, small)

    total = shared.gather_pair(total, 0)
    small = small_sum(small, small_steps)
    total, small = tie(total, small)

    nearest, farthest = shared.gather_first(total)
    grads = unmix(shared, *nearest)
    grads, farthest, input_grad = tie(grads, farthest, input_grad)
    grad_query_weight, grad_key_weight, grad_value_weight, grad_out_weight = unmix(
        shared, *farthest, grads
    )
    share = width // n_dp
    grad_up_bias = lax.dynamic_slice_in_dim(small, 8 + device, 1, 0)
    grad_down_bias = lax.dynamic_slice_in_dim(small[8 + n_dp : 9 + n_dp], device * share, share, 1)
    return (
        block_out.reshape(count, width),
        input_grad,
        small[0],
        small[1],
        grad_query_weight,
        small[2],
        grad_key_weight,
        grad_value_weight,
        small[3],
        grad_out_weight,
        small[4],
        small[5],
        small[6],
        grad_up,
        grad_up_bias,
        grad_down,
        grad_down_bias,
    )


def solution(mesh):
    both = P(("expert", "dp"), None)
    return jax.shard_map(
        functools.partial(per_device, mesh.shape["expert"], mesh.shape["dp"]),
        mesh=mesh,
        in_specs=(both,) * 3
        + (P(),) * 11
        + (P("expert", None, "dp"), P("expert", None), P("expert", "dp", None), P("expert", None), both),
        out_specs=(both,) * 2
        + (P(),) * 11
        + (P("expert", None, "dp"), P("expert", "dp"), P("expert", "dp", None), P("expert", "dp")),
        check_vma=False,
    )
```

```python
import functools
import math

import jax
import jax.numpy as jnp
from jax import lax
from jax.experimental import pallas as pl
from jax.experimental.pallas import tpu as pltpu
from jax.sharding import PartitionSpec as P

HEADS = 16
EPS = 1e-05
NEG = -1e30
LOG2E = math.log2(math.e)
F32 = jnp.float32
BF16 = jnp.bfloat16
VMEM_LIMIT = 60 * 1024 * 1024
ROWS = 256


def nn(a, b):
    return lax.dot_general(a, b, (((1,), (0,)), ((), ())), preferred_element_type=F32)


def nt(a, b):
    return lax.dot_general(a, b, (((1,), (1,)), ((), ())), preferred_element_type=F32)


def tn(a, b):
    return lax.dot_general(a, b, (((0,), (0,)), ((), ())), preferred_element_type=F32)


def params(**more):
    return pltpu.CompilerParams(vmem_limit_bytes=VMEM_LIMIT, **more)


def cost(flops, bytes_accessed, transcendentals=0):
    return pl.CostEstimate(
        flops=int(flops), bytes_accessed=int(bytes_accessed), transcendentals=int(transcendentals)
    )


def whole(shape):
    return pl.BlockSpec(shape, lambda *_: (0,) * len(shape))


def rows_of(block, width):
    return pl.BlockSpec((block, width), lambda i, *_: (i, 0))


def norm_parts(values):
    mean = jnp.mean(values, axis=-1, keepdims=True)
    center = values - mean
    variance = jnp.mean(center * center, axis=-1, keepdims=True)
    root = lax.rsqrt(variance + EPS)
    return center * root, root


def norm_grad(grad, normal, root, gain):
    scaled = grad * gain
    mean_plain = jnp.mean(scaled, axis=-1, keepdims=True)
    mean_normal = jnp.mean(scaled * normal, axis=-1, keepdims=True)
    return root * (scaled - mean_plain - normal * mean_normal)


def pick_rows(first_row, pos_row, rows, count):
    ids = lax.broadcasted_iota(jnp.int32, (rows, count), 0) + first_row
    return jnp.where(ids == pos_row, 1.0, 0.0).astype(BF16)


def pick_slots(pos_col, count):
    ids = lax.broadcasted_iota(jnp.int32, (pos_col.shape[0], count), 1)
    return jnp.where(ids == pos_col, 1.0, 0.0).astype(BF16)


ANYWHERE = pl.BlockSpec(memory_space=pl.ANY)


class Copies:
    def __init__(self, sems):
        self.sems, self.used = sems, 0

    def start(self, source, target):
        copy = pltpu.make_async_copy(source, target, self.sems.at[self.used])
        self.used += 1
        copy.start()
        return copy


def entry_kernel(
    slots, pos_row, gain, offset, wq, bq, wk, wv, bv, tokens, normed, q, k, v,
    slots_in, weights, low_tokens, low_normed, low_out, sems
):
    copies = Copies(sems)
    count = slots.shape[0]
    half = count // 2
    came = copies.start(slots, slots_in)
    weights_came = [copies.start(w, weights.at[n]) for n, w in enumerate((wq, wk, wv))]
    came.wait()
    left = []
    for r in range(0, count, ROWS):
        rows = pl.ds(r, ROWS)
        picked = nn(pick_rows(r, pos_row[...], ROWS, count), slots_in[...])
        low_tokens[rows, :] = picked.astype(BF16)
        normal, _ = norm_parts(picked)
        low_normed[rows, :] = (normal * gain[...] + offset[...]).astype(BF16)
    left += [copies.start(low_tokens, tokens), copies.start(low_normed, normed)]
    for n, out in enumerate((q, k, v)):
        weights_came[n].wait()
        for r in range(0, count, half):
            rows = pl.ds(r, half)
            value = nn(low_normed[rows, :], weights[n])
            if n == 0:
                value = (value + bq[...]).astype(BF16).astype(F32) * 0.125
            elif n == 2:
                value = value + bv[...]
            low_out[n, rows, :] = value.astype(BF16)
            left.append(copies.start(low_out.at[n, rows], out.at[rows]))
    for copy in left:
        copy.wait()


def entry(slots, pos_row, gain, offset, wq, bq, wk, wv, bv):
    count, width = slots.shape
    out = jax.ShapeDtypeStruct((count, width), BF16)
    return pl.pallas_call(
        entry_kernel,
        grid=(1,),
        in_specs=[
            ANYWHERE,
            whole((1, count)),
            whole((1, width)),
            whole((1, width)),
            ANYWHERE,
            whole((1, width)),
            ANYWHERE,
            ANYWHERE,
            whole((1, width)),
        ],
        out_specs=[ANYWHERE] * 5,
        out_shape=[out] * 5,
        scratch_shapes=[
            pltpu.VMEM((count, width), BF16),
            pltpu.VMEM((3, width, width), BF16),
            pltpu.VMEM((count, width), BF16),
            pltpu.VMEM((count, width), BF16),
            pltpu.VMEM((3, count, width), BF16),
            pltpu.SemaphoreType.DMA((12,)),
        ],
        compiler_params=params(),
        cost_estimate=cost(8 * count * width * width, 18 * count * width),
        name="entry",
    )(slots, pos_row, gain, offset, wq, bq, wk, wv, bv)


def half_masks(width):
    lane = lax.broadcasted_iota(jnp.int32, (1, width), 1)
    return lane < width // 2


def split_heads(values):
    first = half_masks(values.shape[1])
    zero = jnp.zeros_like(values)
    return jnp.where(first, values, zero), jnp.where(first, zero, values)


def fill_bias(bias, start_col):
    count = bias.shape[0]
    for i in range(count // ROWS):
        ext = (i + 1) * ROWS
        rows = pl.ds(i * ROWS, ROWS)
        kpos = lax.broadcasted_iota(jnp.int32, (ROWS, ext), 1)
        qpos = lax.broadcasted_iota(jnp.int32, (ROWS, ext), 0) + i * ROWS
        keep = (kpos >= start_col[rows, :]) & (kpos <= qpos)
        bias[rows, :ext] = jnp.where(keep, 0.0, NEG)


def largest_square(values):
    lanes = values.shape[1]
    row = lax.broadcasted_iota(jnp.int32, (8, lanes), 0)
    lane = lax.broadcasted_iota(jnp.int32, (8, lanes), 1)
    select = jnp.where(row == lane // (lanes // 2), 1.0, 0.0).astype(BF16)
    wide = values.astype(F32)
    return jnp.max(nt(select, (wide * wide).astype(BF16)), axis=1, keepdims=True)


SAFE = 50.0


def attend_kernel(start_col, q_ref, k_ref, v_ref, mixed_ref, lse_ref, bias, total, sums):
    count, lanes = q_ref.shape

    @pl.when(pl.program_id(0) == 0)
    def _():
        fill_bias(bias, start_col)

    first = half_masks(lanes)
    bound = jnp.max(largest_square(q_ref[...]) * largest_square(k_ref[...]))
    safe = bound * (LOG2E * LOG2E) < SAFE * SAFE

    @pl.when(safe)
    def _():
        queries = split_heads(q_ref[...])
        work = [(j, h) for j in range(count // ROWS) for h in range(2)]

        def scores(j, h):
            return nt(queries[h][j * ROWS :], k_ref[j * ROWS : (j + 1) * ROWS, :])

        ahead = scores(*work[0])
        for n, (j, h) in enumerate(work):
            score = ahead
            if n + 1 < len(work):
                ahead = scores(*work[n + 1])
            ext = pl.ds(j * ROWS, count - j * ROWS)
            cols = pl.ds(j * ROWS, ROWS)
            terms = jnp.exp2(score * LOG2E + bias[ext, cols])
            part_sum = terms[:, :lanes]
            for c in range(lanes, ROWS, lanes):
                part_sum = part_sum + terms[:, c : c + lanes]
            value = split_heads(v_ref[cols, :])[h]
            part = nn(terms.astype(BF16), value)
            if j == 0:
                sums[h] = part_sum
                total[h] = part
            else:
                sums[h, ext, :] += part_sum
                total[h, ext, :] += part
        norms = [jnp.sum(sums[h], axis=1, keepdims=True) for h in range(2)]
        norm = jnp.where(first, norms[0], norms[1])
        mixed_ref[...] = ((total[0] + total[1]) / norm).astype(BF16)
        turned = jnp.log2(norm).T
        lse_ref[0, 0:1, :] = turned[0:1, :]
        lse_ref[0, 1:2, :] = turned[lanes // 2 : lanes // 2 + 1, :]

    @pl.when(jnp.logical_not(safe))
    def _():
        for i in range(count // ROWS):
            ext = (i + 1) * ROWS
            rows = pl.ds(i * ROWS, ROWS)
            out, stats = None, []
            for query, value in zip(split_heads(q_ref[rows, :]), split_heads(v_ref[:ext, :])):
                score = nt(query, k_ref[:ext, :]) * LOG2E + bias[rows, :ext]
                top = jnp.max(score, axis=1, keepdims=True)
                terms = jnp.exp2(score - top)
                norm = jnp.sum(terms, axis=1, keepdims=True)
                part = nn(terms.astype(BF16), value)
                out = part if out is None else out + part
                stats.append((top + jnp.log2(norm), norm))
            norm = jnp.where(first, stats[0][1], stats[1][1])
            mixed_ref[rows, :] = (out / norm).astype(BF16)
            turned = jnp.where(first, stats[0][0], stats[1][0]).T
            lse_ref[0, 0:1, rows] = turned[0:1, :]
            lse_ref[0, 1:2, rows] = turned[lanes // 2 : lanes // 2 + 1, :]


def attend(start_col, q, k, v):
    count, width = q.shape
    pairs = HEADS // 2
    lanes = width // pairs
    col = pl.BlockSpec((count, lanes), lambda p: (0, p))
    return pl.pallas_call(
        attend_kernel,
        grid=(pairs,),
        in_specs=[whole((count, 1)), col, col, col],
        out_specs=[col, pl.BlockSpec((1, 8, count), lambda p: (p, 0, 0))],
        out_shape=[
            jax.ShapeDtypeStruct((count, width), BF16),
            jax.ShapeDtypeStruct((pairs, 8, count), F32),
        ],
        scratch_shapes=[
            pltpu.VMEM((count, count), F32),
            pltpu.VMEM((2, count, lanes), F32),
            pltpu.VMEM((2, count, lanes), F32),
        ],
        compiler_params=params(),
        cost_estimate=cost(8 * count * count * width, 8 * count * width, HEADS * count * count // 2),
        name="attend",
    )(start_col, q, k, v)


def leave_kernel(
    mixed, wo, bo, tokens, live_col, pos_col, out, residual, mixed_in, wo_in, tokens_in, kept, low, sems
):
    copies = Copies(sems)
    count = kept.shape[0]
    half = count // 2
    first = copies.start(wo, wo_in)
    came = []
    for r in range(0, count, half):
        rows = pl.ds(r, half)
        came.append(copies.start(mixed.at[rows], mixed_in.at[rows]))
        came.append(copies.start(tokens.at[rows], tokens_in.at[rows]))
    first.wait()
    for r in range(0, count, half):
        rows = pl.ds(r, half)
        for copy in came[:2]:
            copy.wait()
        came = came[2:]
        branch = nn(mixed_in[rows, :], wo_in[...]) + bo[...]
        kept[rows, :] = (tokens_in[rows, :].astype(F32) + live_col[rows, :] * branch).astype(BF16)
    left = [copies.start(kept, residual)]
    low[...] = nn(pick_slots(pos_col[...], count), kept[...]).astype(BF16)
    left.append(copies.start(low, out))
    for copy in left:
        copy.wait()


def leave(mixed, wo, bo, tokens, live_col, pos_col):
    count, width = mixed.shape
    rows = pos_col.shape[0]
    return pl.pallas_call(
        leave_kernel,
        grid=(1,),
        in_specs=[
            ANYWHERE,
            ANYWHERE,
            whole((1, width)),
            ANYWHERE,
            whole((count, 1)),
            whole((rows, 1)),
        ],
        out_specs=[ANYWHERE] * 2,
        out_shape=[
            jax.ShapeDtypeStruct((rows, width), BF16),
            jax.ShapeDtypeStruct((count, width), BF16),
        ],
        scratch_shapes=[
            pltpu.VMEM((count, width), BF16),
            pltpu.VMEM((width, width), BF16),
            pltpu.VMEM((count, width), BF16),
            pltpu.VMEM((count, width), BF16),
            pltpu.VMEM((rows, width), BF16),
            pltpu.SemaphoreType.DMA((7,)),
        ],
        compiler_params=params(),
        cost_estimate=cost(3 * count * width * width, 10 * count * width),
        name="leave",
    )(mixed, wo, bo, tokens, live_col, pos_col)


def pick_kernel(residual, pos_col, out):
    out[...] = nn(pick_slots(pos_col[...], residual.shape[0]), residual[...]).astype(BF16)


def pick(residual, pos_col):
    count, width = residual.shape
    rows = pos_col.shape[0]
    return pl.pallas_call(
        pick_kernel,
        grid=(1,),
        in_specs=[whole((count, width)), whole((rows, 1))],
        out_specs=whole((rows, width)),
        out_shape=jax.ShapeDtypeStruct((rows, width), BF16),
        compiler_params=params(),
        cost_estimate=cost(2 * rows * count * width, 6 * count * width),
        name="pick",
    )(residual, pos_col)


def reenter_kernel(parts, *refs):
    slots = refs[:parts]
    pos_row, live_col, wo, grad_residual, grad_proj, grad_mixed, bias_sum = refs[parts : parts + 7]
    slots_in, wo_in, low, sems = refs[parts + 7 :]
    copies = Copies(sems)
    came, start = [], 0
    for part in slots:
        size = part.shape[0]
        came.append(copies.start(part, slots_in.at[pl.ds(start, size)]))
        start += size
    wo_came = copies.start(wo, wo_in)
    for copy in came:
        copy.wait()
    count = slots_in.shape[0]
    half = count // 2
    total, left = None, []
    for r in range(0, count, half):
        rows = pl.ds(r, half)
        picked = nn(pick_rows(r, pos_row[...], half, count), slots_in[...])
        masked = live_col[rows, :] * picked
        low[0, rows, :] = picked.astype(BF16)
        low[1, rows, :] = masked.astype(BF16)
        part = jnp.sum(masked, axis=0, keepdims=True)
        total = part if total is None else total + part
        left.append(copies.start(low.at[0, rows], grad_residual.at[rows]))
        left.append(copies.start(low.at[1, rows], grad_proj.at[rows]))
    bias_sum[...] = total
    wo_came.wait()
    for r in range(0, count, half):
        rows = pl.ds(r, half)
        low[2, rows, :] = nt(low[1, rows, :], wo_in[...]).astype(BF16)
        left.append(copies.start(low.at[2, rows], grad_mixed.at[rows]))
    for copy in left:
        copy.wait()


def reenter(slots, pos_row, live_col, wo):
    parts = len(slots)
    width = slots[0].shape[1]
    count = sum(v.shape[0] for v in slots)
    out = jax.ShapeDtypeStruct((count, width), BF16)
    return pl.pallas_call(
        functools.partial(reenter_kernel, parts),
        grid=(1,),
        in_specs=[ANYWHERE] * parts + [whole((1, count)), whole((count, 1)), ANYWHERE],
        out_specs=[ANYWHERE] * 3 + [whole((1, width))],
        out_shape=[out] * 3 + [jax.ShapeDtypeStruct((1, width), F32)],
        scratch_shapes=[
            pltpu.VMEM((count, width), BF16),
            pltpu.VMEM((width, width), BF16),
            pltpu.VMEM((3, count, width), BF16),
            pltpu.SemaphoreType.DMA((parts + 7,)),
        ],
        compiler_params=params(),
        cost_estimate=cost(4 * count * width * width, 10 * count * width),
        name="reenter",
    )(*slots, pos_row, live_col, wo)


def attend_back_kernel(
    start_row, q_ref, k_ref, v_ref, o_ref, g_ref, lse_ref, out_ref, bias, dq_sum
):
    count, lanes = q_ref.shape

    @pl.when(pl.program_id(0) == 0)
    def _():
        for j in range(count // ROWS):
            cols = pl.ds(j * ROWS, count - j * ROWS)
            shape = (ROWS, count - j * ROWS)
            kpos = lax.broadcasted_iota(jnp.int32, shape, 0) + j * ROWS
            qpos = lax.broadcasted_iota(jnp.int32, shape, 1) + j * ROWS
            keep = (kpos >= start_row[:, cols]) & (kpos <= qpos)
            bias[pl.ds(j * ROWS, ROWS), cols] = jnp.where(keep, 0.0, NEG)

    products = o_ref[...].astype(F32) * g_ref[...].astype(F32)
    high = products.astype(BF16)
    low = (products - high.astype(F32)).astype(BF16)
    sel_row = lax.broadcasted_iota(jnp.int32, (8, lanes), 0)
    sel_lane = lax.broadcasted_iota(jnp.int32, (8, lanes), 1)
    select = jnp.where(sel_row == sel_lane // (lanes // 2), 1.0, 0.0).astype(BF16)
    deltas = nt(select, high) + nt(select, low)

    queries = split_heads(q_ref[...])
    grads = split_heads(g_ref[...])
    for j in range(count // ROWS):
        rows = pl.ds(j * ROWS, ROWS)
        ext = slice(j * ROWS, count)
        keys, vals = k_ref[rows, :], v_ref[rows, :]
        dk = dv = dq = None
        for h, key in enumerate(split_heads(keys)):
            query, grad = queries[h][ext], grads[h][ext]
            score = nt(keys, query) * LOG2E + bias[rows, ext]
            weights = jnp.exp2(score - lse_ref[0, h : h + 1, ext])
            weights_low = weights.astype(BF16)
            grad_weights = nt(vals, grad)
            grad_score = (weights * (grad_weights - deltas[h : h + 1, ext])).astype(BF16)
            dv_part = nn(weights_low, grad)
            dk_part = nn(grad_score, query)
            dq_part = tn(grad_score, key)
            dv = dv_part if dv is None else dv + dv_part
            dk = dk_part if dk is None else dk + dk_part
            dq = dq_part if dq is None else dq + dq_part
        out_ref[1, rows, :] = dk.astype(BF16)
        out_ref[2, rows, :] = dv.astype(BF16)
        if j == 0:
            dq_sum[...] = dq
        else:
            dq_sum[ext, :] += dq
    out_ref[0] = (dq_sum[...] * 0.125).astype(BF16)


def attend_back(start_row, q, k, v, mixed, grad_mixed, lse):
    count, width = q.shape
    pairs = HEADS // 2
    lanes = width // pairs
    col = pl.BlockSpec((count, lanes), lambda p: (0, p))
    return pl.pallas_call(
        attend_back_kernel,
        grid=(pairs,),
        in_specs=[whole((1, count))]
        + [col] * 5
        + [pl.BlockSpec((1, 8, count), lambda p: (p, 0, 0))],
        out_specs=pl.BlockSpec((3, count, lanes), lambda p: (0, 0, p)),
        out_shape=jax.ShapeDtypeStruct((3, count, width), BF16),
        scratch_shapes=[pltpu.VMEM((count, count), F32), pltpu.VMEM((count, lanes), F32)],
        compiler_params=params(),
        cost_estimate=cost(20 * count * count * width, 16 * count * width, HEADS * count * count // 2),
        name="attend_back",
    )(start_row, q, k, v, mixed, grad_mixed, lse)


def finish_kernel(grads, wq, wk, wv, tokens, grad_residual, gain, pos_col, others, *refs):
    outs, sums = refs[:-8], refs[-8]
    grads_in, weights, tokens_in, residual_in, total, kept, sems = refs[-7:]
    copies = Copies(sems)
    came = []
    for n, w in enumerate((wq, wk, wv)):
        came.append((copies.start(grads.at[n], grads_in.at[n]), copies.start(w, weights.at[n])))
    rest = [copies.start(tokens, tokens_in), copies.start(grad_residual, residual_in)]
    count = kept.shape[0]
    half = count // 2
    for n in range(3):
        for copy in came[n]:
            copy.wait()
        for r in range(0, count, half):
            rows = pl.ds(r, half)
            part = nt(grads_in[n, rows, :], weights[n])
            if n == 0:
                total[rows, :] = part
            else:
                total[rows, :] += part
    for copy in rest:
        copy.wait()
    sums[...] = others[...]
    for r in range(0, count, ROWS):
        rows = pl.ds(r, ROWS)
        grad = total[rows, :]
        normal, root = norm_parts(tokens_in[rows, :].astype(F32))
        kept[rows, :] = (
            residual_in[rows, :].astype(F32) + norm_grad(grad, normal, root, gain[...])
        ).astype(BF16)
        sums[0:1, :] += jnp.sum(grad * normal, axis=0, keepdims=True)
        sums[1:2, :] += jnp.sum(grad, axis=0, keepdims=True)
        sums[2:3, :] += jnp.sum(grads_in[0, rows, :].astype(F32), axis=0, keepdims=True)
        sums[3:4, :] += jnp.sum(grads_in[2, rows, :].astype(F32), axis=0, keepdims=True)
    left = []
    for r in range(0, count, half):
        rows = pl.ds(r, half)
        chosen = pick_slots(pos_col[rows, :], count)
        residual_in[rows, :] = nn(chosen, kept[...]).astype(BF16)
    start = 0
    for out in outs:
        rows = out.shape[0]
        left.append(copies.start(residual_in.at[pl.ds(start, rows)], out))
        start += rows
    for copy in left:
        copy.wait()


def finish(sizes, grads, weights, tokens, grad_residual, gain, pos_col, others):
    count, width = tokens.shape
    return pl.pallas_call(
        finish_kernel,
        grid=(1,),
        in_specs=[ANYWHERE] * 6 + [whole((1, width)), whole((count, 1)), whole((8, width))],
        out_specs=[ANYWHERE] * len(sizes) + [whole((8, width))],
        out_shape=[jax.ShapeDtypeStruct((rows, width), BF16) for rows in sizes]
        + [jax.ShapeDtypeStruct((8, width), F32)],
        scratch_shapes=[
            pltpu.VMEM((3, count, width), BF16),
            pltpu.VMEM((3, width, width), BF16),
            pltpu.VMEM((count, width), BF16),
            pltpu.VMEM((count, width), BF16),
            pltpu.VMEM((count, width), F32),
            pltpu.VMEM((count, width), BF16),
            pltpu.SemaphoreType.DMA((8 + len(sizes),)),
        ],
        compiler_params=params(),
        cost_estimate=cost(8 * count * width * width, 20 * count * width),
        name="finish",
    )(grads, *weights, tokens, grad_residual, gain, pos_col, others)


GELU_ROOT = math.sqrt(2.0 / math.pi)
GELU_CUBE = 0.044715
STEP = 1024


def shard_of(step):
    return (step % 2) * 2 + step // 2


def expert_kernel(device, *refs):
    it = iter(refs)
    take = lambda n: [next(it) for _ in range(n)]
    slots, cots, lives = take(3)
    up, down, up_bias, gain, offset = take(5)
    grads, mine, theirs, sums, up_sums = take(5)
    ffn_in, branch, grad_sum = take(3)
    rows, model = slots.shape
    t = pl.program_id(0)

    @pl.when(t == 0)
    def _():
        normal, _ = norm_parts(slots[...].astype(F32))
        ffn_in[...] = (normal * gain[...] + offset[...]).astype(BF16)
        cot = cots[...].reshape(rows, model).astype(F32)
        branch[...] = (lives[...].reshape(rows, 1) * cot).astype(BF16)
        theirs[0] = ffn_in[...]
        theirs[1] = branch[...]
        grad_sum[...] = jnp.zeros_like(grad_sum)

    @pl.when(t == 2)
    def _():
        mine[0] = ffn_in[...]
        mine[1] = branch[...]

    width = up.shape[2]

    def compute(out):
        for c in range(0, width, STEP):
            cols = pl.ds(c, STEP)
            pre = nn(ffn_in[...], up[0, :, cols]) + up_bias[0, :, cols]
            square = pre * pre
            tanh = jnp.tanh(pre * (GELU_ROOT + (GELU_ROOT * GELU_CUBE) * square))
            half = 0.5 * (1.0 + tanh)
            slope = half + (0.5 * pre) * (1.0 - tanh * tanh) * (
                GELU_ROOT + (3.0 * GELU_ROOT * GELU_CUBE) * square
            )
            out[0, :, cols] = (pre * half).astype(BF16)
            grad_pre = (nt(branch[...], down[0, cols, :]) * slope).astype(BF16)
            out[1, :, cols] = grad_pre
            up_sums[0, :, cols] = jnp.sum(grad_pre.astype(F32), axis=0, keepdims=True)
            grad_sum[...] += nt(grad_pre, up[0, :, cols])

    @pl.when(t < 2)
    def _():
        compute(mine)

    @pl.when(t >= 2)
    def _():
        compute(theirs)

    @pl.when(t == 3)
    def _():
        routed = slots[...].astype(F32)
        normal, root = norm_parts(routed)
        grad = grad_sum[...]
        cot = cots[...].reshape(rows, model).astype(F32)
        grads[...] = (cot + norm_grad(grad, normal, root, gain[...])).astype(BF16)
        sums[...] = jnp.zeros_like(sums)
        sums[0:1, :] = jnp.sum(grad * normal, axis=0, keepdims=True)
        sums[1:2, :] = jnp.sum(grad, axis=0, keepdims=True)
        sums[2:3, :] = jnp.sum(branch[...].astype(F32), axis=0, keepdims=True)


def expert_chunk(chunk, device, slots, cot, live, ups, downs, up_bias, gain, offset):
    rows, width = slots.shape
    groups, piece, _ = cot.shape
    short = rows // groups
    part = ups.shape[2]
    assert part == width and ups.shape[0] == 4
    block = pl.BlockSpec((groups, short, width), lambda t, *_: (0, chunk, 0))
    packet = jax.ShapeDtypeStruct((6, rows, width), BF16)
    weights = pl.BlockSpec((1, width, part), lambda t, device: (shard_of(t) ^ device[0], 0, 0))
    bias = pl.BlockSpec((1, 1, part), lambda t, device: (shard_of(t) ^ device[0], 0, 0))
    return pl.pallas_call(
        expert_kernel,
        grid_spec=pltpu.PrefetchScalarGridSpec(
            num_scalar_prefetch=1,
            grid=(4,),
            in_specs=[
                whole((rows, width)),
                block,
                pl.BlockSpec((groups, short, 1), lambda t, *_: (0, chunk, 0)),
            ]
            + [weights, weights, bias, whole((1, width)), whole((1, width))],
            out_specs=[
                whole((rows, width)),
                pl.BlockSpec((2, rows, width), lambda t, *_: (jnp.minimum(t, 2), 0, 0)),
                pl.BlockSpec((2, rows, width), lambda t, *_: (jnp.where(t < 2, 2, t - 2), 0, 0)),
                whole((8, width)),
                bias,
            ],
            scratch_shapes=[
                pltpu.VMEM((rows, width), BF16),
                pltpu.VMEM((rows, width), BF16),
                pltpu.VMEM((rows, width), F32),
            ],
        ),
        out_shape=[
            jax.ShapeDtypeStruct((rows, width), BF16),
            packet,
            packet,
            jax.ShapeDtypeStruct((8, width), F32),
            jax.ShapeDtypeStruct((4, 1, part), F32),
        ],
        compiler_params=params(),
        cost_estimate=cost(24 * rows * width * part, 16 * width * part, 4 * rows * part),
        name="expert_chunk",
    )(device, slots, cot, live, ups, downs, up_bias, gain, offset)


def expert_out_kernel(chunks, device, *refs):
    mine, theirs, slots = refs[:chunks], refs[chunks : 2 * chunks], refs[2 * chunks : 3 * chunks]
    down, bias, live, out, total = refs[3 * chunks :]
    t = pl.program_id(0)
    rows = slots[0].shape[0]
    for n in range(4):

        @pl.when(t == n)
        def _(n=n):
            for c in range(chunks):
                part = nn((mine if n < 2 else theirs)[c][0], down[0])
                if n == 0:
                    total[c * rows : (c + 1) * rows, :] = part
                else:
                    total[c * rows : (c + 1) * rows, :] += part

    @pl.when(t == 3)
    def _():
        groups, piece, width = out.shape
        short = piece // chunks
        for c in range(chunks):
            branch = total[c * rows : (c + 1) * rows, :] + bias[...]
            keep = live[:, c * short : (c + 1) * short, :].reshape(rows, 1)
            value = (slots[c][...].astype(F32) + keep * branch).astype(BF16)
            out[:, c * short : (c + 1) * short, :] = value.reshape(groups, short, width)


def expert_out(device, mine, theirs, slots, downs, bias, live):
    chunks = len(slots)
    rows, width = slots[0].shape
    part = downs.shape[1]
    groups, piece, _ = live.shape
    act = lambda index: pl.BlockSpec((1, rows, part), index)
    return pl.pallas_call(
        functools.partial(expert_out_kernel, chunks),
        grid_spec=pltpu.PrefetchScalarGridSpec(
            num_scalar_prefetch=1,
            grid=(4,),
            in_specs=[act(lambda t, *_: (2 * jnp.minimum(t, 1), 0, 0))] * chunks
            + [act(lambda t, *_: (2 * jnp.maximum(t - 2, 0), 0, 0))] * chunks
            + [whole((rows, width))] * chunks
            + [pl.BlockSpec((1, part, width), lambda t, device: (shard_of(t) ^ device[0], 0, 0))]
            + [whole((1, width)), whole((groups, piece, 1))],
            out_specs=whole((groups, piece, width)),
            scratch_shapes=[pltpu.VMEM((chunks * rows, width), F32)],
        ),
        out_shape=jax.ShapeDtypeStruct((groups, piece, width), BF16),
        compiler_params=params(),
        cost_estimate=cost(8 * chunks * rows * part * width, 32 * rows * width),
        name="expert_out",
    )(device, *mine, *theirs, *slots, downs, bias, live)


CUTS = ((224, 800), (304, 400, 320))


def expert_grads_kernel(count, *refs):
    packets, near, fars = refs[:count], refs[count : count + 2], refs[count + 2 : -9]
    far_act, branch, ffn_in, far_pre, near_act, near_pre, far_low, near_full, sems = refs[-9:]
    copies = Copies(sems)
    rows = packets[0].shape[1]

    def fetch(slot, target):
        return [copies.start(p.at[slot], target.at[pl.ds(n * rows, rows)]) for n, p in enumerate(packets)]

    first = fetch(2, far_act) + fetch(5, branch)
    second = fetch(4, ffn_in) + fetch(3, far_pre)
    third = fetch(0, near_act)
    fourth = fetch(1, near_pre)
    left = []

    def far(m, came, one, two):
        for copy in came:
            copy.wait()
        far_low[m] = tn(one[...], two[...]).astype(BF16)
        start, skip = 0, sum(len(cuts) for cuts in CUTS[:m])
        for n, cut in enumerate(CUTS[m]):
            left.append(copies.start(far_low.at[m, pl.ds(start, cut)], fars[skip + n]))
            start += cut

    def close(m, came, one, two):
        for copy in came:
            copy.wait()
        near_full[m] = tn(one[...], two[...])
        left.append(copies.start(near_full.at[m], near[m].at[0]))

    far(0, first, far_act, branch)
    far(1, second, ffn_in, far_pre)
    close(0, third, near_act, branch)
    close(1, fourth, ffn_in, near_pre)
    for copy in left:
        copy.wait()


def expert_grads(packets):
    _, rows, width = packets[0].shape
    count = len(packets)
    assert sum(CUTS[0]) == sum(CUTS[1]) == width
    cuts = [c for cuts in CUTS for c in cuts]
    return pl.pallas_call(
        functools.partial(expert_grads_kernel, count),
        grid=(1,),
        in_specs=[ANYWHERE] * count,
        out_specs=[ANYWHERE] * (2 + len(cuts)),
        out_shape=[jax.ShapeDtypeStruct((1, width, width), F32)] * 2
        + [jax.ShapeDtypeStruct((c, width), BF16) for c in cuts],
        scratch_shapes=[pltpu.VMEM((count * rows, width), BF16)] * 6
        + [
            pltpu.VMEM((2, width, width), BF16),
            pltpu.VMEM((2, width, width), F32),
            pltpu.SemaphoreType.DMA((6 * count + 2 + len(cuts),)),
        ],
        compiler_params=params(),
        cost_estimate=cost(8 * count * rows * width * width, 30 * width * width),
        name="expert_grads",
    )(*packets)


def shared_grads_kernel(
    streams, blocks, codes, normed, mixed, token_grads, grad_proj, keep, send,
    left_in, right_in, total, low, sems
):
    copies = Copies(sems)
    number = right_in.shape[0]
    came = [[copies.start(normed, left_in.at[0]), copies.start(token_grads.at[0], right_in.at[0])]]
    came += [[copies.start(token_grads.at[m], right_in.at[m])] for m in range(1, number - 1)]
    came.append([copies.start(mixed, left_in.at[1]), copies.start(grad_proj, right_in.at[number - 1])])
    half = blocks // 2
    rows = total.shape[1]
    size = rows // half
    first = codes[0] // half
    left = []
    for m in range(number):
        for copy in came[m]:
            copy.wait()
        for h, target in enumerate((keep, send)):
            n = (2 * m + h) % 2
            side = pl.ds(pl.multiple_of((first ^ h) * rows, rows), rows)
            total[n] = tn(left_in[0 if m < number - 1 else 1, :, side], right_in[m])
            for j in range(half):
                code = codes[(j // (half // streams)) % streams] % half
                place = pl.multiple_of((code ^ j) * size, size)
                low[m, h, pl.ds(j * size, size), :] = total[n, pl.ds(place, size), :].astype(BF16)
            left.append(copies.start(low.at[m, h], target.at[m]))
    for copy in left:
        copy.wait()


def shared_grads(layout, normed, mixed, token_grads, grad_proj):
    count, width = normed.shape
    number = token_grads.shape[0] + 1
    half = width // 2
    return pl.pallas_call(
        functools.partial(shared_grads_kernel, layout.streams, layout.blocks),
        grid_spec=pltpu.PrefetchScalarGridSpec(
            num_scalar_prefetch=1,
            grid=(1,),
            in_specs=[ANYWHERE] * 4,
            out_specs=[ANYWHERE] * 2,
            scratch_shapes=[
                pltpu.VMEM((2, count, width), BF16),
                pltpu.VMEM((number, count, width), BF16),
                pltpu.VMEM((2, half, width), F32),
                pltpu.VMEM((number, 2, half, width), BF16),
                pltpu.SemaphoreType.DMA((3 * number + 2,)),
            ],
        ),
        out_shape=[jax.ShapeDtypeStruct((number, half, width), BF16)] * 2,
        compiler_params=params(),
        cost_estimate=cost(2 * number * count * width * width, 6 * number * width * width),
        name="shared_grads",
    )(layout.codes, normed, mixed, token_grads, grad_proj)


def unmix_kernel(group, parts, codes, half_place, source, pieces, *refs):
    rows_in, came_in, full, sems = refs[-4:]
    number, half, _ = came_in.shape
    outs = refs[-4 - number - min(parts, 1) : -4]
    copies = Copies(sems)
    came = [copies.start(pieces.at[m], came_in.at[m]) for m in range(number)]
    joined, left = [], []
    for r in range(parts):
        size = refs[r].shape[0]
        place = pl.multiple_of(source[r] * size, size)
        joined.append(copies.start(refs[r], rows_in.at[pl.ds(place, size)]))
    rows = half // 4
    size = rows // group
    for m in range(number):
        came[m].wait()
        for n in range(4):
            code = codes[n // 2]
            low = code % group
            block = n ^ ((code // group) % 2)
            for j in range(group):
                place = pl.multiple_of(block * rows + (low ^ j) * size, size)
                start = n * rows + j * size
                full[m, pl.ds(place, size), :] = came_in[m, start : start + size, :].astype(F32)
        target = outs[m].at[pl.ds(pl.multiple_of(half_place[0] * half, half), half)]
        left.append(copies.start(full.at[m], target))
        if m == 0 and parts:
            for copy in joined:
                copy.wait()
            left.append(copies.start(rows_in, outs[number]))
    for copy in left:
        copy.wait()


def unmix(layout, half_place, pieces, before=None, source=None, joined=()):
    number, rows, width = pieces.shape
    earlier = [] if before is None else list(before)
    parts = len(joined)
    source = half_place if source is None else source
    total = sum(v.shape[0] for v in joined)
    return pl.pallas_call(
        functools.partial(unmix_kernel, layout.blocks // 8, parts),
        grid_spec=pltpu.PrefetchScalarGridSpec(
            num_scalar_prefetch=3,
            grid=(1,),
            in_specs=[ANYWHERE] * (1 + parts + len(earlier)),
            out_specs=[ANYWHERE] * (number + min(parts, 1)),
            scratch_shapes=[
                pltpu.VMEM((max(total, 16), width), BF16),
                pltpu.VMEM((number, rows, width), BF16),
                pltpu.VMEM((number, rows, width), F32),
                pltpu.SemaphoreType.DMA((2 * number + parts + 1,)),
            ],
        ),
        out_shape=[jax.ShapeDtypeStruct((2 * rows, width), F32)] * number
        + [jax.ShapeDtypeStruct((total, width), BF16)] * min(parts, 1),
        input_output_aliases={4 + parts + m: m for m in range(len(earlier))},
        compiler_params=params(),
        cost_estimate=cost(number * rows * width, 6 * number * rows * width),
        name="unmix",
    )(layout.codes, half_place, source, pieces, *joined, *earlier)


def swap(values, step):
    axis, size, bit = step
    return lax.ppermute(values, axis, [(i, i ^ bit) for i in range(size)])


def exchange(values):
    return lax.all_to_all(values, "expert", split_axis=0, concat_axis=0, tiled=True)


def turn(values, size, by):
    return lax.ppermute(values, "expert", [(i, (i + by) % size) for i in range(size)])


def bits_of(size):
    return [1 << b for b in range(size.bit_length() - 1)]


def add_low(left, right):
    return (left.astype(F32) + right.astype(F32)).astype(BF16)


def tie(*values):
    return lax.optimization_barrier(values)


class SharedSum:
    streams = 2
    least = 16

    def __init__(self, n_expert, n_dp, rows):
        steps = [("dp", n_dp, b) for b in bits_of(n_dp)] + [
            ("expert", n_expert, b) for b in bits_of(n_expert)
        ]
        steps.sort(key=lambda s: (s[2], s[0]))
        self.steps = steps
        self.first, one, two, *rest = steps
        self.pair = ((two, one), (one, two))
        self.rest, self.left = rest[:2], rest[2:]
        self.blocks = 2 * self.streams * 4 * 4
        assert rows // self.blocks >= self.least and self.rest[0][0] == self.rest[1][0]
        self.codes = jnp.stack([self.code([self.first, None, *pair, *self.rest]) for pair in self.pair])

    def code(self, steps):
        total = jnp.int32(0)
        for step in steps:
            mine = 0 if step is None else (lax.axis_index(step[0]) // step[2]) % 2
            total = total * 2 + mine
        return total.astype(jnp.int32)

    @staticmethod
    def halve(values, step, axis):
        middle = values.shape[axis] // 2
        keep = lax.slice_in_dim(values, 0, middle, axis=axis)
        send = lax.slice_in_dim(values, middle, 2 * middle, axis=axis)
        return add_low(keep, swap(send, step))

    @staticmethod
    def double(values, step, axis):
        return jnp.concatenate([values, swap(values, step)], axis=axis)

    def reduce_first(self, keep, send):
        came = swap(send, self.first)
        size = keep.shape[1] // 4
        quarter = lambda v, n: lax.slice_in_dim(v, n * size, (n + 1) * size, axis=1)
        return [add_low(quarter(keep, n), quarter(came, n)) for n in range(4)]

    def reduce_pair_first(self, quarters):
        return [
            add_low(quarters[2 * n], swap(quarters[2 * n + 1], self.pair[n][0]))
            for n in range(self.streams)
        ]

    def reduce_pair(self, parts, n):
        return [self.halve(part, pair[n], 1) for part, pair in zip(parts, self.pair)]

    def partners(self, total, j):
        (axis, size, high), (_, _, low) = self.rest
        return swap(total, (axis, size, (j // 2) * high + (j % 2) * low))

    def reduce_rest(self, total):
        size = total.shape[2] // 4
        piece = lambda j: total[:, :, j * size : (j + 1) * size]
        sum_all = piece(0).astype(F32)
        for j in range(1, 4):
            sum_all = sum_all + self.partners(piece(j), j).astype(F32)
        total = sum_all.astype(BF16)
        for step in self.left:
            total = add_low(total, swap(total, step))
        return total

    def gather_rest(self, total):
        return jnp.concatenate([total] + [self.partners(total, j) for j in range(1, 4)], axis=2)

    def gather_pair(self, parts, n):
        return [self.double(part, pair[n], 1) for part, pair in zip(parts, self.pair)]

    def gather_first(self, parts):
        total = jnp.concatenate(parts, axis=1)
        mine = ((lax.axis_index(self.first[0]) // self.first[2]) % 2).astype(jnp.int32).reshape(1)
        return (mine, total), (1 - mine, swap(total, self.first))


def small_sum(values, steps):
    for step in steps:
        if step[0] == "dp":
            values = values + swap(values, step)
        else:
            part = values[:8]
            values = jnp.concatenate([part + swap(part, step), values[8:]], axis=0)
    return values


CHUNKS = 2


def per_device(
    n_expert,
    n_dp,
    block_in,
    seq_lengths,
    slot_position,
    first_gain,
    first_bias,
    query_weight,
    query_bias,
    key_weight,
    value_weight,
    value_bias,
    out_weight,
    out_bias,
    second_gain,
    second_bias,
    expert_up,
    expert_up_bias,
    expert_down,
    expert_down_bias,
    block_cot,
):
    count, width = block_in.shape
    piece = count // n_expert
    row = lambda v: v.reshape(1, -1)
    device = lax.axis_index("dp")
    part = expert_up.shape[2]
    dp_steps = [("dp", n_dp, b) for b in bits_of(n_dp)]
    all_steps = dp_steps + [("expert", n_expert, b) for b in bits_of(n_expert)]

    core, far = dp_steps
    ups = lax.all_gather(expert_up[0], "dp", axis=0)
    downs = lax.all_gather(expert_down[0], "dp", axis=0)
    arrived = exchange(block_in)

    position = slot_position[0]
    ends = jnp.cumsum(seq_lengths[0])
    total_live = ends[-1]
    ids = jnp.arange(count, dtype=jnp.int32)
    live = ids < total_live
    begin = jnp.max(jnp.where(ends[None, :] <= ids[:, None], ends[None, :], 0), axis=1)
    begin = jnp.where(live, begin, ids).astype(jnp.int32)
    live_col = live.astype(F32).reshape(count, 1)
    in_chunks = position.reshape(n_expert, CHUNKS, -1).transpose(1, 0, 2).reshape(count)
    slot_live = (position < total_live).astype(F32).reshape(n_expert, piece)
    start_row, start_col = begin.reshape(1, count), begin.reshape(count, 1)
    pos_row, pos_col = position.reshape(1, count), position.reshape(count, 1)
    chunk_row, chunk_col = in_chunks.reshape(1, count), in_chunks.reshape(count, 1)
    shared = SharedSum(n_expert, n_dp, width)
    expert = lax.axis_index("expert")
    codes = jnp.concatenate([jnp.arange(xs, n_expert, 2, dtype=jnp.int32) for xs in range(2)])
    partners = (expert ^ codes).astype(jnp.int32)
    leave_col = jnp.take(position.reshape(n_expert, piece), partners, axis=0).reshape(count, 1)
    leave_col, partners = tie(leave_col, partners)
    arrived, start_row, start_col, pos_row, pos_col, chunk_row, chunk_col, live_col, shared.codes = tie(
        arrived, start_row, start_col, pos_row, pos_col, chunk_row, chunk_col, live_col, shared.codes
    )
    route_live = exchange(slot_live).reshape(n_expert, piece, 1)

    tokens, normed, query, key, value = entry(
        arrived, pos_row, row(first_gain), row(first_bias), query_weight,
        row(query_bias), key_weight, value_weight, row(value_bias),
    )
    mixed, lse = attend(start_col, query, key, value)
    some = count // CHUNKS
    first, residual = leave(
        mixed, out_weight, row(out_bias), tokens, live_col, chunk_col[:some]
    )
    sent = [first] + [
        pick(residual, chunk_col[c * some : (c + 1) * some]) for c in range(1, CHUNKS)
    ]
    routed = [exchange(sent[0])]

    blocks = lambda v: v.reshape(n_expert, piece, width)
    place = device.astype(jnp.int32).reshape(1)
    up_bias = expert_up_bias[0].reshape(n_dp, 1, part)
    grads, mine, theirs, got, sums, up_sums = ([None] * CHUNKS for _ in range(6))
    returned = []
    for c in range(CHUNKS):
        grads[c], mine[c], theirs[c], sums[c], up_sums[c] = expert_chunk(
            c, place, routed[c], blocks(block_cot), route_live, ups, downs, up_bias,
            row(second_gain), row(second_bias),
        )
        if c > 0:
            returned.append(exchange(grads[c - 1]))
            got[c - 1] = swap(theirs[c - 1], core)
            returned[-1], got[c - 1], grads[c], mine[c], theirs[c] = tie(
                returned[-1], got[c - 1], grads[c], mine[c], theirs[c]
            )
        if c + 1 < CHUNKS:
            routed.append(exchange(sent[c + 1]))
            routed[c + 1], grads[c], mine[c], theirs[c] = tie(
                routed[c + 1], grads[c], mine[c], theirs[c]
            )
    returned.append(exchange(grads[-1]))
    got[-1] = swap(theirs[-1], core)

    *near, down_a, down_b, up_a, up_b, up_c = expert_grads([*mine, *got])
    sums, up_sums = sum(sums), sum(up_sums)
    empty = jnp.zeros((8, width), F32)
    biases = jnp.concatenate([up_sums.reshape(-1, width), sums[2:3], empty[: 7 - n_dp]], axis=0)

    fars = [down_a, down_b, up_a, up_b, up_c]

    def over_y(n):
        fars[n] = swap(fars[n], far)

    returned, near, fars, biases = tie(returned, near, fars, biases)
    grad_residual, grad_proj, grad_mixed, out_bias_sum = reenter(
        returned, chunk_row, live_col, out_weight
    )
    over_y(0)
    grad_mixed, fars = tie(grad_mixed, fars)
    unstack = lambda v: [v[:, n] for n in range(shared.streams)]

    over_y(1)
    token_grads = attend_back(
        start_row, query, key, value, mixed, grad_mixed, lse
    )
    token_grads, fars = tie(token_grads, fars)

    over_y(2)
    halves = shared_grads(shared, normed, mixed, token_grads, grad_proj)
    token_grads, halves, fars, out_bias_sum = tie(token_grads, halves, fars, out_bias_sum)

    others = jnp.concatenate([empty[:4], out_bias_sum, sums[0:2], empty[:1]], axis=0)
    total = shared.reduce_first(*halves)
    token_grads, total, others = tie(token_grads, total, others)

    side = n_expert // 2
    *leaving, token_sums = finish(
        [piece] * side + [piece * side // 2] * 2, token_grads, [query_weight, key_weight, value_weight],
        tokens, grad_residual, row(first_gain), leave_col, others,
    )
    total = shared.reduce_pair_first(total)
    leaving, token_sums, total = tie(leaving, token_sums, total)

    *stay, cross, cross_rest = leaving
    to_partner = lambda v, j: swap(v, ("expert", n_expert, 2 * j))
    early = range(1, 1 + (2 * side - 2 + 2) // 3)
    late = range(early.stop, side)
    small_steps = list(shared.steps)
    small_step = lambda v: small_sum(v, [small_steps.pop(0)])
    small = jnp.concatenate([token_sums, biases], axis=0)
    for j in early:
        stay[j] = to_partner(stay[j], j)
    small = small_step(small)
    total = jnp.stack(shared.reduce_pair(total, 1), axis=1)
    total, small, fars, mine, stay, cross, cross_rest = tie(
        total, small, fars, mine, stay, cross, cross_rest
    )

    over_y(3)
    cross = swap(cross, ("expert", n_expert, 1))
    block_out = expert_out(place, mine, theirs, routed, downs, row(expert_down_bias[0]), route_live)
    total = shared.reduce_rest(total)
    total, small, block_out, near, fars, cross, cross_rest = tie(
        total, small, block_out, near, fars, cross, cross_rest
    )

    over_y(4)
    total = unstack(shared.gather_rest(total))
    grad_down = near[0] + jnp.concatenate(fars[:2], axis=0).astype(F32)[None]
    cross_rest = swap(cross_rest, ("expert", n_expert, 1))
    total, small, grad_down, fars, stay, cross, cross_rest = tie(
        total, small, grad_down, fars, stay, cross, cross_rest
    )
    across = [v[j * piece : (j + 1) * piece] for v in (cross, cross_rest) for j in range(side // 2)]

    for j in late:
        stay[j] = to_partner(stay[j], j)
    across[1] = to_partner(across[1], 1)
    small = small_step(small_step(small))
    total = shared.gather_pair(total, 1)
    grad_up = near[1] + jnp.concatenate(fars[2:], axis=0).astype(F32)[None]
    total, small, stay, across, grad_up = tie(total, small, stay, across, grad_up)

    for j in range(2, side):
        across[j] = to_partner(across[j], j)
    total = shared.gather_pair(total, 0)
    small = small_sum(small, small_steps)
    total, small, across = tie(total, small, across)

    nearest, farthest = shared.gather_first(total)
    grads = unmix(shared, *nearest)
    grads, farthest = tie(grads, farthest)
    grad_query_weight, grad_key_weight, grad_value_weight, grad_out_weight, input_grad = unmix(
        shared, *farthest, grads, partners, [*stay, *across]
    )
    share = width // n_dp
    grad_up_bias = lax.dynamic_slice_in_dim(small, 8 + device, 1, 0)
    grad_down_bias = lax.dynamic_slice_in_dim(small[8 + n_dp : 9 + n_dp], device * share, share, 1)
    return (
        block_out.reshape(count, width),
        input_grad,
        small[0],
        small[1],
        grad_query_weight,
        small[2],
        grad_key_weight,
        grad_value_weight,
        small[3],
        grad_out_weight,
        small[4],
        small[5],
        small[6],
        grad_up,
        grad_up_bias,
        grad_down,
        grad_down_bias,
    )


def solution(mesh):
    both = P(("expert", "dp"), None)
    return jax.shard_map(
        functools.partial(per_device, mesh.shape["expert"], mesh.shape["dp"]),
        mesh=mesh,
        in_specs=(both,) * 3
        + (P(),) * 11
        + (P("expert", None, "dp"), P("expert", None), P("expert", "dp", None), P("expert", None), both),
        out_specs=(both,) * 2
        + (P(),) * 11
        + (P("expert", None, "dp"), P("expert", "dp"), P("expert", "dp", None), P("expert", "dp")),
        check_vma=False,
    )
```

```python
import functools
import math

import jax
import jax.numpy as jnp
from jax import lax
from jax.experimental import pallas as pl
from jax.experimental.pallas import tpu as pltpu
from jax.sharding import PartitionSpec as P

HEADS = 16
EPS = 1e-05
NEG = -1e30
LOG2E = math.log2(math.e)
F32 = jnp.float32
BF16 = jnp.bfloat16
VMEM_LIMIT = 60 * 1024 * 1024
ROWS = 256


def nn(a, b):
    return lax.dot_general(a, b, (((1,), (0,)), ((), ())), preferred_element_type=F32)


def nt(a, b):
    return lax.dot_general(a, b, (((1,), (1,)), ((), ())), preferred_element_type=F32)


def tn(a, b):
    return lax.dot_general(a, b, (((0,), (0,)), ((), ())), preferred_element_type=F32)


def params(**more):
    return pltpu.CompilerParams(vmem_limit_bytes=VMEM_LIMIT, **more)


def cost(flops, bytes_accessed, transcendentals=0):
    return pl.CostEstimate(
        flops=int(flops), bytes_accessed=int(bytes_accessed), transcendentals=int(transcendentals)
    )


def whole(shape):
    return pl.BlockSpec(shape, lambda *_: (0,) * len(shape))


def rows_of(block, width):
    return pl.BlockSpec((block, width), lambda i, *_: (i, 0))


def norm_parts(values):
    mean = jnp.mean(values, axis=-1, keepdims=True)
    center = values - mean
    variance = jnp.mean(center * center, axis=-1, keepdims=True)
    root = lax.rsqrt(variance + EPS)
    return center * root, root


def norm_grad(grad, normal, root, gain):
    scaled = grad * gain
    mean_plain = jnp.mean(scaled, axis=-1, keepdims=True)
    mean_normal = jnp.mean(scaled * normal, axis=-1, keepdims=True)
    return root * (scaled - mean_plain - normal * mean_normal)


def pick_rows(first_row, pos_row, rows, count):
    ids = lax.broadcasted_iota(jnp.int32, (rows, count), 0) + first_row
    return jnp.where(ids == pos_row, 1.0, 0.0).astype(BF16)


def pick_slots(pos_col, count):
    ids = lax.broadcasted_iota(jnp.int32, (pos_col.shape[0], count), 1)
    return jnp.where(ids == pos_col, 1.0, 0.0).astype(BF16)


ANYWHERE = pl.BlockSpec(memory_space=pl.ANY)


class Copies:
    def __init__(self, sems):
        self.sems, self.used = sems, 0

    def start(self, source, target):
        copy = pltpu.make_async_copy(source, target, self.sems.at[self.used])
        self.used += 1
        copy.start()
        return copy


def entry_kernel(
    slots, pos_row, gain, offset, wq, bq, wk, wv, bv, tokens, normed, q, k, v,
    slots_in, weights, low_tokens, low_normed, low_out, sems
):
    copies = Copies(sems)
    count = slots.shape[0]
    half = count // 2
    came = copies.start(slots, slots_in)
    weights_came = [copies.start(w, weights.at[n]) for n, w in enumerate((wq, wk, wv))]
    came.wait()
    left = []
    for r in range(0, count, ROWS):
        rows = pl.ds(r, ROWS)
        picked = nn(pick_rows(r, pos_row[...], ROWS, count), slots_in[...])
        low_tokens[rows, :] = picked.astype(BF16)
        normal, _ = norm_parts(picked)
        low_normed[rows, :] = (normal * gain[...] + offset[...]).astype(BF16)
    left += [copies.start(low_tokens, tokens), copies.start(low_normed, normed)]
    for n, out in enumerate((q, k, v)):
        weights_came[n].wait()
        for r in range(0, count, half):
            rows = pl.ds(r, half)
            value = nn(low_normed[rows, :], weights[n])
            if n == 0:
                value = (value + bq[...]).astype(BF16).astype(F32) * 0.125
            elif n == 2:
                value = value + bv[...]
            low_out[n, rows, :] = value.astype(BF16)
            left.append(copies.start(low_out.at[n, rows], out.at[rows]))
    for copy in left:
        copy.wait()


def entry(slots, pos_row, gain, offset, wq, bq, wk, wv, bv):
    count, width = slots.shape
    out = jax.ShapeDtypeStruct((count, width), BF16)
    return pl.pallas_call(
        entry_kernel,
        grid=(1,),
        in_specs=[
            ANYWHERE,
            whole((1, count)),
            whole((1, width)),
            whole((1, width)),
            ANYWHERE,
            whole((1, width)),
            ANYWHERE,
            ANYWHERE,
            whole((1, width)),
        ],
        out_specs=[ANYWHERE] * 5,
        out_shape=[out] * 5,
        scratch_shapes=[
            pltpu.VMEM((count, width), BF16),
            pltpu.VMEM((3, width, width), BF16),
            pltpu.VMEM((count, width), BF16),
            pltpu.VMEM((count, width), BF16),
            pltpu.VMEM((3, count, width), BF16),
            pltpu.SemaphoreType.DMA((12,)),
        ],
        compiler_params=params(),
        cost_estimate=cost(8 * count * width * width, 18 * count * width),
        name="entry",
    )(slots, pos_row, gain, offset, wq, bq, wk, wv, bv)


def half_masks(width):
    lane = lax.broadcasted_iota(jnp.int32, (1, width), 1)
    return lane < width // 2


def split_heads(values):
    first = half_masks(values.shape[1])
    zero = jnp.zeros_like(values)
    return jnp.where(first, values, zero), jnp.where(first, zero, values)


def fill_bias(bias, start_col):
    count = bias.shape[0]
    for i in range(count // ROWS):
        ext = (i + 1) * ROWS
        rows = pl.ds(i * ROWS, ROWS)
        kpos = lax.broadcasted_iota(jnp.int32, (ROWS, ext), 1)
        qpos = lax.broadcasted_iota(jnp.int32, (ROWS, ext), 0) + i * ROWS
        keep = (kpos >= start_col[rows, :]) & (kpos <= qpos)
        bias[rows, :ext] = jnp.where(keep, 0.0, NEG)


def largest_square(values):
    lanes = values.shape[1]
    row = lax.broadcasted_iota(jnp.int32, (8, lanes), 0)
    lane = lax.broadcasted_iota(jnp.int32, (8, lanes), 1)
    select = jnp.where(row == lane // (lanes // 2), 1.0, 0.0).astype(BF16)
    wide = values.astype(F32)
    return jnp.max(nt(select, (wide * wide).astype(BF16)), axis=1, keepdims=True)


SAFE = 50.0


def attend_kernel(start_col, q_ref, k_ref, v_ref, mixed_ref, lse_ref, bias, total, sums):
    count, lanes = q_ref.shape

    @pl.when(pl.program_id(0) == 0)
    def _():
        fill_bias(bias, start_col)

    first = half_masks(lanes)
    bound = jnp.max(largest_square(q_ref[...]) * largest_square(k_ref[...]))
    safe = bound * (LOG2E * LOG2E) < SAFE * SAFE

    @pl.when(safe)
    def _():
        queries = split_heads(q_ref[...])
        work = [(j, h) for j in range(count // ROWS) for h in range(2)]

        def scores(j, h):
            return nt(queries[h][j * ROWS :], k_ref[j * ROWS : (j + 1) * ROWS, :])

        ahead = scores(*work[0])
        for n, (j, h) in enumerate(work):
            score = ahead
            if n + 1 < len(work):
                ahead = scores(*work[n + 1])
            ext = pl.ds(j * ROWS, count - j * ROWS)
            cols = pl.ds(j * ROWS, ROWS)
            terms = jnp.exp2(score * LOG2E + bias[ext, cols])
            part_sum = terms[:, :lanes]
            for c in range(lanes, ROWS, lanes):
                part_sum = part_sum + terms[:, c : c + lanes]
            value = split_heads(v_ref[cols, :])[h]
            part = nn(terms.astype(BF16), value)
            if j == 0:
                sums[h] = part_sum
                total[h] = part
            else:
                sums[h, ext, :] += part_sum
                total[h, ext, :] += part
        norms = [jnp.sum(sums[h], axis=1, keepdims=True) for h in range(2)]
        norm = jnp.where(first, norms[0], norms[1])
        mixed_ref[...] = ((total[0] + total[1]) / norm).astype(BF16)
        turned = jnp.log2(norm).T
        lse_ref[0, 0:1, :] = turned[0:1, :]
        lse_ref[0, 1:2, :] = turned[lanes // 2 : lanes // 2 + 1, :]

    @pl.when(jnp.logical_not(safe))
    def _():
        for i in range(count // ROWS):
            ext = (i + 1) * ROWS
            rows = pl.ds(i * ROWS, ROWS)
            out, stats = None, []
            for query, value in zip(split_heads(q_ref[rows, :]), split_heads(v_ref[:ext, :])):
                score = nt(query, k_ref[:ext, :]) * LOG2E + bias[rows, :ext]
                top = jnp.max(score, axis=1, keepdims=True)
                terms = jnp.exp2(score - top)
                norm = jnp.sum(terms, axis=1, keepdims=True)
                part = nn(terms.astype(BF16), value)
                out = part if out is None else out + part
                stats.append((top + jnp.log2(norm), norm))
            norm = jnp.where(first, stats[0][1], stats[1][1])
            mixed_ref[rows, :] = (out / norm).astype(BF16)
            turned = jnp.where(first, stats[0][0], stats[1][0]).T
            lse_ref[0, 0:1, rows] = turned[0:1, :]
            lse_ref[0, 1:2, rows] = turned[lanes // 2 : lanes // 2 + 1, :]


def attend(start_col, q, k, v):
    count, width = q.shape
    pairs = HEADS // 2
    lanes = width // pairs
    col = pl.BlockSpec((count, lanes), lambda p: (0, p))
    return pl.pallas_call(
        attend_kernel,
        grid=(pairs,),
        in_specs=[whole((count, 1)), col, col, col],
        out_specs=[col, pl.BlockSpec((1, 8, count), lambda p: (p, 0, 0))],
        out_shape=[
            jax.ShapeDtypeStruct((count, width), BF16),
            jax.ShapeDtypeStruct((pairs, 8, count), F32),
        ],
        scratch_shapes=[
            pltpu.VMEM((count, count), F32),
            pltpu.VMEM((2, count, lanes), F32),
            pltpu.VMEM((2, count, lanes), F32),
        ],
        compiler_params=params(),
        cost_estimate=cost(8 * count * count * width, 8 * count * width, HEADS * count * count // 2),
        name="attend",
    )(start_col, q, k, v)


def leave_kernel(
    mixed, wo, bo, tokens, live_col, pos_col, out, residual, mixed_in, wo_in, tokens_in, kept, low, sems
):
    copies = Copies(sems)
    count = kept.shape[0]
    half = count // 2
    first = copies.start(wo, wo_in)
    came = []
    for r in range(0, count, half):
        rows = pl.ds(r, half)
        came.append(copies.start(mixed.at[rows], mixed_in.at[rows]))
        came.append(copies.start(tokens.at[rows], tokens_in.at[rows]))
    first.wait()
    for r in range(0, count, half):
        rows = pl.ds(r, half)
        for copy in came[:2]:
            copy.wait()
        came = came[2:]
        branch = nn(mixed_in[rows, :], wo_in[...]) + bo[...]
        kept[rows, :] = (tokens_in[rows, :].astype(F32) + live_col[rows, :] * branch).astype(BF16)
    left = [copies.start(kept, residual)]
    low[...] = nn(pick_slots(pos_col[...], count), kept[...]).astype(BF16)
    left.append(copies.start(low, out))
    for copy in left:
        copy.wait()


def leave(mixed, wo, bo, tokens, live_col, pos_col):
    count, width = mixed.shape
    rows = pos_col.shape[0]
    return pl.pallas_call(
        leave_kernel,
        grid=(1,),
        in_specs=[
            ANYWHERE,
            ANYWHERE,
            whole((1, width)),
            ANYWHERE,
            whole((count, 1)),
            whole((rows, 1)),
        ],
        out_specs=[ANYWHERE] * 2,
        out_shape=[
            jax.ShapeDtypeStruct((rows, width), BF16),
            jax.ShapeDtypeStruct((count, width), BF16),
        ],
        scratch_shapes=[
            pltpu.VMEM((count, width), BF16),
            pltpu.VMEM((width, width), BF16),
            pltpu.VMEM((count, width), BF16),
            pltpu.VMEM((count, width), BF16),
            pltpu.VMEM((rows, width), BF16),
            pltpu.SemaphoreType.DMA((7,)),
        ],
        compiler_params=params(),
        cost_estimate=cost(3 * count * width * width, 10 * count * width),
        name="leave",
    )(mixed, wo, bo, tokens, live_col, pos_col)


def pick_kernel(residual, pos_col, out):
    out[...] = nn(pick_slots(pos_col[...], residual.shape[0]), residual[...]).astype(BF16)


def pick(residual, pos_col):
    count, width = residual.shape
    rows = pos_col.shape[0]
    return pl.pallas_call(
        pick_kernel,
        grid=(1,),
        in_specs=[whole((count, width)), whole((rows, 1))],
        out_specs=whole((rows, width)),
        out_shape=jax.ShapeDtypeStruct((rows, width), BF16),
        compiler_params=params(),
        cost_estimate=cost(2 * rows * count * width, 6 * count * width),
        name="pick",
    )(residual, pos_col)


def reenter_kernel(parts, *refs):
    slots = refs[:parts]
    pos_row, live_col, wo, grad_residual, grad_proj, grad_mixed, bias_sum = refs[parts : parts + 7]
    slots_in, wo_in, low, sems = refs[parts + 7 :]
    copies = Copies(sems)
    came, start = [], 0
    for part in slots:
        size = part.shape[0]
        came.append(copies.start(part, slots_in.at[pl.ds(start, size)]))
        start += size
    wo_came = copies.start(wo, wo_in)
    for copy in came:
        copy.wait()
    count = slots_in.shape[0]
    half = count // 2
    total, left = None, []
    for r in range(0, count, half):
        rows = pl.ds(r, half)
        picked = nn(pick_rows(r, pos_row[...], half, count), slots_in[...])
        masked = live_col[rows, :] * picked
        low[0, rows, :] = picked.astype(BF16)
        low[1, rows, :] = masked.astype(BF16)
        part = jnp.sum(masked, axis=0, keepdims=True)
        total = part if total is None else total + part
        left.append(copies.start(low.at[0, rows], grad_residual.at[rows]))
        left.append(copies.start(low.at[1, rows], grad_proj.at[rows]))
    bias_sum[...] = total
    wo_came.wait()
    for r in range(0, count, half):
        rows = pl.ds(r, half)
        low[2, rows, :] = nt(low[1, rows, :], wo_in[...]).astype(BF16)
        left.append(copies.start(low.at[2, rows], grad_mixed.at[rows]))
    for copy in left:
        copy.wait()


def reenter(slots, pos_row, live_col, wo):
    parts = len(slots)
    width = slots[0].shape[1]
    count = sum(v.shape[0] for v in slots)
    out = jax.ShapeDtypeStruct((count, width), BF16)
    return pl.pallas_call(
        functools.partial(reenter_kernel, parts),
        grid=(1,),
        in_specs=[ANYWHERE] * parts + [whole((1, count)), whole((count, 1)), ANYWHERE],
        out_specs=[ANYWHERE] * 3 + [whole((1, width))],
        out_shape=[out] * 3 + [jax.ShapeDtypeStruct((1, width), F32)],
        scratch_shapes=[
            pltpu.VMEM((count, width), BF16),
            pltpu.VMEM((width, width), BF16),
            pltpu.VMEM((3, count, width), BF16),
            pltpu.SemaphoreType.DMA((parts + 7,)),
        ],
        compiler_params=params(),
        cost_estimate=cost(4 * count * width * width, 10 * count * width),
        name="reenter",
    )(*slots, pos_row, live_col, wo)


def attend_back_kernel(
    start_row, q_ref, k_ref, v_ref, o_ref, g_ref, lse_ref, out_ref, bias, sums
):
    count, lanes = q_ref.shape

    @pl.when(pl.program_id(0) == 0)
    def _():
        for j in range(count // ROWS):
            cols = pl.ds(j * ROWS, count - j * ROWS)
            shape = (ROWS, count - j * ROWS)
            kpos = lax.broadcasted_iota(jnp.int32, shape, 0) + j * ROWS
            qpos = lax.broadcasted_iota(jnp.int32, shape, 1) + j * ROWS
            keep = (kpos >= start_row[:, cols]) & (kpos <= qpos)
            bias[pl.ds(j * ROWS, ROWS), cols] = jnp.where(keep, 0.0, NEG)

    products = o_ref[...].astype(F32) * g_ref[...].astype(F32)
    high = products.astype(BF16)
    low = (products - high.astype(F32)).astype(BF16)
    sel_row = lax.broadcasted_iota(jnp.int32, (8, lanes), 0)
    sel_lane = lax.broadcasted_iota(jnp.int32, (8, lanes), 1)
    select = jnp.where(sel_row == sel_lane // (lanes // 2), 1.0, 0.0).astype(BF16)
    deltas = nt(select, high) + nt(select, low)

    queries = split_heads(q_ref[...])
    grads = split_heads(g_ref[...])
    wide = 2 * ROWS
    items = []
    for s in range(0, count, wide):
        if s + wide < count:
            items.append((s, s + wide, s + wide, count))
        items.append((s, s + ROWS, s, s + wide))
        items.append((s + ROWS, s + wide, s + ROWS, s + wide))
    work = [(item, h) for item in items for h in range(2)]

    def products_of(item, h):
        k_from, k_to, q_from, q_to = item
        return (
            nt(k_ref[k_from:k_to, :], queries[h][q_from:q_to]),
            nt(v_ref[k_from:k_to, :], grads[h][q_from:q_to]),
        )

    seen_keys, seen_queries = set(), set()

    def add(target, start, part, seen):
        for r in range(0, part.shape[0], ROWS):
            rows = pl.ds(start + r, ROWS)
            if start + r in seen:
                target[rows, :] += part[r : r + ROWS]
            else:
                target[rows, :] = part[r : r + ROWS]

    ahead = products_of(*work[0])
    for n, (item, h) in enumerate(work):
        k_from, k_to, q_from, q_to = item
        score, grad_weights = ahead
        if n + 1 < len(work):
            ahead = products_of(*work[n + 1])
        cols = slice(q_from, q_to)
        weights = jnp.exp2(score * LOG2E + bias[k_from:k_to, cols] - lse_ref[0, h : h + 1, cols])
        grad_score = (weights * (grad_weights - deltas[h : h + 1, cols])).astype(BF16)
        key = split_heads(k_ref[k_from:k_to, :])[h]
        add(sums.at[2], k_from, nn(weights.astype(BF16), grads[h][cols]), seen_keys)
        add(sums.at[1], k_from, nn(grad_score, queries[h][cols]), seen_keys)
        add(sums.at[0], q_from, tn(grad_score, key), seen_queries)
        seen_keys |= set(range(k_from, k_to, ROWS))
        seen_queries |= set(range(q_from, q_to, ROWS))
    out_ref[0] = (sums[0] * 0.125).astype(BF16)
    out_ref[1] = sums[1].astype(BF16)
    out_ref[2] = sums[2].astype(BF16)


def attend_back(start_row, q, k, v, mixed, grad_mixed, lse):
    count, width = q.shape
    pairs = HEADS // 2
    lanes = width // pairs
    col = pl.BlockSpec((count, lanes), lambda p: (0, p))
    return pl.pallas_call(
        attend_back_kernel,
        grid=(pairs,),
        in_specs=[whole((1, count))]
        + [col] * 5
        + [pl.BlockSpec((1, 8, count), lambda p: (p, 0, 0))],
        out_specs=pl.BlockSpec((3, count, lanes), lambda p: (0, 0, p)),
        out_shape=jax.ShapeDtypeStruct((3, count, width), BF16),
        scratch_shapes=[pltpu.VMEM((count, count), F32), pltpu.VMEM((3, count, lanes), F32)],
        compiler_params=params(),
        cost_estimate=cost(20 * count * count * width, 16 * count * width, HEADS * count * count // 2),
        name="attend_back",
    )(start_row, q, k, v, mixed, grad_mixed, lse)


def finish_kernel(grads, wq, wk, wv, tokens, grad_residual, gain, pos_col, others, *refs):
    outs, sums = refs[:-8], refs[-8]
    grads_in, weights, tokens_in, residual_in, total, kept, sems = refs[-7:]
    copies = Copies(sems)
    came = []
    for n, w in enumerate((wq, wk, wv)):
        came.append((copies.start(grads.at[n], grads_in.at[n]), copies.start(w, weights.at[n])))
    rest = [copies.start(tokens, tokens_in), copies.start(grad_residual, residual_in)]
    count = kept.shape[0]
    half = count // 2
    for n in range(3):
        for copy in came[n]:
            copy.wait()
        for r in range(0, count, half):
            rows = pl.ds(r, half)
            part = nt(grads_in[n, rows, :], weights[n])
            if n == 0:
                total[rows, :] = part
            else:
                total[rows, :] += part
    for copy in rest:
        copy.wait()
    sums[...] = others[...]
    for r in range(0, count, ROWS):
        rows = pl.ds(r, ROWS)
        grad = total[rows, :]
        normal, root = norm_parts(tokens_in[rows, :].astype(F32))
        kept[rows, :] = (
            residual_in[rows, :].astype(F32) + norm_grad(grad, normal, root, gain[...])
        ).astype(BF16)
        sums[0:1, :] += jnp.sum(grad * normal, axis=0, keepdims=True)
        sums[1:2, :] += jnp.sum(grad, axis=0, keepdims=True)
        sums[2:3, :] += jnp.sum(grads_in[0, rows, :].astype(F32), axis=0, keepdims=True)
        sums[3:4, :] += jnp.sum(grads_in[2, rows, :].astype(F32), axis=0, keepdims=True)
    left = []
    for r in range(0, count, half):
        rows = pl.ds(r, half)
        chosen = pick_slots(pos_col[rows, :], count)
        residual_in[rows, :] = nn(chosen, kept[...]).astype(BF16)
    start = 0
    for out in outs:
        rows = out.shape[0]
        left.append(copies.start(residual_in.at[pl.ds(start, rows)], out))
        start += rows
    for copy in left:
        copy.wait()


def finish(sizes, grads, weights, tokens, grad_residual, gain, pos_col, others):
    count, width = tokens.shape
    return pl.pallas_call(
        finish_kernel,
        grid=(1,),
        in_specs=[ANYWHERE] * 6 + [whole((1, width)), whole((count, 1)), whole((8, width))],
        out_specs=[ANYWHERE] * len(sizes) + [whole((8, width))],
        out_shape=[jax.ShapeDtypeStruct((rows, width), BF16) for rows in sizes]
        + [jax.ShapeDtypeStruct((8, width), F32)],
        scratch_shapes=[
            pltpu.VMEM((3, count, width), BF16),
            pltpu.VMEM((3, width, width), BF16),
            pltpu.VMEM((count, width), BF16),
            pltpu.VMEM((count, width), BF16),
            pltpu.VMEM((count, width), F32),
            pltpu.VMEM((count, width), BF16),
            pltpu.SemaphoreType.DMA((8 + len(sizes),)),
        ],
        compiler_params=params(),
        cost_estimate=cost(8 * count * width * width, 20 * count * width),
        name="finish",
    )(grads, *weights, tokens, grad_residual, gain, pos_col, others)


GELU_ROOT = math.sqrt(2.0 / math.pi)
GELU_CUBE = 0.044715
STEP = 1024


def shard_of(step):
    return (step % 2) * 2 + step // 2


def expert_kernel(parts, device, source, *refs):
    it = iter(refs)
    take = lambda n: [next(it) for _ in range(n)]
    slots, cots, lives = take(3)
    up, down, up_bias, gain, offset = take(5)
    grads = take(max(len(parts), 1))
    mine, theirs, sums, up_sums = take(4)
    ffn_in, branch, grad_sum, low = take(4)
    rows, model = slots.shape
    t = pl.program_id(0)

    @pl.when(t == 0)
    def _():
        normal, _ = norm_parts(slots[...].astype(F32))
        ffn_in[...] = (normal * gain[...] + offset[...]).astype(BF16)
        cot = cots[...].reshape(rows, model).astype(F32)
        branch[...] = (lives[...].reshape(rows, 1) * cot).astype(BF16)
        theirs[0] = ffn_in[...]
        theirs[1] = branch[...]
        grad_sum[...] = jnp.zeros_like(grad_sum)

    @pl.when(t == 2)
    def _():
        mine[0] = ffn_in[...]
        mine[1] = branch[...]

    width = up.shape[2]

    def compute(out):
        for c in range(0, width, STEP):
            cols = pl.ds(c, STEP)
            pre = nn(ffn_in[...], up[0, :, cols]) + up_bias[0, :, cols]
            square = pre * pre
            tanh = jnp.tanh(pre * (GELU_ROOT + (GELU_ROOT * GELU_CUBE) * square))
            half = 0.5 * (1.0 + tanh)
            slope = half + (0.5 * pre) * (1.0 - tanh * tanh) * (
                GELU_ROOT + (3.0 * GELU_ROOT * GELU_CUBE) * square
            )
            out[0, :, cols] = (pre * half).astype(BF16)
            grad_pre = (nt(branch[...], down[0, cols, :]) * slope).astype(BF16)
            out[1, :, cols] = grad_pre
            up_sums[0, :, cols] = jnp.sum(grad_pre.astype(F32), axis=0, keepdims=True)
            grad_sum[...] += nt(grad_pre, up[0, :, cols])

    @pl.when(t < 2)
    def _():
        compute(mine)

    @pl.when(t >= 2)
    def _():
        compute(theirs)

    @pl.when(t == 3)
    def _():
        routed = slots[...].astype(F32)
        normal, root = norm_parts(routed)
        grad = grad_sum[...]
        cot = cots[...].reshape(rows, model).astype(F32)
        grad_routed = (cot + norm_grad(grad, normal, root, gain[...])).astype(BF16)
        if not parts:
            grads[0][...] = grad_routed
        else:
            low[...] = grad_routed
            short, n = rows // sum(parts), 0
            for part, blocks in zip(grads, parts):
                for j in range(blocks):
                    place = pl.multiple_of(source[n] * short, short)
                    part[j * short : (j + 1) * short, :] = low[pl.ds(place, short), :]
                    n += 1
        sums[...] = jnp.zeros_like(sums)
        sums[0:1, :] = jnp.sum(grad * normal, axis=0, keepdims=True)
        sums[1:2, :] = jnp.sum(grad, axis=0, keepdims=True)
        sums[2:3, :] = jnp.sum(branch[...].astype(F32), axis=0, keepdims=True)


def expert_chunk(chunk, parts, device, source, slots, cot, live, ups, downs, up_bias, gain, offset):
    rows, width = slots.shape
    groups, piece, _ = cot.shape
    short = rows // groups
    sizes = [short * n for n in parts] or [rows]
    part = ups.shape[2]
    assert part == width and ups.shape[0] == 4
    block = pl.BlockSpec((groups, short, width), lambda t, *_: (0, chunk, 0))
    packet = jax.ShapeDtypeStruct((6, rows, width), BF16)
    weights = pl.BlockSpec((1, width, part), lambda t, device, *_: (shard_of(t) ^ device[0], 0, 0))
    bias = pl.BlockSpec((1, 1, part), lambda t, device, *_: (shard_of(t) ^ device[0], 0, 0))
    return pl.pallas_call(
        functools.partial(expert_kernel, parts),
        grid_spec=pltpu.PrefetchScalarGridSpec(
            num_scalar_prefetch=2,
            grid=(4,),
            in_specs=[
                whole((rows, width)),
                block,
                pl.BlockSpec((groups, short, 1), lambda t, *_: (0, chunk, 0)),
            ]
            + [weights, weights, bias, whole((1, width)), whole((1, width))],
            out_specs=[whole((size, width)) for size in sizes]
            + [
                pl.BlockSpec((2, rows, width), lambda t, *_: (jnp.minimum(t, 2), 0, 0)),
                pl.BlockSpec((2, rows, width), lambda t, *_: (jnp.where(t < 2, 2, t - 2), 0, 0)),
                whole((8, width)),
                bias,
            ],
            scratch_shapes=[
                pltpu.VMEM((rows, width), BF16),
                pltpu.VMEM((rows, width), BF16),
                pltpu.VMEM((rows, width), F32),
                pltpu.VMEM((rows, width), BF16),
            ],
        ),
        out_shape=[jax.ShapeDtypeStruct((size, width), BF16) for size in sizes]
        + [
            packet,
            packet,
            jax.ShapeDtypeStruct((8, width), F32),
            jax.ShapeDtypeStruct((4, 1, part), F32),
        ],
        compiler_params=params(),
        cost_estimate=cost(24 * rows * width * part, 16 * width * part, 4 * rows * part),
        name="expert_chunk",
    )(device, source, slots, cot, live, ups, downs, up_bias, gain, offset)


def expert_out_kernel(chunks, device, *refs):
    mine, theirs, slots = refs[:chunks], refs[chunks : 2 * chunks], refs[2 * chunks : 3 * chunks]
    down, bias, live, out, total = refs[3 * chunks :]
    t = pl.program_id(0)
    rows = slots[0].shape[0]
    for n in range(4):

        @pl.when(t == n)
        def _(n=n):
            for c in range(chunks):
                part = nn((mine if n < 2 else theirs)[c][0], down[0])
                if n == 0:
                    total[c * rows : (c + 1) * rows, :] = part
                else:
                    total[c * rows : (c + 1) * rows, :] += part

    @pl.when(t == 3)
    def _():
        groups, piece, width = out.shape
        short = piece // chunks
        for c in range(chunks):
            branch = total[c * rows : (c + 1) * rows, :] + bias[...]
            keep = live[:, c * short : (c + 1) * short, :].reshape(rows, 1)
            value = (slots[c][...].astype(F32) + keep * branch).astype(BF16)
            out[:, c * short : (c + 1) * short, :] = value.reshape(groups, short, width)


def expert_out(device, mine, theirs, slots, downs, bias, live):
    chunks = len(slots)
    rows, width = slots[0].shape
    part = downs.shape[1]
    groups, piece, _ = live.shape
    act = lambda index: pl.BlockSpec((1, rows, part), index)
    return pl.pallas_call(
        functools.partial(expert_out_kernel, chunks),
        grid_spec=pltpu.PrefetchScalarGridSpec(
            num_scalar_prefetch=1,
            grid=(4,),
            in_specs=[act(lambda t, *_: (2 * jnp.minimum(t, 1), 0, 0))] * chunks
            + [act(lambda t, *_: (2 * jnp.maximum(t - 2, 0), 0, 0))] * chunks
            + [whole((rows, width))] * chunks
            + [pl.BlockSpec((1, part, width), lambda t, device: (shard_of(t) ^ device[0], 0, 0))]
            + [whole((1, width)), whole((groups, piece, 1))],
            out_specs=whole((groups, piece, width)),
            scratch_shapes=[pltpu.VMEM((chunks * rows, width), F32)],
        ),
        out_shape=jax.ShapeDtypeStruct((groups, piece, width), BF16),
        compiler_params=params(),
        cost_estimate=cost(8 * chunks * rows * part * width, 32 * rows * width),
        name="expert_out",
    )(device, *mine, *theirs, *slots, downs, bias, live)


CUTS = ((224, 800), (304, 400, 320))


def expert_grads_kernel(count, near, *refs):
    packets, outs = refs[:count], refs[count:-6]
    act, branch, ffn_in, pre, full, sems = refs[-6:]
    copies = Copies(sems)
    rows = packets[0].shape[1]

    def fetch(slot, target):
        return [copies.start(p.at[slot], target.at[pl.ds(n * rows, rows)]) for n, p in enumerate(packets)]

    shard = 0 if near else 2
    first = fetch(shard, act) + fetch(5, branch)
    second = fetch(4, ffn_in) + fetch(shard + 1, pre)
    left = []
    for m, (came, one, two) in enumerate(((first, act, branch), (second, ffn_in, pre))):
        for copy in came:
            copy.wait()
        full[m] = tn(one[...], two[...]).astype(full.dtype)
        if near:
            left.append(copies.start(full.at[m], outs[m].at[0]))
            continue
        start, skip = 0, sum(len(cuts) for cuts in CUTS[:m])
        for n, cut in enumerate(CUTS[m]):
            left.append(copies.start(full.at[m, pl.ds(start, cut)], outs[skip + n]))
            start += cut
    for copy in left:
        copy.wait()


def expert_grads(near, packets):
    _, rows, width = packets[0].shape
    count = len(packets)
    assert sum(CUTS[0]) == sum(CUTS[1]) == width
    if near:
        shapes = [jax.ShapeDtypeStruct((1, width, width), F32)] * 2
    else:
        shapes = [jax.ShapeDtypeStruct((c, width), BF16) for cuts in CUTS for c in cuts]
    return pl.pallas_call(
        functools.partial(expert_grads_kernel, count, near),
        grid=(1,),
        in_specs=[ANYWHERE] * count,
        out_specs=[ANYWHERE] * len(shapes),
        out_shape=shapes,
        scratch_shapes=[pltpu.VMEM((count * rows, width), BF16)] * 4
        + [
            pltpu.VMEM((2, width, width), F32 if near else BF16),
            pltpu.SemaphoreType.DMA((4 * count + len(shapes),)),
        ],
        compiler_params=params(),
        cost_estimate=cost(4 * count * rows * width * width, 20 * width * width),
        name="near_grads" if near else "far_grads",
    )(*packets)


def shared_grads_kernel(
    streams, blocks, codes, normed, mixed, token_grads, grad_proj, keep, send,
    left_in, right_in, total, low, sems
):
    copies = Copies(sems)
    number = right_in.shape[0]
    came = [[copies.start(normed, left_in.at[0]), copies.start(token_grads.at[0], right_in.at[0])]]
    came += [[copies.start(token_grads.at[m], right_in.at[m])] for m in range(1, number - 1)]
    came.append([copies.start(mixed, left_in.at[1]), copies.start(grad_proj, right_in.at[number - 1])])
    half = blocks // 2
    rows = total.shape[1]
    size = rows // half
    first = codes[0] // half
    left = []
    for m in range(number):
        for copy in came[m]:
            copy.wait()
        for h, target in enumerate((keep, send)):
            n = (2 * m + h) % 2
            side = pl.ds(pl.multiple_of((first ^ h) * rows, rows), rows)
            total[n] = tn(left_in[0 if m < number - 1 else 1, :, side], right_in[m])
            for j in range(half):
                code = codes[(j // (half // streams)) % streams] % half
                place = pl.multiple_of((code ^ j) * size, size)
                low[m, h, pl.ds(j * size, size), :] = total[n, pl.ds(place, size), :].astype(BF16)
            left.append(copies.start(low.at[m, h], target.at[m]))
    for copy in left:
        copy.wait()


def shared_grads(layout, normed, mixed, token_grads, grad_proj):
    count, width = normed.shape
    number = token_grads.shape[0] + 1
    half = width // 2
    return pl.pallas_call(
        functools.partial(shared_grads_kernel, layout.streams, layout.blocks),
        grid_spec=pltpu.PrefetchScalarGridSpec(
            num_scalar_prefetch=1,
            grid=(1,),
            in_specs=[ANYWHERE] * 4,
            out_specs=[ANYWHERE] * 2,
            scratch_shapes=[
                pltpu.VMEM((2, count, width), BF16),
                pltpu.VMEM((number, count, width), BF16),
                pltpu.VMEM((2, half, width), F32),
                pltpu.VMEM((number, 2, half, width), BF16),
                pltpu.SemaphoreType.DMA((3 * number + 2,)),
            ],
        ),
        out_shape=[jax.ShapeDtypeStruct((number, half, width), BF16)] * 2,
        compiler_params=params(),
        cost_estimate=cost(2 * number * count * width * width, 6 * number * width * width),
        name="shared_grads",
    )(layout.codes, normed, mixed, token_grads, grad_proj)


def unmix_kernel(group, parts, codes, half_place, source, pieces, *refs):
    rows_in, came_in, full, sems = refs[-4:]
    number, half, _ = came_in.shape
    outs = refs[-4 - number - min(parts, 1) : -4]
    copies = Copies(sems)
    came = [copies.start(pieces.at[m], came_in.at[m]) for m in range(number)]
    joined, left = [], []
    for r in range(parts):
        size = refs[r].shape[0]
        place = pl.multiple_of(source[r] * size, size)
        joined.append(copies.start(refs[r], rows_in.at[pl.ds(place, size)]))
    rows = half // 4
    size = rows // group
    for m in range(number):
        came[m].wait()
        for n in range(4):
            code = codes[n // 2]
            low = code % group
            block = n ^ ((code // group) % 2)
            for j in range(group):
                place = pl.multiple_of(block * rows + (low ^ j) * size, size)
                start = n * rows + j * size
                full[m, pl.ds(place, size), :] = came_in[m, start : start + size, :].astype(F32)
        target = outs[m].at[pl.ds(pl.multiple_of(half_place[0] * half, half), half)]
        left.append(copies.start(full.at[m], target))
        if m == 0 and parts:
            for copy in joined:
                copy.wait()
            left.append(copies.start(rows_in, outs[number]))
    for copy in left:
        copy.wait()


def unmix(layout, half_place, pieces, before=None, source=None, joined=()):
    number, rows, width = pieces.shape
    earlier = [] if before is None else list(before)
    parts = len(joined)
    source = half_place if source is None else source
    total = sum(v.shape[0] for v in joined)
    return pl.pallas_call(
        functools.partial(unmix_kernel, layout.blocks // 8, parts),
        grid_spec=pltpu.PrefetchScalarGridSpec(
            num_scalar_prefetch=3,
            grid=(1,),
            in_specs=[ANYWHERE] * (1 + parts + len(earlier)),
            out_specs=[ANYWHERE] * (number + min(parts, 1)),
            scratch_shapes=[
                pltpu.VMEM((max(total, 16), width), BF16),
                pltpu.VMEM((number, rows, width), BF16),
                pltpu.VMEM((number, rows, width), F32),
                pltpu.SemaphoreType.DMA((2 * number + parts + 1,)),
            ],
        ),
        out_shape=[jax.ShapeDtypeStruct((2 * rows, width), F32)] * number
        + [jax.ShapeDtypeStruct((total, width), BF16)] * min(parts, 1),
        input_output_aliases={4 + parts + m: m for m in range(len(earlier))},
        compiler_params=params(),
        cost_estimate=cost(number * rows * width, 6 * number * rows * width),
        name="unmix",
    )(layout.codes, half_place, source, pieces, *joined, *earlier)


def swap(values, step):
    axis, size, bit = step
    return lax.ppermute(values, axis, [(i, i ^ bit) for i in range(size)])


def exchange(values):
    return lax.all_to_all(values, "expert", split_axis=0, concat_axis=0, tiled=True)


def turn(values, size, by):
    return lax.ppermute(values, "expert", [(i, (i + by) % size) for i in range(size)])


def bits_of(size):
    return [1 << b for b in range(size.bit_length() - 1)]


def add_low(left, right):
    return (left.astype(F32) + right.astype(F32)).astype(BF16)


def tie(*values):
    return lax.optimization_barrier(values)


class SharedSum:
    streams = 2
    least = 16

    def __init__(self, n_expert, n_dp, rows):
        steps = [("dp", n_dp, b) for b in bits_of(n_dp)] + [
            ("expert", n_expert, b) for b in bits_of(n_expert)
        ]
        steps.sort(key=lambda s: (s[2], s[0]))
        self.steps = steps
        self.first, one, two, *rest = steps
        self.pair = ((two, one), (one, two))
        self.rest, self.left = rest[:2], rest[2:]
        self.blocks = 2 * self.streams * 4 * 4
        assert rows // self.blocks >= self.least and self.rest[0][0] == self.rest[1][0]
        self.codes = jnp.stack([self.code([self.first, None, *pair, *self.rest]) for pair in self.pair])

    def code(self, steps):
        total = jnp.int32(0)
        for step in steps:
            mine = 0 if step is None else (lax.axis_index(step[0]) // step[2]) % 2
            total = total * 2 + mine
        return total.astype(jnp.int32)

    @staticmethod
    def halve(values, step, axis):
        middle = values.shape[axis] // 2
        keep = lax.slice_in_dim(values, 0, middle, axis=axis)
        send = lax.slice_in_dim(values, middle, 2 * middle, axis=axis)
        return add_low(keep, swap(send, step))

    @staticmethod
    def double(values, step, axis):
        return jnp.concatenate([values, swap(values, step)], axis=axis)

    def reduce_first(self, keep, send):
        came = swap(send, self.first)
        size = keep.shape[1] // 4
        quarter = lambda v, n: lax.slice_in_dim(v, n * size, (n + 1) * size, axis=1)
        return [add_low(quarter(keep, n), quarter(came, n)) for n in range(4)]

    def reduce_pair_first(self, quarters):
        return [
            add_low(quarters[2 * n], swap(quarters[2 * n + 1], self.pair[n][0]))
            for n in range(self.streams)
        ]

    def reduce_pair(self, parts, n):
        return [self.halve(part, pair[n], 1) for part, pair in zip(parts, self.pair)]

    def partners(self, total, j):
        (axis, size, high), (_, _, low) = self.rest
        return swap(total, (axis, size, (j // 2) * high + (j % 2) * low))

    def reduce_rest(self, total):
        size = total.shape[2] // 4
        piece = lambda j: total[:, :, j * size : (j + 1) * size]
        sum_all = piece(0).astype(F32)
        for j in range(1, 4):
            sum_all = sum_all + self.partners(piece(j), j).astype(F32)
        total = sum_all.astype(BF16)
        for step in self.left:
            total = add_low(total, swap(total, step))
        return total

    def gather_rest(self, total):
        return jnp.concatenate([total] + [self.partners(total, j) for j in range(1, 4)], axis=2)

    def gather_pair(self, parts, n):
        return [self.double(part, pair[n], 1) for part, pair in zip(parts, self.pair)]

    def gather_first(self, parts):
        total = jnp.concatenate(parts, axis=1)
        mine = ((lax.axis_index(self.first[0]) // self.first[2]) % 2).astype(jnp.int32).reshape(1)
        return (mine, total), (1 - mine, swap(total, self.first))


def small_sum(values, steps):
    for step in steps:
        if step[0] == "dp":
            values = values + swap(values, step)
        else:
            part = values[:8]
            values = jnp.concatenate([part + swap(part, step), values[8:]], axis=0)
    return values


CHUNKS = 2


def per_device(
    n_expert,
    n_dp,
    block_in,
    seq_lengths,
    slot_position,
    first_gain,
    first_bias,
    query_weight,
    query_bias,
    key_weight,
    value_weight,
    value_bias,
    out_weight,
    out_bias,
    second_gain,
    second_bias,
    expert_up,
    expert_up_bias,
    expert_down,
    expert_down_bias,
    block_cot,
):
    count, width = block_in.shape
    piece = count // n_expert
    row = lambda v: v.reshape(1, -1)
    device = lax.axis_index("dp")
    part = expert_up.shape[2]
    dp_steps = [("dp", n_dp, b) for b in bits_of(n_dp)]
    all_steps = dp_steps + [("expert", n_expert, b) for b in bits_of(n_expert)]

    core, far = dp_steps
    ups = lax.all_gather(expert_up[0], "dp", axis=0)
    downs = lax.all_gather(expert_down[0], "dp", axis=0)
    arrived = exchange(block_in)

    position = slot_position[0]
    ends = jnp.cumsum(seq_lengths[0])
    total_live = ends[-1]
    ids = jnp.arange(count, dtype=jnp.int32)
    live = ids < total_live
    begin = jnp.max(jnp.where(ends[None, :] <= ids[:, None], ends[None, :], 0), axis=1)
    begin = jnp.where(live, begin, ids).astype(jnp.int32)
    live_col = live.astype(F32).reshape(count, 1)
    in_chunks = position.reshape(n_expert, CHUNKS, -1).transpose(1, 0, 2).reshape(count)
    slot_live = (position < total_live).astype(F32).reshape(n_expert, piece)
    start_row, start_col = begin.reshape(1, count), begin.reshape(count, 1)
    pos_row, chunk_col = position.reshape(1, count), in_chunks.reshape(count, 1)
    shared = SharedSum(n_expert, n_dp, width)
    expert = lax.axis_index("expert")
    codes = jnp.concatenate([jnp.arange(xs, n_expert, 2, dtype=jnp.int32) for xs in range(2)])
    partners = (expert ^ codes).astype(jnp.int32)
    leave_col = jnp.take(position.reshape(n_expert, piece), partners, axis=0).reshape(count, 1)
    last_slots = jnp.take(position.reshape(n_expert, CHUNKS, -1)[:, -1], partners, axis=0)
    came_row = jnp.concatenate([in_chunks[: count - count // CHUNKS], last_slots.reshape(-1)])
    came_row = came_row.reshape(1, count)
    leave_col, partners, came_row = tie(leave_col, partners, came_row)
    arrived, start_row, start_col, pos_row, chunk_col, live_col, shared.codes = tie(
        arrived, start_row, start_col, pos_row, chunk_col, live_col, shared.codes
    )
    route_live = exchange(slot_live).reshape(n_expert, piece, 1)

    tokens, normed, query, key, value = entry(
        arrived, pos_row, row(first_gain), row(first_bias), query_weight,
        row(query_bias), key_weight, value_weight, row(value_bias),
    )
    mixed, lse = attend(start_col, query, key, value)
    some = count // CHUNKS
    first, residual = leave(
        mixed, out_weight, row(out_bias), tokens, live_col, chunk_col[:some]
    )
    sent = [first] + [
        pick(residual, chunk_col[c * some : (c + 1) * some]) for c in range(1, CHUNKS)
    ]
    routed = [exchange(sent[0])]

    blocks = lambda v: v.reshape(n_expert, piece, width)
    place = device.astype(jnp.int32).reshape(1)
    up_bias = expert_up_bias[0].reshape(n_dp, 1, part)
    grads, mine, theirs, got, sums, up_sums = ([None] * CHUNKS for _ in range(6))
    returned = []
    side = n_expert // 2
    to_partner = lambda v, j: swap(v, ("expert", n_expert, 2 * j))
    for c in range(CHUNKS):
        last = c + 1 == CHUNKS
        *grads[c], mine[c], theirs[c], sums[c], up_sums[c] = expert_chunk(
            c, (1,) * side + (side,) if last else (), place, partners, routed[c],
            blocks(block_cot), route_live, ups, downs, up_bias, row(second_gain), row(second_bias),
        )
        if c > 0:
            returned.append(exchange(grads[c - 1][0]))
            got[c - 1] = swap(theirs[c - 1], core)
            returned[-1], got[c - 1], grads[c], mine[c], theirs[c] = tie(
                returned[-1], got[c - 1], grads[c], mine[c], theirs[c]
            )
        if not last:
            routed.append(exchange(sent[c + 1]))
            routed[c + 1], grads[c], mine[c], theirs[c] = tie(
                routed[c + 1], grads[c], mine[c], theirs[c]
            )
    *stay, cross = grads[-1]
    got[-1] = swap(theirs[-1], core)
    cross = swap(cross, ("expert", n_expert, 1))
    stay = [v if j == 0 else to_partner(v, j) for j, v in enumerate(stay)]
    cross, got[-1] = tie(cross, got[-1])
    short = cross.shape[0] // side
    across = [cross[j * short : (j + 1) * short] for j in range(side)]
    across = [v if j == 0 else to_partner(v, j) for j, v in enumerate(across)]
    returned += stay + across

    fars = list(expert_grads(False, [*mine, *got]))
    sums, up_sums = sum(sums), sum(up_sums)
    empty = jnp.zeros((8, width), F32)
    biases = jnp.concatenate([up_sums.reshape(-1, width), sums[2:3], empty[: 7 - n_dp]], axis=0)

    def over_y(n):
        fars[n] = swap(fars[n], far)

    returned, fars, biases = tie(returned, fars, biases)
    packets = [*mine, *got]
    grad_residual, grad_proj, grad_mixed, out_bias_sum = reenter(
        returned, came_row, live_col, out_weight
    )
    over_y(0)
    grad_mixed, fars = tie(grad_mixed, fars)
    unstack = lambda v: [v[:, n] for n in range(shared.streams)]

    over_y(1)
    token_grads = attend_back(
        start_row, query, key, value, mixed, grad_mixed, lse
    )
    token_grads, fars = tie(token_grads, fars)

    over_y(2)
    halves = shared_grads(shared, normed, mixed, token_grads, grad_proj)
    token_grads, halves, fars, out_bias_sum = tie(token_grads, halves, fars, out_bias_sum)

    others = jnp.concatenate([empty[:4], out_bias_sum, sums[0:2], empty[:1]], axis=0)
    total = shared.reduce_first(*halves)
    token_grads, total, others = tie(token_grads, total, others)

    *leaving, token_sums = finish(
        [piece] * side + [piece * side // 2] * 2, token_grads, [query_weight, key_weight, value_weight],
        tokens, grad_residual, row(first_gain), leave_col, others,
    )
    total = shared.reduce_pair_first(total)
    leaving, token_sums, total = tie(leaving, token_sums, total)

    *stay, cross, cross_rest = leaving
    early = range(1, 1 + (2 * side - 2 + 2) // 3)
    late = range(early.stop, side)
    small_steps = list(shared.steps)
    small_step = lambda v: small_sum(v, [small_steps.pop(0)])
    small = jnp.concatenate([token_sums, biases], axis=0)
    for j in early:
        stay[j] = to_partner(stay[j], j)
    small = small_step(small)
    total = jnp.stack(shared.reduce_pair(total, 1), axis=1)
    total, small, fars, mine, stay, cross, cross_rest = tie(
        total, small, fars, mine, stay, cross, cross_rest
    )

    over_y(3)
    cross = swap(cross, ("expert", n_expert, 1))
    block_out = expert_out(place, mine, theirs, routed, downs, row(expert_down_bias[0]), route_live)
    total = shared.reduce_rest(total)
    total, small, block_out, packets, fars, cross, cross_rest = tie(
        total, small, block_out, packets, fars, cross, cross_rest
    )

    over_y(4)
    total = unstack(shared.gather_rest(total))
    near = list(expert_grads(True, packets))
    cross_rest = swap(cross_rest, ("expert", n_expert, 1))
    total, small, near, fars, stay, cross, cross_rest = tie(
        total, small, near, fars, stay, cross, cross_rest
    )
    across = [v[j * piece : (j + 1) * piece] for v in (cross, cross_rest) for j in range(side // 2)]

    for j in late:
        stay[j] = to_partner(stay[j], j)
    small = small_step(small_step(small))
    total = shared.gather_pair(total, 1)
    grad_up = near[1] + jnp.concatenate(fars[2:], axis=0).astype(F32)[None]
    total, small, stay, across, grad_up, near[0] = tie(total, small, stay, across, grad_up, near[0])

    middle = (side + 1) // 2 + 1
    for j in range(1, middle):
        across[j] = to_partner(across[j], j)
    total = shared.gather_pair(total, 0)
    small = small_sum(small, small_steps)
    grad_down = near[0] + jnp.concatenate(fars[:2], axis=0).astype(F32)[None]
    total, small, across, grad_down = tie(total, small, across, grad_down)

    for j in range(middle, side):
        across[j] = to_partner(across[j], j)
    nearest, farthest = shared.gather_first(total)
    grads = unmix(shared, *nearest)
    grads, farthest = tie(grads, farthest)
    grad_query_weight, grad_key_weight, grad_value_weight, grad_out_weight, input_grad = unmix(
        shared, *farthest, grads, partners, [*stay, *across]
    )
    share = width // n_dp
    grad_up_bias = lax.dynamic_slice_in_dim(small, 8 + device, 1, 0)
    grad_down_bias = lax.dynamic_slice_in_dim(small[8 + n_dp : 9 + n_dp], device * share, share, 1)
    return (
        block_out.reshape(count, width),
        input_grad,
        small[0],
        small[1],
        grad_query_weight,
        small[2],
        grad_key_weight,
        grad_value_weight,
        small[3],
        grad_out_weight,
        small[4],
        small[5],
        small[6],
        grad_up,
        grad_up_bias,
        grad_down,
        grad_down_bias,
    )


def solution(mesh):
    both = P(("expert", "dp"), None)
    return jax.shard_map(
        functools.partial(per_device, mesh.shape["expert"], mesh.shape["dp"]),
        mesh=mesh,
        in_specs=(both,) * 3
        + (P(),) * 11
        + (P("expert", None, "dp"), P("expert", None), P("expert", "dp", None), P("expert", None), both),
        out_specs=(both,) * 2
        + (P(),) * 11
        + (P("expert", None, "dp"), P("expert", "dp"), P("expert", "dp", None), P("expert", "dp")),
        check_vma=False,
    )
```

```python
import functools
import math

import jax
import jax.numpy as jnp
from jax import lax
from jax.experimental import pallas as pl
from jax.experimental.pallas import tpu as pltpu
from jax.sharding import PartitionSpec as P

HEADS = 16
EPS = 1e-05
NEG = -1e30
LOG2E = math.log2(math.e)
F32 = jnp.float32
BF16 = jnp.bfloat16
VMEM_LIMIT = 60 * 1024 * 1024
ROWS = 256


def nn(a, b):
    return lax.dot_general(a, b, (((1,), (0,)), ((), ())), preferred_element_type=F32)


def nt(a, b):
    return lax.dot_general(a, b, (((1,), (1,)), ((), ())), preferred_element_type=F32)


def tn(a, b):
    return lax.dot_general(a, b, (((0,), (0,)), ((), ())), preferred_element_type=F32)


def params(**more):
    return pltpu.CompilerParams(vmem_limit_bytes=VMEM_LIMIT, **more)


def cost(flops, bytes_accessed, transcendentals=0):
    return pl.CostEstimate(
        flops=int(flops), bytes_accessed=int(bytes_accessed), transcendentals=int(transcendentals)
    )


def whole(shape):
    return pl.BlockSpec(shape, lambda *_: (0,) * len(shape))


def rows_of(block, width):
    return pl.BlockSpec((block, width), lambda i, *_: (i, 0))


def norm_parts(values):
    mean = jnp.mean(values, axis=-1, keepdims=True)
    center = values - mean
    variance = jnp.mean(center * center, axis=-1, keepdims=True)
    root = lax.rsqrt(variance + EPS)
    return center * root, root


def norm_grad(grad, normal, root, gain):
    scaled = grad * gain
    mean_plain = jnp.mean(scaled, axis=-1, keepdims=True)
    mean_normal = jnp.mean(scaled * normal, axis=-1, keepdims=True)
    return root * (scaled - mean_plain - normal * mean_normal)


def pick_rows(first_row, pos_row, rows, count):
    ids = lax.broadcasted_iota(jnp.int32, (rows, count), 0) + first_row
    return jnp.where(ids == pos_row, 1.0, 0.0).astype(BF16)


def pick_slots(pos_col, count):
    ids = lax.broadcasted_iota(jnp.int32, (pos_col.shape[0], count), 1)
    return jnp.where(ids == pos_col, 1.0, 0.0).astype(BF16)


ANYWHERE = pl.BlockSpec(memory_space=pl.ANY)


class Copies:
    def __init__(self, sems):
        self.sems, self.used = sems, 0

    def start(self, source, target):
        copy = pltpu.make_async_copy(source, target, self.sems.at[self.used])
        self.used += 1
        copy.start()
        return copy


def entry_kernel(
    slots, pos_row, gain, offset, wq, bq, wk, wv, bv, tokens, normed, q, k, v,
    slots_in, weights, low_tokens, low_normed, low_out, sems
):
    copies = Copies(sems)
    count = slots.shape[0]
    half = count // 2
    came = copies.start(slots, slots_in)
    weights_came = [copies.start(w, weights.at[n]) for n, w in enumerate((wq, wk, wv))]
    came.wait()
    left = []
    for r in range(0, count, ROWS):
        rows = pl.ds(r, ROWS)
        picked = nn(pick_rows(r, pos_row[...], ROWS, count), slots_in[...])
        low_tokens[rows, :] = picked.astype(BF16)
        normal, _ = norm_parts(picked)
        low_normed[rows, :] = (normal * gain[...] + offset[...]).astype(BF16)
    left += [copies.start(low_tokens, tokens), copies.start(low_normed, normed)]
    for n, out in enumerate((q, k, v)):
        weights_came[n].wait()
        for r in range(0, count, half):
            rows = pl.ds(r, half)
            value = nn(low_normed[rows, :], weights[n])
            if n == 0:
                value = (value + bq[...]).astype(BF16).astype(F32) * 0.125
            elif n == 2:
                value = value + bv[...]
            low_out[n, rows, :] = value.astype(BF16)
            left.append(copies.start(low_out.at[n, rows], out.at[rows]))
    for copy in left:
        copy.wait()


def entry(slots, pos_row, gain, offset, wq, bq, wk, wv, bv):
    count, width = slots.shape
    out = jax.ShapeDtypeStruct((count, width), BF16)
    return pl.pallas_call(
        entry_kernel,
        grid=(1,),
        in_specs=[
            ANYWHERE,
            whole((1, count)),
            whole((1, width)),
            whole((1, width)),
            ANYWHERE,
            whole((1, width)),
            ANYWHERE,
            ANYWHERE,
            whole((1, width)),
        ],
        out_specs=[ANYWHERE] * 5,
        out_shape=[out] * 5,
        scratch_shapes=[
            pltpu.VMEM((count, width), BF16),
            pltpu.VMEM((3, width, width), BF16),
            pltpu.VMEM((count, width), BF16),
            pltpu.VMEM((count, width), BF16),
            pltpu.VMEM((3, count, width), BF16),
            pltpu.SemaphoreType.DMA((12,)),
        ],
        compiler_params=params(),
        cost_estimate=cost(8 * count * width * width, 18 * count * width),
        name="entry",
    )(slots, pos_row, gain, offset, wq, bq, wk, wv, bv)


def half_masks(width):
    lane = lax.broadcasted_iota(jnp.int32, (1, width), 1)
    return lane < width // 2


def split_heads(values):
    first = half_masks(values.shape[1])
    zero = jnp.zeros_like(values)
    return jnp.where(first, values, zero), jnp.where(first, zero, values)


def fill_bias(bias, start_col):
    count = bias.shape[0]
    for i in range(count // ROWS):
        ext = (i + 1) * ROWS
        rows = pl.ds(i * ROWS, ROWS)
        kpos = lax.broadcasted_iota(jnp.int32, (ROWS, ext), 1)
        qpos = lax.broadcasted_iota(jnp.int32, (ROWS, ext), 0) + i * ROWS
        keep = (kpos >= start_col[rows, :]) & (kpos <= qpos)
        bias[rows, :ext] = jnp.where(keep, 0.0, NEG)


def largest_square(values):
    lanes = values.shape[1]
    row = lax.broadcasted_iota(jnp.int32, (8, lanes), 0)
    lane = lax.broadcasted_iota(jnp.int32, (8, lanes), 1)
    select = jnp.where(row == lane // (lanes // 2), 1.0, 0.0).astype(BF16)
    wide = values.astype(F32)
    return jnp.max(nt(select, (wide * wide).astype(BF16)), axis=1, keepdims=True)


SAFE = 50.0


def attend_kernel(start_col, q_ref, k_ref, v_ref, mixed_ref, lse_ref, bias, total, sums):
    count, lanes = q_ref.shape

    @pl.when(pl.program_id(0) == 0)
    def _():
        fill_bias(bias, start_col)

    first = half_masks(lanes)
    bound = jnp.max(largest_square(q_ref[...]) * largest_square(k_ref[...]))
    safe = bound * (LOG2E * LOG2E) < SAFE * SAFE

    @pl.when(safe)
    def _():
        queries = split_heads(q_ref[...])
        work = [(j, h) for j in range(count // ROWS) for h in range(2)]

        def scores(j, h):
            return nt(queries[h][j * ROWS :], k_ref[j * ROWS : (j + 1) * ROWS, :])

        ahead = scores(*work[0])
        for n, (j, h) in enumerate(work):
            score = ahead
            if n + 1 < len(work):
                ahead = scores(*work[n + 1])
            ext = pl.ds(j * ROWS, count - j * ROWS)
            cols = pl.ds(j * ROWS, ROWS)
            terms = jnp.exp2(score * LOG2E + bias[ext, cols])
            part_sum = terms[:, :lanes]
            for c in range(lanes, ROWS, lanes):
                part_sum = part_sum + terms[:, c : c + lanes]
            value = split_heads(v_ref[cols, :])[h]
            part = nn(terms.astype(BF16), value)
            if j == 0:
                sums[h] = part_sum
                total[h] = part
            else:
                sums[h, ext, :] += part_sum
                total[h, ext, :] += part
        norms = [jnp.sum(sums[h], axis=1, keepdims=True) for h in range(2)]
        norm = jnp.where(first, norms[0], norms[1])
        mixed_ref[...] = ((total[0] + total[1]) / norm).astype(BF16)
        turned = jnp.log2(norm).T
        lse_ref[0, 0:1, :] = turned[0:1, :]
        lse_ref[0, 1:2, :] = turned[lanes // 2 : lanes // 2 + 1, :]

    @pl.when(jnp.logical_not(safe))
    def _():
        for i in range(count // ROWS):
            ext = (i + 1) * ROWS
            rows = pl.ds(i * ROWS, ROWS)
            out, stats = None, []
            for query, value in zip(split_heads(q_ref[rows, :]), split_heads(v_ref[:ext, :])):
                score = nt(query, k_ref[:ext, :]) * LOG2E + bias[rows, :ext]
                top = jnp.max(score, axis=1, keepdims=True)
                terms = jnp.exp2(score - top)
                norm = jnp.sum(terms, axis=1, keepdims=True)
                part = nn(terms.astype(BF16), value)
                out = part if out is None else out + part
                stats.append((top + jnp.log2(norm), norm))
            norm = jnp.where(first, stats[0][1], stats[1][1])
            mixed_ref[rows, :] = (out / norm).astype(BF16)
            turned = jnp.where(first, stats[0][0], stats[1][0]).T
            lse_ref[0, 0:1, rows] = turned[0:1, :]
            lse_ref[0, 1:2, rows] = turned[lanes // 2 : lanes // 2 + 1, :]


def attend(start_col, q, k, v):
    count, width = q.shape
    pairs = HEADS // 2
    lanes = width // pairs
    col = pl.BlockSpec((count, lanes), lambda p: (0, p))
    return pl.pallas_call(
        attend_kernel,
        grid=(pairs,),
        in_specs=[whole((count, 1)), col, col, col],
        out_specs=[col, pl.BlockSpec((1, 8, count), lambda p: (p, 0, 0))],
        out_shape=[
            jax.ShapeDtypeStruct((count, width), BF16),
            jax.ShapeDtypeStruct((pairs, 8, count), F32),
        ],
        scratch_shapes=[
            pltpu.VMEM((count, count), F32),
            pltpu.VMEM((2, count, lanes), F32),
            pltpu.VMEM((2, count, lanes), F32),
        ],
        compiler_params=params(),
        cost_estimate=cost(8 * count * count * width, 8 * count * width, HEADS * count * count // 2),
        name="attend",
    )(start_col, q, k, v)


def leave_kernel(
    mixed, wo, bo, tokens, live_col, pos_col, out, residual, mixed_in, wo_in, tokens_in, kept, low, sems
):
    copies = Copies(sems)
    count = kept.shape[0]
    half = count // 2
    first = copies.start(wo, wo_in)
    came = []
    for r in range(0, count, half):
        rows = pl.ds(r, half)
        came.append(copies.start(mixed.at[rows], mixed_in.at[rows]))
        came.append(copies.start(tokens.at[rows], tokens_in.at[rows]))
    first.wait()
    for r in range(0, count, half):
        rows = pl.ds(r, half)
        for copy in came[:2]:
            copy.wait()
        came = came[2:]
        branch = nn(mixed_in[rows, :], wo_in[...]) + bo[...]
        kept[rows, :] = (tokens_in[rows, :].astype(F32) + live_col[rows, :] * branch).astype(BF16)
    left = [copies.start(kept, residual)]
    low[...] = nn(pick_slots(pos_col[...], count), kept[...]).astype(BF16)
    left.append(copies.start(low, out))
    for copy in left:
        copy.wait()


def leave(mixed, wo, bo, tokens, live_col, pos_col):
    count, width = mixed.shape
    rows = pos_col.shape[0]
    return pl.pallas_call(
        leave_kernel,
        grid=(1,),
        in_specs=[
            ANYWHERE,
            ANYWHERE,
            whole((1, width)),
            ANYWHERE,
            whole((count, 1)),
            whole((rows, 1)),
        ],
        out_specs=[ANYWHERE] * 2,
        out_shape=[
            jax.ShapeDtypeStruct((rows, width), BF16),
            jax.ShapeDtypeStruct((count, width), BF16),
        ],
        scratch_shapes=[
            pltpu.VMEM((count, width), BF16),
            pltpu.VMEM((width, width), BF16),
            pltpu.VMEM((count, width), BF16),
            pltpu.VMEM((count, width), BF16),
            pltpu.VMEM((rows, width), BF16),
            pltpu.SemaphoreType.DMA((7,)),
        ],
        compiler_params=params(),
        cost_estimate=cost(3 * count * width * width, 10 * count * width),
        name="leave",
    )(mixed, wo, bo, tokens, live_col, pos_col)


def pick_kernel(residual, pos_col, out):
    out[...] = nn(pick_slots(pos_col[...], residual.shape[0]), residual[...]).astype(BF16)


def pick(residual, pos_col):
    count, width = residual.shape
    rows = pos_col.shape[0]
    return pl.pallas_call(
        pick_kernel,
        grid=(1,),
        in_specs=[whole((count, width)), whole((rows, 1))],
        out_specs=whole((rows, width)),
        out_shape=jax.ShapeDtypeStruct((rows, width), BF16),
        compiler_params=params(),
        cost_estimate=cost(2 * rows * count * width, 6 * count * width),
        name="pick",
    )(residual, pos_col)


def reenter_kernel(parts, *refs):
    slots = refs[:parts]
    pos_row, live_col, wo, grad_residual, grad_proj, grad_mixed, bias_sum = refs[parts : parts + 7]
    slots_in, wo_in, low, sems = refs[parts + 7 :]
    copies = Copies(sems)
    came, start = [], 0
    for part in slots:
        size = part.shape[0]
        came.append(copies.start(part, slots_in.at[pl.ds(start, size)]))
        start += size
    wo_came = copies.start(wo, wo_in)
    for copy in came:
        copy.wait()
    count = slots_in.shape[0]
    half = count // 2
    total, left = None, []
    for r in range(0, count, half):
        rows = pl.ds(r, half)
        picked = nn(pick_rows(r, pos_row[...], half, count), slots_in[...])
        masked = live_col[rows, :] * picked
        low[0, rows, :] = picked.astype(BF16)
        low[1, rows, :] = masked.astype(BF16)
        part = jnp.sum(masked, axis=0, keepdims=True)
        total = part if total is None else total + part
        left.append(copies.start(low.at[0, rows], grad_residual.at[rows]))
        left.append(copies.start(low.at[1, rows], grad_proj.at[rows]))
    bias_sum[...] = total
    wo_came.wait()
    for r in range(0, count, half):
        rows = pl.ds(r, half)
        low[2, rows, :] = nt(low[1, rows, :], wo_in[...]).astype(BF16)
        left.append(copies.start(low.at[2, rows], grad_mixed.at[rows]))
    for copy in left:
        copy.wait()


def reenter(slots, pos_row, live_col, wo):
    parts = len(slots)
    width = slots[0].shape[1]
    count = sum(v.shape[0] for v in slots)
    out = jax.ShapeDtypeStruct((count, width), BF16)
    return pl.pallas_call(
        functools.partial(reenter_kernel, parts),
        grid=(1,),
        in_specs=[ANYWHERE] * parts + [whole((1, count)), whole((count, 1)), ANYWHERE],
        out_specs=[ANYWHERE] * 3 + [whole((1, width))],
        out_shape=[out] * 3 + [jax.ShapeDtypeStruct((1, width), F32)],
        scratch_shapes=[
            pltpu.VMEM((count, width), BF16),
            pltpu.VMEM((width, width), BF16),
            pltpu.VMEM((3, count, width), BF16),
            pltpu.SemaphoreType.DMA((parts + 7,)),
        ],
        compiler_params=params(),
        cost_estimate=cost(4 * count * width * width, 10 * count * width),
        name="reenter",
    )(*slots, pos_row, live_col, wo)


def attend_back_kernel(
    start_row, q_ref, k_ref, v_ref, o_ref, g_ref, lse_ref, out_ref, bias, sums
):
    count, lanes = q_ref.shape

    @pl.when(pl.program_id(0) == 0)
    def _():
        for j in range(count // ROWS):
            cols = pl.ds(j * ROWS, count - j * ROWS)
            shape = (ROWS, count - j * ROWS)
            kpos = lax.broadcasted_iota(jnp.int32, shape, 0) + j * ROWS
            qpos = lax.broadcasted_iota(jnp.int32, shape, 1) + j * ROWS
            keep = (kpos >= start_row[:, cols]) & (kpos <= qpos)
            bias[pl.ds(j * ROWS, ROWS), cols] = jnp.where(keep, 0.0, NEG)

    products = o_ref[...].astype(F32) * g_ref[...].astype(F32)
    high = products.astype(BF16)
    low = (products - high.astype(F32)).astype(BF16)
    sel_row = lax.broadcasted_iota(jnp.int32, (8, lanes), 0)
    sel_lane = lax.broadcasted_iota(jnp.int32, (8, lanes), 1)
    select = jnp.where(sel_row == sel_lane // (lanes // 2), 1.0, 0.0).astype(BF16)
    deltas = nt(select, high) + nt(select, low)

    queries = split_heads(q_ref[...])
    grads = split_heads(g_ref[...])
    wide = 2 * ROWS
    items = []
    for s in range(0, count, wide):
        if s + wide < count:
            items.append((s, s + wide, s + wide, count))
        items.append((s, s + ROWS, s, s + wide))
        items.append((s + ROWS, s + wide, s + ROWS, s + wide))
    work = [(item, h) for item in items for h in range(2)]

    def products_of(item, h):
        k_from, k_to, q_from, q_to = item
        return (
            nt(k_ref[k_from:k_to, :], queries[h][q_from:q_to]),
            nt(v_ref[k_from:k_to, :], grads[h][q_from:q_to]),
        )

    seen_keys, seen_queries = set(), set()

    def add(target, start, part, seen):
        for r in range(0, part.shape[0], ROWS):
            rows = pl.ds(start + r, ROWS)
            if start + r in seen:
                target[rows, :] += part[r : r + ROWS]
            else:
                target[rows, :] = part[r : r + ROWS]

    ahead = products_of(*work[0])
    for n, (item, h) in enumerate(work):
        k_from, k_to, q_from, q_to = item
        score, grad_weights = ahead
        if n + 1 < len(work):
            ahead = products_of(*work[n + 1])
        cols = slice(q_from, q_to)
        weights = jnp.exp2(score * LOG2E + bias[k_from:k_to, cols] - lse_ref[0, h : h + 1, cols])
        grad_score = (weights * (grad_weights - deltas[h : h + 1, cols])).astype(BF16)
        key = split_heads(k_ref[k_from:k_to, :])[h]
        add(sums.at[2], k_from, nn(weights.astype(BF16), grads[h][cols]), seen_keys)
        add(sums.at[1], k_from, nn(grad_score, queries[h][cols]), seen_keys)
        add(sums.at[0], q_from, tn(grad_score, key), seen_queries)
        seen_keys |= set(range(k_from, k_to, ROWS))
        seen_queries |= set(range(q_from, q_to, ROWS))
    out_ref[0] = (sums[0] * 0.125).astype(BF16)
    out_ref[1] = sums[1].astype(BF16)
    out_ref[2] = sums[2].astype(BF16)


def attend_back(start_row, q, k, v, mixed, grad_mixed, lse):
    count, width = q.shape
    pairs = HEADS // 2
    lanes = width // pairs
    col = pl.BlockSpec((count, lanes), lambda p: (0, p))
    return pl.pallas_call(
        attend_back_kernel,
        grid=(pairs,),
        in_specs=[whole((1, count))]
        + [col] * 5
        + [pl.BlockSpec((1, 8, count), lambda p: (p, 0, 0))],
        out_specs=pl.BlockSpec((3, count, lanes), lambda p: (0, 0, p)),
        out_shape=jax.ShapeDtypeStruct((3, count, width), BF16),
        scratch_shapes=[pltpu.VMEM((count, count), F32), pltpu.VMEM((3, count, lanes), F32)],
        compiler_params=params(),
        cost_estimate=cost(20 * count * count * width, 16 * count * width, HEADS * count * count // 2),
        name="attend_back",
    )(start_row, q, k, v, mixed, grad_mixed, lse)


def finish_kernel(grads, wq, wk, wv, tokens, grad_residual, gain, pos_col, others, *refs):
    outs, sums = refs[:-8], refs[-8]
    grads_in, weights, tokens_in, residual_in, total, kept, sems = refs[-7:]
    copies = Copies(sems)
    came = []
    for n, w in enumerate((wq, wk, wv)):
        came.append((copies.start(grads.at[n], grads_in.at[n]), copies.start(w, weights.at[n])))
    rest = [copies.start(tokens, tokens_in), copies.start(grad_residual, residual_in)]
    count = kept.shape[0]
    half = count // 2
    for n in range(3):
        for copy in came[n]:
            copy.wait()
        for r in range(0, count, half):
            rows = pl.ds(r, half)
            part = nt(grads_in[n, rows, :], weights[n])
            if n == 0:
                total[rows, :] = part
            else:
                total[rows, :] += part
    for copy in rest:
        copy.wait()
    sums[...] = others[...]
    for r in range(0, count, ROWS):
        rows = pl.ds(r, ROWS)
        grad = total[rows, :]
        normal, root = norm_parts(tokens_in[rows, :].astype(F32))
        kept[rows, :] = (
            residual_in[rows, :].astype(F32) + norm_grad(grad, normal, root, gain[...])
        ).astype(BF16)
        sums[0:1, :] += jnp.sum(grad * normal, axis=0, keepdims=True)
        sums[1:2, :] += jnp.sum(grad, axis=0, keepdims=True)
        sums[2:3, :] += jnp.sum(grads_in[0, rows, :].astype(F32), axis=0, keepdims=True)
        sums[3:4, :] += jnp.sum(grads_in[2, rows, :].astype(F32), axis=0, keepdims=True)
    left = []
    for r in range(0, count, half):
        rows = pl.ds(r, half)
        chosen = pick_slots(pos_col[rows, :], count)
        residual_in[rows, :] = nn(chosen, kept[...]).astype(BF16)
    start = 0
    for out in outs:
        rows = out.shape[0]
        left.append(copies.start(residual_in.at[pl.ds(start, rows)], out))
        start += rows
    for copy in left:
        copy.wait()


def finish(sizes, grads, weights, tokens, grad_residual, gain, pos_col, others):
    count, width = tokens.shape
    return pl.pallas_call(
        finish_kernel,
        grid=(1,),
        in_specs=[ANYWHERE] * 6 + [whole((1, width)), whole((count, 1)), whole((8, width))],
        out_specs=[ANYWHERE] * len(sizes) + [whole((8, width))],
        out_shape=[jax.ShapeDtypeStruct((rows, width), BF16) for rows in sizes]
        + [jax.ShapeDtypeStruct((8, width), F32)],
        scratch_shapes=[
            pltpu.VMEM((3, count, width), BF16),
            pltpu.VMEM((3, width, width), BF16),
            pltpu.VMEM((count, width), BF16),
            pltpu.VMEM((count, width), BF16),
            pltpu.VMEM((count, width), F32),
            pltpu.VMEM((count, width), BF16),
            pltpu.SemaphoreType.DMA((8 + len(sizes),)),
        ],
        compiler_params=params(),
        cost_estimate=cost(8 * count * width * width, 20 * count * width),
        name="finish",
    )(grads, *weights, tokens, grad_residual, gain, pos_col, others)


GELU_ROOT = math.sqrt(2.0 / math.pi)
GELU_CUBE = 0.044715
STEP = 1024


def shard_of(step):
    return (step % 2) * 2 + step // 2


def expert_kernel(parts, device, source, *refs):
    it = iter(refs)
    take = lambda n: [next(it) for _ in range(n)]
    slots, cots, lives = take(3)
    up, down, up_bias, gain, offset = take(5)
    grads = take(max(len(parts), 1))
    mine, theirs, sums, up_sums = take(4)
    ffn_in, branch, grad_sum, low = take(4)
    rows, model = slots.shape
    t = pl.program_id(0)

    @pl.when(t == 0)
    def _():
        normal, _ = norm_parts(slots[...].astype(F32))
        ffn_in[...] = (normal * gain[...] + offset[...]).astype(BF16)
        cot = cots[...].reshape(rows, model).astype(F32)
        branch[...] = (lives[...].reshape(rows, 1) * cot).astype(BF16)
        theirs[0] = ffn_in[...]
        theirs[1] = branch[...]
        grad_sum[...] = jnp.zeros_like(grad_sum)

    @pl.when(t == 2)
    def _():
        mine[0] = ffn_in[...]
        mine[1] = branch[...]

    width = up.shape[2]

    def compute(out):
        for c in range(0, width, STEP):
            cols = pl.ds(c, STEP)
            pre = nn(ffn_in[...], up[0, :, cols]) + up_bias[0, :, cols]
            square = pre * pre
            tanh = jnp.tanh(pre * (GELU_ROOT + (GELU_ROOT * GELU_CUBE) * square))
            half = 0.5 * (1.0 + tanh)
            slope = half + (0.5 * pre) * (1.0 - tanh * tanh) * (
                GELU_ROOT + (3.0 * GELU_ROOT * GELU_CUBE) * square
            )
            out[0, :, cols] = (pre * half).astype(BF16)
            grad_pre = (nt(branch[...], down[0, cols, :]) * slope).astype(BF16)
            out[1, :, cols] = grad_pre
            up_sums[0, :, cols] = jnp.sum(grad_pre.astype(F32), axis=0, keepdims=True)
            grad_sum[...] += nt(grad_pre, up[0, :, cols])

    @pl.when(t < 2)
    def _():
        compute(mine)

    @pl.when(t >= 2)
    def _():
        compute(theirs)

    @pl.when(t == 3)
    def _():
        routed = slots[...].astype(F32)
        normal, root = norm_parts(routed)
        grad = grad_sum[...]
        cot = cots[...].reshape(rows, model).astype(F32)
        grad_routed = (cot + norm_grad(grad, normal, root, gain[...])).astype(BF16)
        if not parts:
            grads[0][...] = grad_routed
        else:
            low[...] = grad_routed
            short, n = rows // sum(parts), 0
            for part, blocks in zip(grads, parts):
                for j in range(blocks):
                    place = pl.multiple_of(source[n] * short, short)
                    part[j * short : (j + 1) * short, :] = low[pl.ds(place, short), :]
                    n += 1
        sums[...] = jnp.zeros_like(sums)
        sums[0:1, :] = jnp.sum(grad * normal, axis=0, keepdims=True)
        sums[1:2, :] = jnp.sum(grad, axis=0, keepdims=True)
        sums[2:3, :] = jnp.sum(branch[...].astype(F32), axis=0, keepdims=True)


def expert_chunk(chunk, parts, device, source, slots, cot, live, ups, downs, up_bias, gain, offset):
    rows, width = slots.shape
    groups, piece, _ = cot.shape
    short = rows // groups
    sizes = [short * n for n in parts] or [rows]
    part = ups.shape[2]
    assert part == width and ups.shape[0] == 4
    block = pl.BlockSpec((groups, short, width), lambda t, *_: (0, chunk, 0))
    packet = jax.ShapeDtypeStruct((6, rows, width), BF16)
    weights = pl.BlockSpec((1, width, part), lambda t, device, *_: (shard_of(t) ^ device[0], 0, 0))
    bias = pl.BlockSpec((1, 1, part), lambda t, device, *_: (shard_of(t) ^ device[0], 0, 0))
    return pl.pallas_call(
        functools.partial(expert_kernel, parts),
        grid_spec=pltpu.PrefetchScalarGridSpec(
            num_scalar_prefetch=2,
            grid=(4,),
            in_specs=[
                whole((rows, width)),
                block,
                pl.BlockSpec((groups, short, 1), lambda t, *_: (0, chunk, 0)),
            ]
            + [weights, weights, bias, whole((1, width)), whole((1, width))],
            out_specs=[whole((size, width)) for size in sizes]
            + [
                pl.BlockSpec((2, rows, width), lambda t, *_: (jnp.minimum(t, 2), 0, 0)),
                pl.BlockSpec((2, rows, width), lambda t, *_: (jnp.where(t < 2, 2, t - 2), 0, 0)),
                whole((8, width)),
                bias,
            ],
            scratch_shapes=[
                pltpu.VMEM((rows, width), BF16),
                pltpu.VMEM((rows, width), BF16),
                pltpu.VMEM((rows, width), F32),
                pltpu.VMEM((rows, width), BF16),
            ],
        ),
        out_shape=[jax.ShapeDtypeStruct((size, width), BF16) for size in sizes]
        + [
            packet,
            packet,
            jax.ShapeDtypeStruct((8, width), F32),
            jax.ShapeDtypeStruct((4, 1, part), F32),
        ],
        compiler_params=params(),
        cost_estimate=cost(24 * rows * width * part, 16 * width * part, 4 * rows * part),
        name="expert_chunk",
    )(device, source, slots, cot, live, ups, downs, up_bias, gain, offset)


def expert_out_kernel(chunks, device, *refs):
    mine, theirs, slots = refs[:chunks], refs[chunks : 2 * chunks], refs[2 * chunks : 3 * chunks]
    down, bias, live, out, total = refs[3 * chunks :]
    t = pl.program_id(0)
    rows = slots[0].shape[0]
    for n in range(4):

        @pl.when(t == n)
        def _(n=n):
            for c in range(chunks):
                part = nn((mine if n < 2 else theirs)[c][0], down[0])
                if n == 0:
                    total[c * rows : (c + 1) * rows, :] = part
                else:
                    total[c * rows : (c + 1) * rows, :] += part

    @pl.when(t == 3)
    def _():
        groups, piece, width = out.shape
        short = piece // chunks
        for c in range(chunks):
            branch = total[c * rows : (c + 1) * rows, :] + bias[...]
            keep = live[:, c * short : (c + 1) * short, :].reshape(rows, 1)
            value = (slots[c][...].astype(F32) + keep * branch).astype(BF16)
            out[:, c * short : (c + 1) * short, :] = value.reshape(groups, short, width)


def expert_out(device, mine, theirs, slots, downs, bias, live):
    chunks = len(slots)
    rows, width = slots[0].shape
    part = downs.shape[1]
    groups, piece, _ = live.shape
    act = lambda index: pl.BlockSpec((1, rows, part), index)
    return pl.pallas_call(
        functools.partial(expert_out_kernel, chunks),
        grid_spec=pltpu.PrefetchScalarGridSpec(
            num_scalar_prefetch=1,
            grid=(4,),
            in_specs=[act(lambda t, *_: (2 * jnp.minimum(t, 1), 0, 0))] * chunks
            + [act(lambda t, *_: (2 * jnp.maximum(t - 2, 0), 0, 0))] * chunks
            + [whole((rows, width))] * chunks
            + [pl.BlockSpec((1, part, width), lambda t, device: (shard_of(t) ^ device[0], 0, 0))]
            + [whole((1, width)), whole((groups, piece, 1))],
            out_specs=whole((groups, piece, width)),
            scratch_shapes=[pltpu.VMEM((chunks * rows, width), F32)],
        ),
        out_shape=jax.ShapeDtypeStruct((groups, piece, width), BF16),
        compiler_params=params(),
        cost_estimate=cost(8 * chunks * rows * part * width, 32 * rows * width),
        name="expert_out",
    )(device, *mine, *theirs, *slots, downs, bias, live)


CUTS = ((224, 800), (304, 400, 320))


def expert_grads_kernel(count, shard, added, *refs):
    packets, parts, outs = refs[:count], refs[count : count + added], refs[count + added : -7]
    act, branch, ffn_in, pre, earlier, full, sems = refs[-7:]
    copies = Copies(sems)
    rows = packets[0].shape[1]

    def fetch(slot, target):
        return [copies.start(p.at[slot], target.at[pl.ds(n * rows, rows)]) for n, p in enumerate(packets)]

    first = fetch(shard, act) + fetch(5, branch)
    before = [copies.start(p.at[0], earlier.at[m]) for m, p in enumerate(parts)]
    second = fetch(4, ffn_in) + fetch(shard + 1, pre)
    left = []
    for m, (came, one, two) in enumerate(((first, act, branch), (second, ffn_in, pre))):
        for copy in came:
            copy.wait()
        total = tn(one[...], two[...])
        if added:
            before[m].wait()
            total = total + earlier[m]
        full[m] = total.astype(full.dtype)
        if not added:
            left.append(copies.start(full.at[m], outs[m].at[0]))
            continue
        start, skip = 0, sum(len(cuts) for cuts in CUTS[:m])
        for n, cut in enumerate(CUTS[m]):
            left.append(copies.start(full.at[m, pl.ds(start, cut)], outs[skip + n]))
            start += cut
    for copy in left:
        copy.wait()


def expert_grads(far, packets, parts=()):
    _, rows, width = packets[0].shape
    count, added = len(packets), len(parts)
    assert sum(CUTS[0]) == sum(CUTS[1]) == width
    if added:
        shapes = [jax.ShapeDtypeStruct((c, width), BF16) for cuts in CUTS for c in cuts]
    else:
        shapes = [jax.ShapeDtypeStruct((1, width, width), F32)] * 2
    return pl.pallas_call(
        functools.partial(expert_grads_kernel, count, 2 if far else 0, added),
        grid=(1,),
        in_specs=[ANYWHERE] * (count + added),
        out_specs=[ANYWHERE] * len(shapes),
        out_shape=shapes,
        scratch_shapes=[pltpu.VMEM((count * rows, width), BF16)] * 4
        + [
            pltpu.VMEM((2, width, width) if added else (2, 16, 128), F32),
            pltpu.VMEM((2, width, width), BF16 if added else F32),
            pltpu.SemaphoreType.DMA((4 * count + added + len(shapes),)),
        ],
        compiler_params=params(),
        cost_estimate=cost(4 * count * rows * width * width, 20 * width * width),
        name="far_rest" if added else ("far_part" if far else "near_grads"),
    )(*packets, *parts)


def shared_grads_kernel(
    streams, blocks, codes, normed, mixed, token_grads, grad_proj, keep, send,
    left_in, right_in, total, low, sems
):
    copies = Copies(sems)
    number = right_in.shape[0]
    came = [[copies.start(normed, left_in.at[0]), copies.start(token_grads.at[0], right_in.at[0])]]
    came += [[copies.start(token_grads.at[m], right_in.at[m])] for m in range(1, number - 1)]
    came.append([copies.start(mixed, left_in.at[1]), copies.start(grad_proj, right_in.at[number - 1])])
    half = blocks // 2
    rows = total.shape[1]
    size = rows // half
    first = codes[0] // half
    left = []
    for m in range(number):
        for copy in came[m]:
            copy.wait()
        for h, target in enumerate((keep, send)):
            n = (2 * m + h) % 2
            side = pl.ds(pl.multiple_of((first ^ h) * rows, rows), rows)
            total[n] = tn(left_in[0 if m < number - 1 else 1, :, side], right_in[m])
            for j in range(half):
                code = codes[(j // (half // streams)) % streams] % half
                place = pl.multiple_of((code ^ j) * size, size)
                low[m, h, pl.ds(j * size, size), :] = total[n, pl.ds(place, size), :].astype(BF16)
            left.append(copies.start(low.at[m, h], target.at[m]))
    for copy in left:
        copy.wait()


def shared_grads(layout, normed, mixed, token_grads, grad_proj):
    count, width = normed.shape
    number = token_grads.shape[0] + 1
    half = width // 2
    return pl.pallas_call(
        functools.partial(shared_grads_kernel, layout.streams, layout.blocks),
        grid_spec=pltpu.PrefetchScalarGridSpec(
            num_scalar_prefetch=1,
            grid=(1,),
            in_specs=[ANYWHERE] * 4,
            out_specs=[ANYWHERE] * 2,
            scratch_shapes=[
                pltpu.VMEM((2, count, width), BF16),
                pltpu.VMEM((number, count, width), BF16),
                pltpu.VMEM((2, half, width), F32),
                pltpu.VMEM((number, 2, half, width), BF16),
                pltpu.SemaphoreType.DMA((3 * number + 2,)),
            ],
        ),
        out_shape=[jax.ShapeDtypeStruct((number, half, width), BF16)] * 2,
        compiler_params=params(),
        cost_estimate=cost(2 * number * count * width * width, 6 * number * width * width),
        name="shared_grads",
    )(layout.codes, normed, mixed, token_grads, grad_proj)


def unmix_kernel(group, parts, codes, half_place, source, pieces, *refs):
    rows_in, came_in, full, sems = refs[-4:]
    number, half, _ = came_in.shape
    outs = refs[-4 - number - min(parts, 1) : -4]
    copies = Copies(sems)
    came = [copies.start(pieces.at[m], came_in.at[m]) for m in range(number)]
    joined, left = [], []
    for r in range(parts):
        size = refs[r].shape[0]
        place = pl.multiple_of(source[r] * size, size)
        joined.append(copies.start(refs[r], rows_in.at[pl.ds(place, size)]))
    rows = half // 4
    size = rows // group
    for m in range(number):
        came[m].wait()
        for n in range(4):
            code = codes[n // 2]
            low = code % group
            block = n ^ ((code // group) % 2)
            for j in range(group):
                place = pl.multiple_of(block * rows + (low ^ j) * size, size)
                start = n * rows + j * size
                full[m, pl.ds(place, size), :] = came_in[m, start : start + size, :].astype(F32)
        target = outs[m].at[pl.ds(pl.multiple_of(half_place[0] * half, half), half)]
        left.append(copies.start(full.at[m], target))
        if m == 0 and parts:
            for copy in joined:
                copy.wait()
            left.append(copies.start(rows_in, outs[number]))
    for copy in left:
        copy.wait()


def unmix(layout, half_place, pieces, before=None, source=None, joined=()):
    number, rows, width = pieces.shape
    earlier = [] if before is None else list(before)
    parts = len(joined)
    source = half_place if source is None else source
    total = sum(v.shape[0] for v in joined)
    return pl.pallas_call(
        functools.partial(unmix_kernel, layout.blocks // 8, parts),
        grid_spec=pltpu.PrefetchScalarGridSpec(
            num_scalar_prefetch=3,
            grid=(1,),
            in_specs=[ANYWHERE] * (1 + parts + len(earlier)),
            out_specs=[ANYWHERE] * (number + min(parts, 1)),
            scratch_shapes=[
                pltpu.VMEM((max(total, 16), width), BF16),
                pltpu.VMEM((number, rows, width), BF16),
                pltpu.VMEM((number, rows, width), F32),
                pltpu.SemaphoreType.DMA((2 * number + parts + 1,)),
            ],
        ),
        out_shape=[jax.ShapeDtypeStruct((2 * rows, width), F32)] * number
        + [jax.ShapeDtypeStruct((total, width), BF16)] * min(parts, 1),
        input_output_aliases={4 + parts + m: m for m in range(len(earlier))},
        compiler_params=params(),
        cost_estimate=cost(number * rows * width, 6 * number * rows * width),
        name="unmix",
    )(layout.codes, half_place, source, pieces, *joined, *earlier)


def swap(values, step):
    axis, size, bit = step
    return lax.ppermute(values, axis, [(i, i ^ bit) for i in range(size)])


def exchange(values):
    return lax.all_to_all(values, "expert", split_axis=0, concat_axis=0, tiled=True)


def turn(values, size, by):
    return lax.ppermute(values, "expert", [(i, (i + by) % size) for i in range(size)])


def bits_of(size):
    return [1 << b for b in range(size.bit_length() - 1)]


def add_low(left, right):
    return (left.astype(F32) + right.astype(F32)).astype(BF16)


def tie(*values):
    return lax.optimization_barrier(values)


class SharedSum:
    streams = 2
    least = 16

    def __init__(self, n_expert, n_dp, rows):
        steps = [("dp", n_dp, b) for b in bits_of(n_dp)] + [
            ("expert", n_expert, b) for b in bits_of(n_expert)
        ]
        steps.sort(key=lambda s: (s[2], s[0]))
        self.steps = steps
        self.first, one, two, *rest = steps
        self.pair = ((two, one), (one, two))
        self.rest, self.left = rest[:2], rest[2:]
        self.blocks = 2 * self.streams * 4 * 4
        assert rows // self.blocks >= self.least and self.rest[0][0] == self.rest[1][0]
        self.codes = jnp.stack([self.code([self.first, None, *pair, *self.rest]) for pair in self.pair])

    def code(self, steps):
        total = jnp.int32(0)
        for step in steps:
            mine = 0 if step is None else (lax.axis_index(step[0]) // step[2]) % 2
            total = total * 2 + mine
        return total.astype(jnp.int32)

    @staticmethod
    def halve(values, step, axis):
        middle = values.shape[axis] // 2
        keep = lax.slice_in_dim(values, 0, middle, axis=axis)
        send = lax.slice_in_dim(values, middle, 2 * middle, axis=axis)
        return add_low(keep, swap(send, step))

    @staticmethod
    def double(values, step, axis):
        return jnp.concatenate([values, swap(values, step)], axis=axis)

    def reduce_first(self, keep, send):
        came = swap(send, self.first)
        size = keep.shape[1] // 4
        quarter = lambda v, n: lax.slice_in_dim(v, n * size, (n + 1) * size, axis=1)
        return [add_low(quarter(keep, n), quarter(came, n)) for n in range(4)]

    def reduce_pair_first(self, quarters):
        return [
            add_low(quarters[2 * n], swap(quarters[2 * n + 1], self.pair[n][0]))
            for n in range(self.streams)
        ]

    def reduce_pair(self, parts, n):
        return [self.halve(part, pair[n], 1) for part, pair in zip(parts, self.pair)]

    def partners(self, total, j):
        (axis, size, high), (_, _, low) = self.rest
        return swap(total, (axis, size, (j // 2) * high + (j % 2) * low))

    def reduce_rest(self, total):
        size = total.shape[2] // 4
        piece = lambda j: total[:, :, j * size : (j + 1) * size]
        sum_all = piece(0).astype(F32)
        for j in range(1, 4):
            sum_all = sum_all + self.partners(piece(j), j).astype(F32)
        total = sum_all.astype(BF16)
        for step in self.left:
            total = add_low(total, swap(total, step))
        return total

    def gather_rest(self, total):
        return jnp.concatenate([total] + [self.partners(total, j) for j in range(1, 4)], axis=2)

    def gather_pair(self, parts, n):
        return [self.double(part, pair[n], 1) for part, pair in zip(parts, self.pair)]

    def gather_first(self, parts):
        total = jnp.concatenate(parts, axis=1)
        mine = ((lax.axis_index(self.first[0]) // self.first[2]) % 2).astype(jnp.int32).reshape(1)
        return (mine, total), (1 - mine, swap(total, self.first))


def small_sum(values, steps):
    for step in steps:
        if step[0] == "dp":
            values = values + swap(values, step)
        else:
            part = values[:8]
            values = jnp.concatenate([part + swap(part, step), values[8:]], axis=0)
    return values


CHUNKS = 2


def per_device(
    n_expert,
    n_dp,
    block_in,
    seq_lengths,
    slot_position,
    first_gain,
    first_bias,
    query_weight,
    query_bias,
    key_weight,
    value_weight,
    value_bias,
    out_weight,
    out_bias,
    second_gain,
    second_bias,
    expert_up,
    expert_up_bias,
    expert_down,
    expert_down_bias,
    block_cot,
):
    count, width = block_in.shape
    piece = count // n_expert
    row = lambda v: v.reshape(1, -1)
    device = lax.axis_index("dp")
    part = expert_up.shape[2]
    dp_steps = [("dp", n_dp, b) for b in bits_of(n_dp)]
    all_steps = dp_steps + [("expert", n_expert, b) for b in bits_of(n_expert)]

    core, far = dp_steps
    ups = lax.all_gather(expert_up[0], "dp", axis=0)
    downs = lax.all_gather(expert_down[0], "dp", axis=0)
    arrived = exchange(block_in)

    position = slot_position[0]
    ends = jnp.cumsum(seq_lengths[0])
    total_live = ends[-1]
    ids = jnp.arange(count, dtype=jnp.int32)
    live = ids < total_live
    begin = jnp.max(jnp.where(ends[None, :] <= ids[:, None], ends[None, :], 0), axis=1)
    begin = jnp.where(live, begin, ids).astype(jnp.int32)
    live_col = live.astype(F32).reshape(count, 1)
    in_chunks = position.reshape(n_expert, CHUNKS, -1).transpose(1, 0, 2).reshape(count)
    slot_live = (position < total_live).astype(F32).reshape(n_expert, piece)
    start_row, start_col = begin.reshape(1, count), begin.reshape(count, 1)
    pos_row, chunk_col = position.reshape(1, count), in_chunks.reshape(count, 1)
    shared = SharedSum(n_expert, n_dp, width)
    expert = lax.axis_index("expert")
    codes = jnp.concatenate([jnp.arange(xs, n_expert, 2, dtype=jnp.int32) for xs in range(2)])
    partners = (expert ^ codes).astype(jnp.int32)
    leave_col = jnp.take(position.reshape(n_expert, piece), partners, axis=0).reshape(count, 1)
    side = n_expert // 2
    back_codes = [0] + [2 * j for j in range(2, side)] + [2, 3, 1] + [2 * j + 1 for j in range(2, side)]
    back = (expert ^ jnp.array(back_codes, jnp.int32)).astype(jnp.int32)
    last_slots = jnp.take(position.reshape(n_expert, CHUNKS, -1)[:, -1], back, axis=0)
    came_row = jnp.concatenate([in_chunks[: count - count // CHUNKS], last_slots.reshape(-1)])
    came_row = came_row.reshape(1, count)
    leave_col, partners, back, came_row = tie(leave_col, partners, back, came_row)
    arrived, start_row, start_col, pos_row, chunk_col, live_col, shared.codes = tie(
        arrived, start_row, start_col, pos_row, chunk_col, live_col, shared.codes
    )
    route_live = exchange(slot_live).reshape(n_expert, piece, 1)

    tokens, normed, query, key, value = entry(
        arrived, pos_row, row(first_gain), row(first_bias), query_weight,
        row(query_bias), key_weight, value_weight, row(value_bias),
    )
    mixed, lse = attend(start_col, query, key, value)
    some = count // CHUNKS
    first, residual = leave(
        mixed, out_weight, row(out_bias), tokens, live_col, chunk_col[:some]
    )
    sent = [first] + [
        pick(residual, chunk_col[c * some : (c + 1) * some]) for c in range(1, CHUNKS)
    ]
    routed = [exchange(sent[0])]

    blocks = lambda v: v.reshape(n_expert, piece, width)
    place = device.astype(jnp.int32).reshape(1)
    up_bias = expert_up_bias[0].reshape(n_dp, 1, part)
    grads, mine, theirs, got, sums, up_sums = ([None] * CHUNKS for _ in range(6))
    returned = []
    to_partner = lambda v, j: swap(v, ("expert", n_expert, 2 * j))
    for c in range(CHUNKS):
        last = c + 1 == CHUNKS
        *grads[c], mine[c], theirs[c], sums[c], up_sums[c] = expert_chunk(
            c, (1,) * (side - 1) + (2, side - 1) if last else (), place, back, routed[c],
            blocks(block_cot), route_live, ups, downs, up_bias, row(second_gain), row(second_bias),
        )
        if c > 0:
            returned.append(exchange(grads[c - 1][0]))
            got[c - 1] = swap(theirs[c - 1], core)
            returned[-1], got[c - 1], grads[c], mine[c], theirs[c] = tie(
                returned[-1], got[c - 1], grads[c], mine[c], theirs[c]
            )
        if not last:
            routed.append(exchange(sent[c + 1]))
            routed[c + 1], grads[c], mine[c], theirs[c] = tie(
                routed[c + 1], grads[c], mine[c], theirs[c]
            )
    across = lambda v: swap(v, ("expert", n_expert, 1))
    own, *stay, pair, cross = grads[-1]
    got[-1] = swap(theirs[-1], core)
    pair, cross = to_partner(pair, 1), across(cross)
    stay = [to_partner(v, j) for j, v in enumerate(stay, 2)]
    parts = list(expert_grads(True, [*mine, *got[:-1]]))
    pair, cross, parts = tie(pair, cross, parts)
    short = own.shape[0]
    cut = lambda v: [v[n * short : (n + 1) * short] for n in range(v.shape[0] // short)]
    near_pair, far_pair = cut(pair)
    crossed, *rest = cut(cross)
    rest = [to_partner(v, j) for j, v in enumerate(rest, 2)]
    returned += [own, *stay, near_pair, across(far_pair), crossed, *rest]

    fars = list(expert_grads(True, got[-1:], parts))
    sums, up_sums = sum(sums), sum(up_sums)
    empty = jnp.zeros((8, width), F32)
    biases = jnp.concatenate([up_sums.reshape(-1, width), sums[2:3], empty[: 7 - n_dp]], axis=0)

    def over_y(n):
        fars[n] = swap(fars[n], far)

    returned, fars, biases = tie(returned, fars, biases)
    packets = [*mine, *got]
    grad_residual, grad_proj, grad_mixed, out_bias_sum = reenter(
        returned, came_row, live_col, out_weight
    )
    over_y(0)
    grad_mixed, fars = tie(grad_mixed, fars)
    unstack = lambda v: [v[:, n] for n in range(shared.streams)]

    over_y(1)
    token_grads = attend_back(
        start_row, query, key, value, mixed, grad_mixed, lse
    )
    token_grads, fars = tie(token_grads, fars)

    over_y(2)
    halves = shared_grads(shared, normed, mixed, token_grads, grad_proj)
    token_grads, halves, fars, out_bias_sum = tie(token_grads, halves, fars, out_bias_sum)

    others = jnp.concatenate([empty[:4], out_bias_sum, sums[0:2], empty[:1]], axis=0)
    total = shared.reduce_first(*halves)
    token_grads, total, others = tie(token_grads, total, others)

    *leaving, token_sums = finish(
        [piece] * side + [piece * side // 2] * 2, token_grads, [query_weight, key_weight, value_weight],
        tokens, grad_residual, row(first_gain), leave_col, others,
    )
    total = shared.reduce_pair_first(total)
    leaving, token_sums, total = tie(leaving, token_sums, total)

    *stay, cross, cross_rest = leaving
    early = range(1, 1 + (2 * side - 2 + 2) // 3)
    late = range(early.stop, side)
    small_steps = list(shared.steps)
    small_step = lambda v: small_sum(v, [small_steps.pop(0)])
    small = jnp.concatenate([token_sums, biases], axis=0)
    for j in early:
        stay[j] = to_partner(stay[j], j)
    small = small_step(small)
    total = jnp.stack(shared.reduce_pair(total, 1), axis=1)
    total, small, fars, mine, stay, cross, cross_rest = tie(
        total, small, fars, mine, stay, cross, cross_rest
    )

    over_y(3)
    cross = swap(cross, ("expert", n_expert, 1))
    block_out = expert_out(place, mine, theirs, routed, downs, row(expert_down_bias[0]), route_live)
    total = shared.reduce_rest(total)
    total, small, block_out, packets, fars, cross, cross_rest = tie(
        total, small, block_out, packets, fars, cross, cross_rest
    )

    over_y(4)
    total = unstack(shared.gather_rest(total))
    near = list(expert_grads(False, packets))
    cross_rest = swap(cross_rest, ("expert", n_expert, 1))
    total, small, near, fars, stay, cross, cross_rest = tie(
        total, small, near, fars, stay, cross, cross_rest
    )
    across = [v[j * piece : (j + 1) * piece] for v in (cross, cross_rest) for j in range(side // 2)]

    for j in late:
        stay[j] = to_partner(stay[j], j)
    small = small_step(small_step(small))
    total = shared.gather_pair(total, 1)
    grad_up = near[1] + jnp.concatenate(fars[2:], axis=0).astype(F32)[None]
    total, small, stay, across, grad_up, near[0] = tie(total, small, stay, across, grad_up, near[0])

    middle = (side + 1) // 2 + 1
    for j in range(1, middle):
        across[j] = to_partner(across[j], j)
    total = shared.gather_pair(total, 0)
    small = small_sum(small, small_steps)
    grad_down = near[0] + jnp.concatenate(fars[:2], axis=0).astype(F32)[None]
    total, small, across, grad_down = tie(total, small, across, grad_down)

    for j in range(middle, side):
        across[j] = to_partner(across[j], j)
    nearest, farthest = shared.gather_first(total)
    grads = unmix(shared, *nearest)
    grads, farthest = tie(grads, farthest)
    grad_query_weight, grad_key_weight, grad_value_weight, grad_out_weight, input_grad = unmix(
        shared, *farthest, grads, partners, [*stay, *across]
    )
    share = width // n_dp
    grad_up_bias = lax.dynamic_slice_in_dim(small, 8 + device, 1, 0)
    grad_down_bias = lax.dynamic_slice_in_dim(small[8 + n_dp : 9 + n_dp], device * share, share, 1)
    return (
        block_out.reshape(count, width),
        input_grad,
        small[0],
        small[1],
        grad_query_weight,
        small[2],
        grad_key_weight,
        grad_value_weight,
        small[3],
        grad_out_weight,
        small[4],
        small[5],
        small[6],
        grad_up,
        grad_up_bias,
        grad_down,
        grad_down_bias,
    )


def solution(mesh):
    both = P(("expert", "dp"), None)
    return jax.shard_map(
        functools.partial(per_device, mesh.shape["expert"], mesh.shape["dp"]),
        mesh=mesh,
        in_specs=(both,) * 3
        + (P(),) * 11
        + (P("expert", None, "dp"), P("expert", None), P("expert", "dp", None), P("expert", None), both),
        out_specs=(both,) * 2
        + (P(),) * 11
        + (P("expert", None, "dp"), P("expert", "dp"), P("expert", "dp", None), P("expert", "dp")),
        check_vma=False,
    )
```

```python
import functools
import math

import jax
import jax.numpy as jnp
from jax import lax
from jax.experimental import pallas as pl
from jax.experimental.pallas import tpu as pltpu
from jax.sharding import PartitionSpec as P

HEADS = 16
EPS = 1e-05
NEG = -1e30
LOG2E = math.log2(math.e)
F32 = jnp.float32
BF16 = jnp.bfloat16
VMEM_LIMIT = 60 * 1024 * 1024
ROWS = 256


def nn(a, b):
    return lax.dot_general(a, b, (((1,), (0,)), ((), ())), preferred_element_type=F32)


def nt(a, b):
    return lax.dot_general(a, b, (((1,), (1,)), ((), ())), preferred_element_type=F32)


def tn(a, b):
    return lax.dot_general(a, b, (((0,), (0,)), ((), ())), preferred_element_type=F32)


def params(**more):
    return pltpu.CompilerParams(vmem_limit_bytes=VMEM_LIMIT, **more)


def cost(flops, bytes_accessed, transcendentals=0):
    return pl.CostEstimate(
        flops=int(flops), bytes_accessed=int(bytes_accessed), transcendentals=int(transcendentals)
    )


def whole(shape):
    return pl.BlockSpec(shape, lambda *_: (0,) * len(shape))


def rows_of(block, width):
    return pl.BlockSpec((block, width), lambda i, *_: (i, 0))


def norm_parts(values):
    mean = jnp.mean(values, axis=-1, keepdims=True)
    center = values - mean
    variance = jnp.mean(center * center, axis=-1, keepdims=True)
    root = lax.rsqrt(variance + EPS)
    return center * root, root


def norm_grad(grad, normal, root, gain):
    scaled = grad * gain
    mean_plain = jnp.mean(scaled, axis=-1, keepdims=True)
    mean_normal = jnp.mean(scaled * normal, axis=-1, keepdims=True)
    return root * (scaled - mean_plain - normal * mean_normal)


def pick_rows(first_row, pos_row, rows, count):
    ids = lax.broadcasted_iota(jnp.int32, (rows, count), 0) + first_row
    return jnp.where(ids == pos_row, 1.0, 0.0).astype(BF16)


def pick_slots(pos_col, count):
    ids = lax.broadcasted_iota(jnp.int32, (pos_col.shape[0], count), 1)
    return jnp.where(ids == pos_col, 1.0, 0.0).astype(BF16)


ANYWHERE = pl.BlockSpec(memory_space=pl.ANY)


class Copies:
    def __init__(self, sems):
        self.sems, self.used = sems, 0

    def start(self, source, target):
        copy = pltpu.make_async_copy(source, target, self.sems.at[self.used])
        self.used += 1
        copy.start()
        return copy


def entry_kernel(
    slots, pos_row, gain, offset, wq, bq, wk, wv, bv, tokens, normed, q, k, v,
    slots_in, weights, low_tokens, low_normed, low_out, sems
):
    copies = Copies(sems)
    count = slots.shape[0]
    half = count // 2
    came = copies.start(slots, slots_in)
    weights_came = [copies.start(w, weights.at[n]) for n, w in enumerate((wq, wk, wv))]
    came.wait()
    left = []
    for r in range(0, count, ROWS):
        rows = pl.ds(r, ROWS)
        picked = nn(pick_rows(r, pos_row[...], ROWS, count), slots_in[...])
        low_tokens[rows, :] = picked.astype(BF16)
        normal, _ = norm_parts(picked)
        low_normed[rows, :] = (normal * gain[...] + offset[...]).astype(BF16)
    left += [copies.start(low_tokens, tokens), copies.start(low_normed, normed)]
    for n, out in enumerate((q, k, v)):
        weights_came[n].wait()
        for r in range(0, count, half):
            rows = pl.ds(r, half)
            value = nn(low_normed[rows, :], weights[n])
            if n == 0:
                value = (value + bq[...]).astype(BF16).astype(F32) * 0.125
            elif n == 2:
                value = value + bv[...]
            low_out[n, rows, :] = value.astype(BF16)
            left.append(copies.start(low_out.at[n, rows], out.at[rows]))
    for copy in left:
        copy.wait()


def entry(slots, pos_row, gain, offset, wq, bq, wk, wv, bv):
    count, width = slots.shape
    out = jax.ShapeDtypeStruct((count, width), BF16)
    return pl.pallas_call(
        entry_kernel,
        grid=(1,),
        in_specs=[
            ANYWHERE,
            whole((1, count)),
            whole((1, width)),
            whole((1, width)),
            ANYWHERE,
            whole((1, width)),
            ANYWHERE,
            ANYWHERE,
            whole((1, width)),
        ],
        out_specs=[ANYWHERE] * 5,
        out_shape=[out] * 5,
        scratch_shapes=[
            pltpu.VMEM((count, width), BF16),
            pltpu.VMEM((3, width, width), BF16),
            pltpu.VMEM((count, width), BF16),
            pltpu.VMEM((count, width), BF16),
            pltpu.VMEM((3, count, width), BF16),
            pltpu.SemaphoreType.DMA((12,)),
        ],
        compiler_params=params(),
        cost_estimate=cost(8 * count * width * width, 18 * count * width),
        name="entry",
    )(slots, pos_row, gain, offset, wq, bq, wk, wv, bv)


def half_masks(width):
    lane = lax.broadcasted_iota(jnp.int32, (1, width), 1)
    return lane < width // 2


def split_heads(values):
    first = half_masks(values.shape[1])
    zero = jnp.zeros_like(values)
    return jnp.where(first, values, zero), jnp.where(first, zero, values)


def fill_bias(bias, start_col):
    count = bias.shape[0]
    for i in range(count // ROWS):
        ext = (i + 1) * ROWS
        rows = pl.ds(i * ROWS, ROWS)
        kpos = lax.broadcasted_iota(jnp.int32, (ROWS, ext), 1)
        qpos = lax.broadcasted_iota(jnp.int32, (ROWS, ext), 0) + i * ROWS
        keep = (kpos >= start_col[rows, :]) & (kpos <= qpos)
        bias[rows, :ext] = jnp.where(keep, 0.0, NEG)


def largest_square(values):
    lanes = values.shape[1]
    row = lax.broadcasted_iota(jnp.int32, (8, lanes), 0)
    lane = lax.broadcasted_iota(jnp.int32, (8, lanes), 1)
    select = jnp.where(row == lane // (lanes // 2), 1.0, 0.0).astype(BF16)
    wide = values.astype(F32)
    return jnp.max(nt(select, (wide * wide).astype(BF16)), axis=1, keepdims=True)


SAFE = 50.0


def attend_kernel(start_col, q_ref, k_ref, v_ref, mixed_ref, lse_ref, bias, total, sums):
    count, lanes = q_ref.shape

    @pl.when(pl.program_id(0) == 0)
    def _():
        fill_bias(bias, start_col)

    first = half_masks(lanes)
    bound = jnp.max(largest_square(q_ref[...]) * largest_square(k_ref[...]))
    safe = bound * (LOG2E * LOG2E) < SAFE * SAFE

    @pl.when(safe)
    def _():
        queries = split_heads(q_ref[...])
        work = [(j, h) for j in range(count // ROWS) for h in range(2)]

        def scores(j, h):
            return nt(queries[h][j * ROWS :], k_ref[j * ROWS : (j + 1) * ROWS, :])

        ahead = scores(*work[0])
        for n, (j, h) in enumerate(work):
            score = ahead
            if n + 1 < len(work):
                ahead = scores(*work[n + 1])
            ext = pl.ds(j * ROWS, count - j * ROWS)
            cols = pl.ds(j * ROWS, ROWS)
            terms = jnp.exp2(score * LOG2E + bias[ext, cols])
            part_sum = terms[:, :lanes]
            for c in range(lanes, ROWS, lanes):
                part_sum = part_sum + terms[:, c : c + lanes]
            value = split_heads(v_ref[cols, :])[h]
            part = nn(terms.astype(BF16), value)
            if j == 0:
                sums[h] = part_sum
                total[h] = part
            else:
                sums[h, ext, :] += part_sum
                total[h, ext, :] += part
        norms = [jnp.sum(sums[h], axis=1, keepdims=True) for h in range(2)]
        norm = jnp.where(first, norms[0], norms[1])
        mixed_ref[...] = ((total[0] + total[1]) / norm).astype(BF16)
        turned = jnp.log2(norm).T
        lse_ref[0, 0:1, :] = turned[0:1, :]
        lse_ref[0, 1:2, :] = turned[lanes // 2 : lanes // 2 + 1, :]

    @pl.when(jnp.logical_not(safe))
    def _():
        for i in range(count // ROWS):
            ext = (i + 1) * ROWS
            rows = pl.ds(i * ROWS, ROWS)
            out, stats = None, []
            for query, value in zip(split_heads(q_ref[rows, :]), split_heads(v_ref[:ext, :])):
                score = nt(query, k_ref[:ext, :]) * LOG2E + bias[rows, :ext]
                top = jnp.max(score, axis=1, keepdims=True)
                terms = jnp.exp2(score - top)
                norm = jnp.sum(terms, axis=1, keepdims=True)
                part = nn(terms.astype(BF16), value)
                out = part if out is None else out + part
                stats.append((top + jnp.log2(norm), norm))
            norm = jnp.where(first, stats[0][1], stats[1][1])
            mixed_ref[rows, :] = (out / norm).astype(BF16)
            turned = jnp.where(first, stats[0][0], stats[1][0]).T
            lse_ref[0, 0:1, rows] = turned[0:1, :]
            lse_ref[0, 1:2, rows] = turned[lanes // 2 : lanes // 2 + 1, :]


def attend(start_col, q, k, v):
    count, width = q.shape
    pairs = HEADS // 2
    lanes = width // pairs
    col = pl.BlockSpec((count, lanes), lambda p: (0, p))
    return pl.pallas_call(
        attend_kernel,
        grid=(pairs,),
        in_specs=[whole((count, 1)), col, col, col],
        out_specs=[col, pl.BlockSpec((1, 8, count), lambda p: (p, 0, 0))],
        out_shape=[
            jax.ShapeDtypeStruct((count, width), BF16),
            jax.ShapeDtypeStruct((pairs, 8, count), F32),
        ],
        scratch_shapes=[
            pltpu.VMEM((count, count), F32),
            pltpu.VMEM((2, count, lanes), F32),
            pltpu.VMEM((2, count, lanes), F32),
        ],
        compiler_params=params(),
        cost_estimate=cost(8 * count * count * width, 8 * count * width, HEADS * count * count // 2),
        name="attend",
    )(start_col, q, k, v)


def leave_kernel(
    mixed, wo, bo, tokens, live_col, pos_col, out, residual, mixed_in, wo_in, tokens_in, kept, low, sems
):
    copies = Copies(sems)
    count = kept.shape[0]
    half = count // 2
    first = copies.start(wo, wo_in)
    came = []
    for r in range(0, count, half):
        rows = pl.ds(r, half)
        came.append(copies.start(mixed.at[rows], mixed_in.at[rows]))
        came.append(copies.start(tokens.at[rows], tokens_in.at[rows]))
    first.wait()
    for r in range(0, count, half):
        rows = pl.ds(r, half)
        for copy in came[:2]:
            copy.wait()
        came = came[2:]
        branch = nn(mixed_in[rows, :], wo_in[...]) + bo[...]
        kept[rows, :] = (tokens_in[rows, :].astype(F32) + live_col[rows, :] * branch).astype(BF16)
    left = [copies.start(kept, residual)]
    low[...] = nn(pick_slots(pos_col[...], count), kept[...]).astype(BF16)
    left.append(copies.start(low, out))
    for copy in left:
        copy.wait()


def leave(mixed, wo, bo, tokens, live_col, pos_col):
    count, width = mixed.shape
    rows = pos_col.shape[0]
    return pl.pallas_call(
        leave_kernel,
        grid=(1,),
        in_specs=[
            ANYWHERE,
            ANYWHERE,
            whole((1, width)),
            ANYWHERE,
            whole((count, 1)),
            whole((rows, 1)),
        ],
        out_specs=[ANYWHERE] * 2,
        out_shape=[
            jax.ShapeDtypeStruct((rows, width), BF16),
            jax.ShapeDtypeStruct((count, width), BF16),
        ],
        scratch_shapes=[
            pltpu.VMEM((count, width), BF16),
            pltpu.VMEM((width, width), BF16),
            pltpu.VMEM((count, width), BF16),
            pltpu.VMEM((count, width), BF16),
            pltpu.VMEM((rows, width), BF16),
            pltpu.SemaphoreType.DMA((7,)),
        ],
        compiler_params=params(),
        cost_estimate=cost(3 * count * width * width, 10 * count * width),
        name="leave",
    )(mixed, wo, bo, tokens, live_col, pos_col)


def pick_kernel(residual, pos_col, out):
    out[...] = nn(pick_slots(pos_col[...], residual.shape[0]), residual[...]).astype(BF16)


def pick(residual, pos_col):
    count, width = residual.shape
    rows = pos_col.shape[0]
    return pl.pallas_call(
        pick_kernel,
        grid=(1,),
        in_specs=[whole((count, width)), whole((rows, 1))],
        out_specs=whole((rows, width)),
        out_shape=jax.ShapeDtypeStruct((rows, width), BF16),
        compiler_params=params(),
        cost_estimate=cost(2 * rows * count * width, 6 * count * width),
        name="pick",
    )(residual, pos_col)


def reenter_kernel(parts, *refs):
    slots = refs[:parts]
    pos_row, live_col, wo, grad_residual, grad_proj, grad_mixed, bias_sum = refs[parts : parts + 7]
    slots_in, wo_in, low, sems = refs[parts + 7 :]
    copies = Copies(sems)
    came, start = [], 0
    for part in slots:
        size = part.shape[0]
        came.append(copies.start(part, slots_in.at[pl.ds(start, size)]))
        start += size
    wo_came = copies.start(wo, wo_in)
    for copy in came:
        copy.wait()
    count = slots_in.shape[0]
    half = count // 2
    total, left = None, []
    for r in range(0, count, half):
        rows = pl.ds(r, half)
        picked = nn(pick_rows(r, pos_row[...], half, count), slots_in[...])
        masked = live_col[rows, :] * picked
        low[0, rows, :] = picked.astype(BF16)
        low[1, rows, :] = masked.astype(BF16)
        part = jnp.sum(masked, axis=0, keepdims=True)
        total = part if total is None else total + part
        left.append(copies.start(low.at[0, rows], grad_residual.at[rows]))
        left.append(copies.start(low.at[1, rows], grad_proj.at[rows]))
    bias_sum[...] = total
    wo_came.wait()
    for r in range(0, count, half):
        rows = pl.ds(r, half)
        low[2, rows, :] = nt(low[1, rows, :], wo_in[...]).astype(BF16)
        left.append(copies.start(low.at[2, rows], grad_mixed.at[rows]))
    for copy in left:
        copy.wait()


def reenter(slots, pos_row, live_col, wo):
    parts = len(slots)
    width = slots[0].shape[1]
    count = sum(v.shape[0] for v in slots)
    out = jax.ShapeDtypeStruct((count, width), BF16)
    return pl.pallas_call(
        functools.partial(reenter_kernel, parts),
        grid=(1,),
        in_specs=[ANYWHERE] * parts + [whole((1, count)), whole((count, 1)), ANYWHERE],
        out_specs=[ANYWHERE] * 3 + [whole((1, width))],
        out_shape=[out] * 3 + [jax.ShapeDtypeStruct((1, width), F32)],
        scratch_shapes=[
            pltpu.VMEM((count, width), BF16),
            pltpu.VMEM((width, width), BF16),
            pltpu.VMEM((3, count, width), BF16),
            pltpu.SemaphoreType.DMA((parts + 7,)),
        ],
        compiler_params=params(),
        cost_estimate=cost(4 * count * width * width, 10 * count * width),
        name="reenter",
    )(*slots, pos_row, live_col, wo)


def attend_back_kernel(
    start_row, q_ref, k_ref, v_ref, o_ref, g_ref, lse_ref, out_ref, bias, sums
):
    count, lanes = q_ref.shape

    @pl.when(pl.program_id(0) == 0)
    def _():
        for j in range(count // ROWS):
            cols = pl.ds(j * ROWS, count - j * ROWS)
            shape = (ROWS, count - j * ROWS)
            kpos = lax.broadcasted_iota(jnp.int32, shape, 0) + j * ROWS
            qpos = lax.broadcasted_iota(jnp.int32, shape, 1) + j * ROWS
            keep = (kpos >= start_row[:, cols]) & (kpos <= qpos)
            bias[pl.ds(j * ROWS, ROWS), cols] = jnp.where(keep, 0.0, NEG)

    products = o_ref[...].astype(F32) * g_ref[...].astype(F32)
    high = products.astype(BF16)
    low = (products - high.astype(F32)).astype(BF16)
    sel_row = lax.broadcasted_iota(jnp.int32, (8, lanes), 0)
    sel_lane = lax.broadcasted_iota(jnp.int32, (8, lanes), 1)
    select = jnp.where(sel_row == sel_lane // (lanes // 2), 1.0, 0.0).astype(BF16)
    deltas = nt(select, high) + nt(select, low)

    queries = split_heads(q_ref[...])
    grads = split_heads(g_ref[...])
    wide = 2 * ROWS
    items = []
    for s in range(0, count, wide):
        if s + wide < count:
            items.append((s, s + wide, s + wide, count))
        items.append((s, s + ROWS, s, s + wide))
        items.append((s + ROWS, s + wide, s + ROWS, s + wide))
    work = [(item, h) for item in items for h in range(2)]

    def products_of(item, h):
        k_from, k_to, q_from, q_to = item
        return (
            nt(k_ref[k_from:k_to, :], queries[h][q_from:q_to]),
            nt(v_ref[k_from:k_to, :], grads[h][q_from:q_to]),
        )

    seen_keys, seen_queries = set(), set()

    def add(target, start, part, seen):
        for r in range(0, part.shape[0], ROWS):
            rows = pl.ds(start + r, ROWS)
            if start + r in seen:
                target[rows, :] += part[r : r + ROWS]
            else:
                target[rows, :] = part[r : r + ROWS]

    ahead = products_of(*work[0])
    for n, (item, h) in enumerate(work):
        k_from, k_to, q_from, q_to = item
        score, grad_weights = ahead
        if n + 1 < len(work):
            ahead = products_of(*work[n + 1])
        cols = slice(q_from, q_to)
        weights = jnp.exp2(score * LOG2E + bias[k_from:k_to, cols] - lse_ref[0, h : h + 1, cols])
        grad_score = (weights * (grad_weights - deltas[h : h + 1, cols])).astype(BF16)
        key = split_heads(k_ref[k_from:k_to, :])[h]
        add(sums.at[2], k_from, nn(weights.astype(BF16), grads[h][cols]), seen_keys)
        add(sums.at[1], k_from, nn(grad_score, queries[h][cols]), seen_keys)
        add(sums.at[0], q_from, tn(grad_score, key), seen_queries)
        seen_keys |= set(range(k_from, k_to, ROWS))
        seen_queries |= set(range(q_from, q_to, ROWS))
    out_ref[0] = (sums[0] * 0.125).astype(BF16)
    out_ref[1] = sums[1].astype(BF16)
    out_ref[2] = sums[2].astype(BF16)


def attend_back(start_row, q, k, v, mixed, grad_mixed, lse):
    count, width = q.shape
    pairs = HEADS // 2
    lanes = width // pairs
    col = pl.BlockSpec((count, lanes), lambda p: (0, p))
    return pl.pallas_call(
        attend_back_kernel,
        grid=(pairs,),
        in_specs=[whole((1, count))]
        + [col] * 5
        + [pl.BlockSpec((1, 8, count), lambda p: (p, 0, 0))],
        out_specs=pl.BlockSpec((3, count, lanes), lambda p: (0, 0, p)),
        out_shape=jax.ShapeDtypeStruct((3, count, width), BF16),
        scratch_shapes=[pltpu.VMEM((count, count), F32), pltpu.VMEM((3, count, lanes), F32)],
        compiler_params=params(),
        cost_estimate=cost(20 * count * count * width, 16 * count * width, HEADS * count * count // 2),
        name="attend_back",
    )(start_row, q, k, v, mixed, grad_mixed, lse)


def finish_kernel(grads, wq, wk, wv, tokens, grad_residual, gain, pos_col, others, *refs):
    outs, sums = refs[:-8], refs[-8]
    grads_in, weights, tokens_in, residual_in, total, kept, sems = refs[-7:]
    copies = Copies(sems)
    came = []
    for n, w in enumerate((wq, wk, wv)):
        came.append((copies.start(grads.at[n], grads_in.at[n]), copies.start(w, weights.at[n])))
    rest = [copies.start(tokens, tokens_in), copies.start(grad_residual, residual_in)]
    count = kept.shape[0]
    half = count // 2
    for n in range(3):
        for copy in came[n]:
            copy.wait()
        for r in range(0, count, half):
            rows = pl.ds(r, half)
            part = nt(grads_in[n, rows, :], weights[n])
            if n == 0:
                total[rows, :] = part
            else:
                total[rows, :] += part
    for copy in rest:
        copy.wait()
    sums[...] = others[...]
    for r in range(0, count, ROWS):
        rows = pl.ds(r, ROWS)
        grad = total[rows, :]
        normal, root = norm_parts(tokens_in[rows, :].astype(F32))
        kept[rows, :] = (
            residual_in[rows, :].astype(F32) + norm_grad(grad, normal, root, gain[...])
        ).astype(BF16)
        sums[0:1, :] += jnp.sum(grad * normal, axis=0, keepdims=True)
        sums[1:2, :] += jnp.sum(grad, axis=0, keepdims=True)
        sums[2:3, :] += jnp.sum(grads_in[0, rows, :].astype(F32), axis=0, keepdims=True)
        sums[3:4, :] += jnp.sum(grads_in[2, rows, :].astype(F32), axis=0, keepdims=True)
    left = []
    for r in range(0, count, half):
        rows = pl.ds(r, half)
        chosen = pick_slots(pos_col[rows, :], count)
        residual_in[rows, :] = nn(chosen, kept[...]).astype(BF16)
    start = 0
    for out in outs:
        rows = out.shape[0]
        left.append(copies.start(residual_in.at[pl.ds(start, rows)], out))
        start += rows
    for copy in left:
        copy.wait()


def finish(sizes, grads, weights, tokens, grad_residual, gain, pos_col, others):
    count, width = tokens.shape
    return pl.pallas_call(
        finish_kernel,
        grid=(1,),
        in_specs=[ANYWHERE] * 6 + [whole((1, width)), whole((count, 1)), whole((8, width))],
        out_specs=[ANYWHERE] * len(sizes) + [whole((8, width))],
        out_shape=[jax.ShapeDtypeStruct((rows, width), BF16) for rows in sizes]
        + [jax.ShapeDtypeStruct((8, width), F32)],
        scratch_shapes=[
            pltpu.VMEM((3, count, width), BF16),
            pltpu.VMEM((3, width, width), BF16),
            pltpu.VMEM((count, width), BF16),
            pltpu.VMEM((count, width), BF16),
            pltpu.VMEM((count, width), F32),
            pltpu.VMEM((count, width), BF16),
            pltpu.SemaphoreType.DMA((8 + len(sizes),)),
        ],
        compiler_params=params(),
        cost_estimate=cost(8 * count * width * width, 20 * count * width),
        name="finish",
    )(grads, *weights, tokens, grad_residual, gain, pos_col, others)


GELU_ROOT = math.sqrt(2.0 / math.pi)
GELU_CUBE = 0.044715
STEP = 1024


def shard_of(step):
    return (step % 2) * 2 + step // 2


def expert_kernel(parts, device, source, *refs):
    it = iter(refs)
    take = lambda n: [next(it) for _ in range(n)]
    slots, cots, lives = take(3)
    up, down, up_bias, gain, offset = take(5)
    grads = take(max(len(parts), 1))
    mine, theirs, sums, up_sums = take(4)
    ffn_in, branch, grad_sum, low = take(4)
    rows, model = slots.shape
    t = pl.program_id(0)

    @pl.when(t == 0)
    def _():
        normal, _ = norm_parts(slots[...].astype(F32))
        ffn_in[...] = (normal * gain[...] + offset[...]).astype(BF16)
        cot = cots[...].reshape(rows, model).astype(F32)
        branch[...] = (lives[...].reshape(rows, 1) * cot).astype(BF16)
        theirs[0] = ffn_in[...]
        theirs[1] = branch[...]
        grad_sum[...] = jnp.zeros_like(grad_sum)

    @pl.when(t == 2)
    def _():
        mine[0] = ffn_in[...]
        mine[1] = branch[...]

    width = up.shape[2]

    def compute(out):
        for c in range(0, width, STEP):
            cols = pl.ds(c, STEP)
            pre = nn(ffn_in[...], up[0, :, cols]) + up_bias[0, :, cols]
            square = pre * pre
            tanh = jnp.tanh(pre * (GELU_ROOT + (GELU_ROOT * GELU_CUBE) * square))
            half = 0.5 * (1.0 + tanh)
            slope = half + (0.5 * pre) * (1.0 - tanh * tanh) * (
                GELU_ROOT + (3.0 * GELU_ROOT * GELU_CUBE) * square
            )
            out[0, :, cols] = (pre * half).astype(BF16)
            grad_pre = (nt(branch[...], down[0, cols, :]) * slope).astype(BF16)
            out[1, :, cols] = grad_pre
            up_sums[0, :, cols] = jnp.sum(grad_pre.astype(F32), axis=0, keepdims=True)
            grad_sum[...] += nt(grad_pre, up[0, :, cols])

    @pl.when(t < 2)
    def _():
        compute(mine)

    @pl.when(t >= 2)
    def _():
        compute(theirs)

    @pl.when(t == 3)
    def _():
        routed = slots[...].astype(F32)
        normal, root = norm_parts(routed)
        grad = grad_sum[...]
        cot = cots[...].reshape(rows, model).astype(F32)
        grad_routed = (cot + norm_grad(grad, normal, root, gain[...])).astype(BF16)
        if not parts:
            grads[0][...] = grad_routed
        else:
            low[...] = grad_routed
            short, n = rows // sum(parts), 0
            for part, blocks in zip(grads, parts):
                for j in range(blocks):
                    place = pl.multiple_of(source[n] * short, short)
                    part[j * short : (j + 1) * short, :] = low[pl.ds(place, short), :]
                    n += 1
        sums[...] = jnp.zeros_like(sums)
        sums[0:1, :] = jnp.sum(grad * normal, axis=0, keepdims=True)
        sums[1:2, :] = jnp.sum(grad, axis=0, keepdims=True)
        sums[2:3, :] = jnp.sum(branch[...].astype(F32), axis=0, keepdims=True)


def expert_chunk(chunk, parts, device, source, slots, cot, live, ups, downs, up_bias, gain, offset):
    rows, width = slots.shape
    groups, piece, _ = cot.shape
    short = rows // groups
    sizes = [short * n for n in parts] or [rows]
    part = ups.shape[2]
    assert part == width and ups.shape[0] == 4
    block = pl.BlockSpec((groups, short, width), lambda t, *_: (0, chunk, 0))
    packet = jax.ShapeDtypeStruct((6, rows, width), BF16)
    weights = pl.BlockSpec((1, width, part), lambda t, device, *_: (shard_of(t) ^ device[0], 0, 0))
    bias = pl.BlockSpec((1, 1, part), lambda t, device, *_: (shard_of(t) ^ device[0], 0, 0))
    return pl.pallas_call(
        functools.partial(expert_kernel, parts),
        grid_spec=pltpu.PrefetchScalarGridSpec(
            num_scalar_prefetch=2,
            grid=(4,),
            in_specs=[
                whole((rows, width)),
                block,
                pl.BlockSpec((groups, short, 1), lambda t, *_: (0, chunk, 0)),
            ]
            + [weights, weights, bias, whole((1, width)), whole((1, width))],
            out_specs=[whole((size, width)) for size in sizes]
            + [
                pl.BlockSpec((2, rows, width), lambda t, *_: (jnp.minimum(t, 2), 0, 0)),
                pl.BlockSpec((2, rows, width), lambda t, *_: (jnp.where(t < 2, 2, t - 2), 0, 0)),
                whole((8, width)),
                bias,
            ],
            scratch_shapes=[
                pltpu.VMEM((rows, width), BF16),
                pltpu.VMEM((rows, width), BF16),
                pltpu.VMEM((rows, width), F32),
                pltpu.VMEM((rows, width), BF16),
            ],
        ),
        out_shape=[jax.ShapeDtypeStruct((size, width), BF16) for size in sizes]
        + [
            packet,
            packet,
            jax.ShapeDtypeStruct((8, width), F32),
            jax.ShapeDtypeStruct((4, 1, part), F32),
        ],
        compiler_params=params(),
        cost_estimate=cost(24 * rows * width * part, 16 * width * part, 4 * rows * part),
        name="expert_chunk",
    )(device, source, slots, cot, live, ups, downs, up_bias, gain, offset)


def expert_out_kernel(chunks, device, *refs):
    mine, theirs, slots = refs[:chunks], refs[chunks : 2 * chunks], refs[2 * chunks : 3 * chunks]
    down, bias, live, out, total = refs[3 * chunks :]
    t = pl.program_id(0)
    rows = slots[0].shape[0]
    for n in range(4):

        @pl.when(t == n)
        def _(n=n):
            for c in range(chunks):
                part = nn((mine if n < 2 else theirs)[c][0], down[0])
                if n == 0:
                    total[c * rows : (c + 1) * rows, :] = part
                else:
                    total[c * rows : (c + 1) * rows, :] += part

    @pl.when(t == 3)
    def _():
        groups, piece, width = out.shape
        short = piece // chunks
        for c in range(chunks):
            branch = total[c * rows : (c + 1) * rows, :] + bias[...]
            keep = live[:, c * short : (c + 1) * short, :].reshape(rows, 1)
            value = (slots[c][...].astype(F32) + keep * branch).astype(BF16)
            out[:, c * short : (c + 1) * short, :] = value.reshape(groups, short, width)


def expert_out(device, mine, theirs, slots, downs, bias, live):
    chunks = len(slots)
    rows, width = slots[0].shape
    part = downs.shape[1]
    groups, piece, _ = live.shape
    act = lambda index: pl.BlockSpec((1, rows, part), index)
    return pl.pallas_call(
        functools.partial(expert_out_kernel, chunks),
        grid_spec=pltpu.PrefetchScalarGridSpec(
            num_scalar_prefetch=1,
            grid=(4,),
            in_specs=[act(lambda t, *_: (2 * jnp.minimum(t, 1), 0, 0))] * chunks
            + [act(lambda t, *_: (2 * jnp.maximum(t - 2, 0), 0, 0))] * chunks
            + [whole((rows, width))] * chunks
            + [pl.BlockSpec((1, part, width), lambda t, device: (shard_of(t) ^ device[0], 0, 0))]
            + [whole((1, width)), whole((groups, piece, 1))],
            out_specs=whole((groups, piece, width)),
            scratch_shapes=[pltpu.VMEM((chunks * rows, width), F32)],
        ),
        out_shape=jax.ShapeDtypeStruct((groups, piece, width), BF16),
        compiler_params=params(),
        cost_estimate=cost(8 * chunks * rows * part * width, 32 * rows * width),
        name="expert_out",
    )(device, *mine, *theirs, *slots, downs, bias, live)


CUTS = ((1024,), (304, 400, 320))


def expert_grads_kernel(count, shard, added, *refs):
    packets, parts, outs = refs[:count], refs[count : count + added], refs[count + added : -7]
    act, branch, ffn_in, pre, earlier, full, sems = refs[-7:]
    copies = Copies(sems)
    rows = packets[0].shape[1]

    def fetch(slot, target):
        return [copies.start(p.at[slot], target.at[pl.ds(n * rows, rows)]) for n, p in enumerate(packets)]

    first = fetch(shard, act) + fetch(5, branch)
    before = [copies.start(p.at[0], earlier.at[m]) for m, p in enumerate(parts)]
    second = fetch(4, ffn_in) + fetch(shard + 1, pre)
    left = []
    for m, (came, one, two) in enumerate(((first, act, branch), (second, ffn_in, pre))):
        for copy in came:
            copy.wait()
        total = tn(one[...], two[...])
        if added:
            before[m].wait()
            total = total + earlier[m]
        full[m] = total.astype(full.dtype)
        if not added:
            left.append(copies.start(full.at[m], outs[m].at[0]))
            continue
        start, skip = 0, sum(len(cuts) for cuts in CUTS[:m])
        for n, cut in enumerate(CUTS[m]):
            left.append(copies.start(full.at[m, pl.ds(start, cut)], outs[skip + n]))
            start += cut
    for copy in left:
        copy.wait()


def expert_grads(far, packets, parts=()):
    _, rows, width = packets[0].shape
    count, added = len(packets), len(parts)
    assert sum(CUTS[0]) == sum(CUTS[1]) == width
    if added:
        shapes = [jax.ShapeDtypeStruct((c, width), BF16) for cuts in CUTS for c in cuts]
    else:
        shapes = [jax.ShapeDtypeStruct((1, width, width), F32)] * 2
    return pl.pallas_call(
        functools.partial(expert_grads_kernel, count, 2 if far else 0, added),
        grid=(1,),
        in_specs=[ANYWHERE] * (count + added),
        out_specs=[ANYWHERE] * len(shapes),
        out_shape=shapes,
        scratch_shapes=[pltpu.VMEM((count * rows, width), BF16)] * 4
        + [
            pltpu.VMEM((2, width, width) if added else (2, 16, 128), F32),
            pltpu.VMEM((2, width, width), BF16 if added else F32),
            pltpu.SemaphoreType.DMA((4 * count + added + len(shapes),)),
        ],
        compiler_params=params(),
        cost_estimate=cost(4 * count * rows * width * width, 20 * width * width),
        name="far_rest" if added else ("far_part" if far else "near_grads"),
    )(*packets, *parts)


def shared_grads_kernel(
    streams, blocks, codes, normed, mixed, token_grads, grad_proj, keep, send,
    left_in, right_in, total, low, sems
):
    copies = Copies(sems)
    number = right_in.shape[0]
    came = [[copies.start(normed, left_in.at[0]), copies.start(token_grads.at[0], right_in.at[0])]]
    came += [[copies.start(token_grads.at[m], right_in.at[m])] for m in range(1, number - 1)]
    came.append([copies.start(mixed, left_in.at[1]), copies.start(grad_proj, right_in.at[number - 1])])
    half = blocks // 2
    rows = total.shape[1]
    size = rows // half
    first = codes[0] // half
    left = []
    for m in range(number):
        for copy in came[m]:
            copy.wait()
        for h, target in enumerate((keep, send)):
            n = (2 * m + h) % 2
            side = pl.ds(pl.multiple_of((first ^ h) * rows, rows), rows)
            total[n] = tn(left_in[0 if m < number - 1 else 1, :, side], right_in[m])
            for j in range(half):
                code = codes[(j // (half // streams)) % streams] % half
                place = pl.multiple_of((code ^ j) * size, size)
                low[m, h, pl.ds(j * size, size), :] = total[n, pl.ds(place, size), :].astype(BF16)
            left.append(copies.start(low.at[m, h], target.at[m]))
    for copy in left:
        copy.wait()


def shared_grads(layout, normed, mixed, token_grads, grad_proj):
    count, width = normed.shape
    number = token_grads.shape[0] + 1
    half = width // 2
    return pl.pallas_call(
        functools.partial(shared_grads_kernel, layout.streams, layout.blocks),
        grid_spec=pltpu.PrefetchScalarGridSpec(
            num_scalar_prefetch=1,
            grid=(1,),
            in_specs=[ANYWHERE] * 4,
            out_specs=[ANYWHERE] * 2,
            scratch_shapes=[
                pltpu.VMEM((2, count, width), BF16),
                pltpu.VMEM((number, count, width), BF16),
                pltpu.VMEM((2, half, width), F32),
                pltpu.VMEM((number, 2, half, width), BF16),
                pltpu.SemaphoreType.DMA((3 * number + 2,)),
            ],
        ),
        out_shape=[jax.ShapeDtypeStruct((number, half, width), BF16)] * 2,
        compiler_params=params(),
        cost_estimate=cost(2 * number * count * width * width, 6 * number * width * width),
        name="shared_grads",
    )(layout.codes, normed, mixed, token_grads, grad_proj)


def unmix_kernel(group, parts, codes, half_place, source, pieces, *refs):
    rows_in, came_in, full, sems = refs[-4:]
    number, half, _ = came_in.shape
    outs = refs[-4 - number - min(parts, 1) : -4]
    copies = Copies(sems)
    came = [copies.start(pieces.at[m], came_in.at[m]) for m in range(number)]
    joined, left = [], []
    for r in range(parts):
        size = refs[r].shape[0]
        place = pl.multiple_of(source[r] * size, size)
        joined.append(copies.start(refs[r], rows_in.at[pl.ds(place, size)]))
    rows = half // 4
    size = rows // group
    for m in range(number):
        came[m].wait()
        for n in range(4):
            code = codes[n // 2]
            low = code % group
            block = n ^ ((code // group) % 2)
            for j in range(group):
                place = pl.multiple_of(block * rows + (low ^ j) * size, size)
                start = n * rows + j * size
                full[m, pl.ds(place, size), :] = came_in[m, start : start + size, :].astype(F32)
        target = outs[m].at[pl.ds(pl.multiple_of(half_place[0] * half, half), half)]
        left.append(copies.start(full.at[m], target))
        if m == 0 and parts:
            for copy in joined:
                copy.wait()
            left.append(copies.start(rows_in, outs[number]))
    for copy in left:
        copy.wait()


def unmix(layout, half_place, pieces, before=None, source=None, joined=()):
    number, rows, width = pieces.shape
    earlier = [] if before is None else list(before)
    parts = len(joined)
    source = half_place if source is None else source
    total = sum(v.shape[0] for v in joined)
    return pl.pallas_call(
        functools.partial(unmix_kernel, layout.blocks // 8, parts),
        grid_spec=pltpu.PrefetchScalarGridSpec(
            num_scalar_prefetch=3,
            grid=(1,),
            in_specs=[ANYWHERE] * (1 + parts + len(earlier)),
            out_specs=[ANYWHERE] * (number + min(parts, 1)),
            scratch_shapes=[
                pltpu.VMEM((max(total, 16), width), BF16),
                pltpu.VMEM((number, rows, width), BF16),
                pltpu.VMEM((number, rows, width), F32),
                pltpu.SemaphoreType.DMA((2 * number + parts + 1,)),
            ],
        ),
        out_shape=[jax.ShapeDtypeStruct((2 * rows, width), F32)] * number
        + [jax.ShapeDtypeStruct((total, width), BF16)] * min(parts, 1),
        input_output_aliases={4 + parts + m: m for m in range(len(earlier))},
        compiler_params=params(),
        cost_estimate=cost(number * rows * width, 6 * number * rows * width),
        name="unmix",
    )(layout.codes, half_place, source, pieces, *joined, *earlier)


def swap(values, step):
    axis, size, bit = step
    return lax.ppermute(values, axis, [(i, i ^ bit) for i in range(size)])


def exchange(values):
    return lax.all_to_all(values, "expert", split_axis=0, concat_axis=0, tiled=True)


def turn(values, size, by):
    return lax.ppermute(values, "expert", [(i, (i + by) % size) for i in range(size)])


def bits_of(size):
    return [1 << b for b in range(size.bit_length() - 1)]


def add_low(left, right):
    return (left.astype(F32) + right.astype(F32)).astype(BF16)


def tie(*values):
    return lax.optimization_barrier(values)


class SharedSum:
    streams = 2
    least = 16

    def __init__(self, n_expert, n_dp, rows):
        steps = [("dp", n_dp, b) for b in bits_of(n_dp)] + [
            ("expert", n_expert, b) for b in bits_of(n_expert)
        ]
        steps.sort(key=lambda s: (s[2], s[0]))
        self.steps = steps
        self.first, one, two, *rest = steps
        self.pair = ((two, one), (one, two))
        self.rest, self.left = rest[:2], rest[2:]
        self.blocks = 2 * self.streams * 4 * 4
        assert rows // self.blocks >= self.least and self.rest[0][0] == self.rest[1][0]
        self.codes = jnp.stack([self.code([self.first, None, *pair, *self.rest]) for pair in self.pair])

    def code(self, steps):
        total = jnp.int32(0)
        for step in steps:
            mine = 0 if step is None else (lax.axis_index(step[0]) // step[2]) % 2
            total = total * 2 + mine
        return total.astype(jnp.int32)

    @staticmethod
    def halve(values, step, axis):
        middle = values.shape[axis] // 2
        keep = lax.slice_in_dim(values, 0, middle, axis=axis)
        send = lax.slice_in_dim(values, middle, 2 * middle, axis=axis)
        return add_low(keep, swap(send, step))

    @staticmethod
    def double(values, step, axis):
        return jnp.concatenate([values, swap(values, step)], axis=axis)

    def reduce_first(self, keep, send):
        came = swap(send, self.first)
        size = keep.shape[1] // 4
        quarter = lambda v, n: lax.slice_in_dim(v, n * size, (n + 1) * size, axis=1)
        return [add_low(quarter(keep, n), quarter(came, n)) for n in range(4)]

    def reduce_pair_first(self, quarters):
        return [
            add_low(quarters[2 * n], swap(quarters[2 * n + 1], self.pair[n][0]))
            for n in range(self.streams)
        ]

    def reduce_pair(self, parts, n):
        return [self.halve(part, pair[n], 1) for part, pair in zip(parts, self.pair)]

    def partners(self, total, j):
        (axis, size, high), (_, _, low) = self.rest
        return swap(total, (axis, size, (j // 2) * high + (j % 2) * low))

    def reduce_rest(self, total):
        size = total.shape[2] // 4
        piece = lambda j: total[:, :, j * size : (j + 1) * size]
        sum_all = piece(0).astype(F32)
        for j in range(1, 4):
            sum_all = sum_all + self.partners(piece(j), j).astype(F32)
        total = sum_all.astype(BF16)
        for step in self.left:
            total = add_low(total, swap(total, step))
        return total

    def gather_rest(self, total):
        return jnp.concatenate([total] + [self.partners(total, j) for j in range(1, 4)], axis=2)

    def gather_pair(self, parts, n):
        return [self.double(part, pair[n], 1) for part, pair in zip(parts, self.pair)]

    def gather_first(self, parts):
        total = jnp.concatenate(parts, axis=1)
        mine = ((lax.axis_index(self.first[0]) // self.first[2]) % 2).astype(jnp.int32).reshape(1)
        return (mine, total), (1 - mine, swap(total, self.first))


def small_sum(values, steps):
    for step in steps:
        if step[0] == "dp":
            values = values + swap(values, step)
        else:
            part = values[:8]
            values = jnp.concatenate([part + swap(part, step), values[8:]], axis=0)
    return values


CHUNKS = 2


def per_device(
    n_expert,
    n_dp,
    block_in,
    seq_lengths,
    slot_position,
    first_gain,
    first_bias,
    query_weight,
    query_bias,
    key_weight,
    value_weight,
    value_bias,
    out_weight,
    out_bias,
    second_gain,
    second_bias,
    expert_up,
    expert_up_bias,
    expert_down,
    expert_down_bias,
    block_cot,
):
    count, width = block_in.shape
    piece = count // n_expert
    row = lambda v: v.reshape(1, -1)
    device = lax.axis_index("dp")
    part = expert_up.shape[2]
    dp_steps = [("dp", n_dp, b) for b in bits_of(n_dp)]
    all_steps = dp_steps + [("expert", n_expert, b) for b in bits_of(n_expert)]

    core, far = dp_steps
    ups = lax.all_gather(expert_up[0], "dp", axis=0)
    downs = lax.all_gather(expert_down[0], "dp", axis=0)
    arrived = exchange(block_in)

    position = slot_position[0]
    ends = jnp.cumsum(seq_lengths[0])
    total_live = ends[-1]
    ids = jnp.arange(count, dtype=jnp.int32)
    live = ids < total_live
    begin = jnp.max(jnp.where(ends[None, :] <= ids[:, None], ends[None, :], 0), axis=1)
    begin = jnp.where(live, begin, ids).astype(jnp.int32)
    live_col = live.astype(F32).reshape(count, 1)
    in_chunks = position.reshape(n_expert, CHUNKS, -1).transpose(1, 0, 2).reshape(count)
    slot_live = (position < total_live).astype(F32).reshape(n_expert, piece)
    start_row, start_col = begin.reshape(1, count), begin.reshape(count, 1)
    pos_row, chunk_col = position.reshape(1, count), in_chunks.reshape(count, 1)
    shared = SharedSum(n_expert, n_dp, width)
    expert = lax.axis_index("expert")
    codes = jnp.concatenate([jnp.arange(xs, n_expert, 2, dtype=jnp.int32) for xs in range(2)])
    partners = (expert ^ codes).astype(jnp.int32)
    leave_col = jnp.take(position.reshape(n_expert, piece), partners, axis=0).reshape(count, 1)
    side = n_expert // 2
    back_codes = [0] + [2 * j for j in range(2, side)] + [2, 3, 1] + [2 * j + 1 for j in range(2, side)]
    back = (expert ^ jnp.array(back_codes, jnp.int32)).astype(jnp.int32)
    last_slots = jnp.take(position.reshape(n_expert, CHUNKS, -1)[:, -1], back, axis=0)
    came_row = jnp.concatenate([in_chunks[: count - count // CHUNKS], last_slots.reshape(-1)])
    came_row = came_row.reshape(1, count)
    leave_col, partners, back, came_row = tie(leave_col, partners, back, came_row)
    arrived, start_row, start_col, pos_row, chunk_col, live_col, shared.codes = tie(
        arrived, start_row, start_col, pos_row, chunk_col, live_col, shared.codes
    )
    route_live = exchange(slot_live).reshape(n_expert, piece, 1)

    tokens, normed, query, key, value = entry(
        arrived, pos_row, row(first_gain), row(first_bias), query_weight,
        row(query_bias), key_weight, value_weight, row(value_bias),
    )
    mixed, lse = attend(start_col, query, key, value)
    some = count // CHUNKS
    first, residual = leave(
        mixed, out_weight, row(out_bias), tokens, live_col, chunk_col[:some]
    )
    sent = [first] + [
        pick(residual, chunk_col[c * some : (c + 1) * some]) for c in range(1, CHUNKS)
    ]
    routed = [exchange(sent[0])]

    blocks = lambda v: v.reshape(n_expert, piece, width)
    place = device.astype(jnp.int32).reshape(1)
    up_bias = expert_up_bias[0].reshape(n_dp, 1, part)
    grads, mine, theirs, got, sums, up_sums = ([None] * CHUNKS for _ in range(6))
    returned = []
    to_partner = lambda v, j: swap(v, ("expert", n_expert, 2 * j))
    for c in range(CHUNKS):
        last = c + 1 == CHUNKS
        *grads[c], mine[c], theirs[c], sums[c], up_sums[c] = expert_chunk(
            c, (1,) * (side - 1) + (2, side - 1) if last else (), place, back, routed[c],
            blocks(block_cot), route_live, ups, downs, up_bias, row(second_gain), row(second_bias),
        )
        if c > 0:
            returned.append(exchange(grads[c - 1][0]))
            got[c - 1] = swap(theirs[c - 1], core)
            returned[-1], got[c - 1], grads[c], mine[c], theirs[c] = tie(
                returned[-1], got[c - 1], grads[c], mine[c], theirs[c]
            )
        if not last:
            routed.append(exchange(sent[c + 1]))
            routed[c + 1], grads[c], mine[c], theirs[c] = tie(
                routed[c + 1], grads[c], mine[c], theirs[c]
            )
    across = lambda v: swap(v, ("expert", n_expert, 1))
    own, *stay, pair, cross = grads[-1]
    got[-1] = swap(theirs[-1], core)
    pair, cross = to_partner(pair, 1), across(cross)
    stay = [to_partner(v, j) for j, v in enumerate(stay, 2)]
    parts = list(expert_grads(True, [*mine, *got[:-1]]))
    pair, cross, parts = tie(pair, cross, parts)
    short = own.shape[0]
    cut = lambda v: [v[n * short : (n + 1) * short] for n in range(v.shape[0] // short)]
    near_pair, far_pair = cut(pair)
    crossed, *rest = cut(cross)
    rest = [to_partner(v, j) for j, v in enumerate(rest, 2)]
    returned += [own, *stay, near_pair, across(far_pair), crossed, *rest]

    fars = list(expert_grads(True, got[-1:], parts))
    sums, up_sums = sum(sums), sum(up_sums)
    empty = jnp.zeros((8, width), F32)
    biases = jnp.concatenate([up_sums.reshape(-1, width), sums[2:3], empty[: 7 - n_dp]], axis=0)

    def over_y(n):
        fars[n] = swap(fars[n], far)

    returned, fars, biases = tie(returned, fars, biases)
    packets = [*mine, *got]
    grad_residual, grad_proj, grad_mixed, out_bias_sum = reenter(
        returned, came_row, live_col, out_weight
    )
    over_y(0)
    grad_mixed, fars[1:] = tie(grad_mixed, fars[1:])
    unstack = lambda v: [v[:, n] for n in range(shared.streams)]

    token_grads = attend_back(
        start_row, query, key, value, mixed, grad_mixed, lse
    )
    token_grads, fars = tie(token_grads, fars)

    over_y(1)
    halves = shared_grads(shared, normed, mixed, token_grads, grad_proj)
    token_grads, halves, fars, out_bias_sum = tie(token_grads, halves, fars, out_bias_sum)

    others = jnp.concatenate([empty[:4], out_bias_sum, sums[0:2], empty[:1]], axis=0)
    total = shared.reduce_first(*halves)
    token_grads, total, others = tie(token_grads, total, others)

    *leaving, token_sums = finish(
        [piece] * side + [piece * side // 2] * 2, token_grads, [query_weight, key_weight, value_weight],
        tokens, grad_residual, row(first_gain), leave_col, others,
    )
    total = shared.reduce_pair_first(total)
    leaving, token_sums, total = tie(leaving, token_sums, total)

    *stay, cross, cross_rest = leaving
    early = range(1, 1 + (2 * side - 2 + 2) // 3)
    late = range(early.stop, side)
    small_steps = list(shared.steps)
    small_step = lambda v: small_sum(v, [small_steps.pop(0)])
    small = jnp.concatenate([token_sums, biases], axis=0)
    for j in early:
        stay[j] = to_partner(stay[j], j)
    small = small_step(small)
    total = jnp.stack(shared.reduce_pair(total, 1), axis=1)
    total, small, fars, mine, stay, cross, cross_rest = tie(
        total, small, fars, mine, stay, cross, cross_rest
    )

    over_y(2)
    cross = swap(cross, ("expert", n_expert, 1))
    block_out = expert_out(place, mine, theirs, routed, downs, row(expert_down_bias[0]), route_live)
    total = shared.reduce_rest(total)
    total, small, block_out, packets, fars, cross, cross_rest = tie(
        total, small, block_out, packets, fars, cross, cross_rest
    )

    over_y(3)
    total = unstack(shared.gather_rest(total))
    near = list(expert_grads(False, packets))
    cross_rest = swap(cross_rest, ("expert", n_expert, 1))
    total, small, near, fars, stay, cross, cross_rest = tie(
        total, small, near, fars, stay, cross, cross_rest
    )
    across = [v[j * piece : (j + 1) * piece] for v in (cross, cross_rest) for j in range(side // 2)]

    for j in late:
        stay[j] = to_partner(stay[j], j)
    small = small_step(small_step(small))
    total = shared.gather_pair(total, 1)
    grad_up = near[1] + jnp.concatenate(fars[1:], axis=0).astype(F32)[None]
    total, small, stay, across, grad_up, near[0] = tie(total, small, stay, across, grad_up, near[0])

    middle = (side + 1) // 2 + 1
    for j in range(1, middle):
        across[j] = to_partner(across[j], j)
    total = shared.gather_pair(total, 0)
    small = small_sum(small, small_steps)
    grad_down = near[0] + jnp.concatenate(fars[:1], axis=0).astype(F32)[None]
    total, small, across, grad_down = tie(total, small, across, grad_down)

    for j in range(middle, side):
        across[j] = to_partner(across[j], j)
    nearest, farthest = shared.gather_first(total)
    grads = unmix(shared, *nearest)
    grads, farthest = tie(grads, farthest)
    grad_query_weight, grad_key_weight, grad_value_weight, grad_out_weight, input_grad = unmix(
        shared, *farthest, grads, partners, [*stay, *across]
    )
    share = width // n_dp
    grad_up_bias = lax.dynamic_slice_in_dim(small, 8 + device, 1, 0)
    grad_down_bias = lax.dynamic_slice_in_dim(small[8 + n_dp : 9 + n_dp], device * share, share, 1)
    return (
        block_out.reshape(count, width),
        input_grad,
        small[0],
        small[1],
        grad_query_weight,
        small[2],
        grad_key_weight,
        grad_value_weight,
        small[3],
        grad_out_weight,
        small[4],
        small[5],
        small[6],
        grad_up,
        grad_up_bias,
        grad_down,
        grad_down_bias,
    )


def solution(mesh):
    both = P(("expert", "dp"), None)
    return jax.shard_map(
        functools.partial(per_device, mesh.shape["expert"], mesh.shape["dp"]),
        mesh=mesh,
        in_specs=(both,) * 3
        + (P(),) * 11
        + (P("expert", None, "dp"), P("expert", None), P("expert", "dp", None), P("expert", None), both),
        out_specs=(both,) * 2
        + (P(),) * 11
        + (P("expert", None, "dp"), P("expert", "dp"), P("expert", "dp", None), P("expert", "dp")),
        check_vma=False,
    )
```
